32 devices in a mesh: dp: 8 (over z, y), seq: 4 (over x, core).
Axes of the slice: x: 2, y: 2, z: 4, core: 2. Of those that a mesh axis runs over, the one named last changes fastest.
Arguments:
- hidden_in: bfloat16 [4096, 768], P(('dp', 'seq')), may hold values from -6 to 6
- lengths: int32 [8, 4], P('dp'), may hold values from 1 to 509, as said below
- grad_out: bfloat16 [4096, 768], P(('dp', 'seq')), may hold values from -6 to 6
- attn_gain: bfloat16 [768], P(('dp', 'seq')), may hold values from 0.5 to 1.5
- attn_shift: bfloat16 [768], P(('dp', 'seq')), may hold values from -3 to 3
- mlp_gain: bfloat16 [768], P(('dp', 'seq')), may hold values from 0.5 to 1.5
- mlp_shift: bfloat16 [768], P(('dp', 'seq')), may hold values from -3 to 3
- qkv_weight: bfloat16 [768, 2304], P(('dp', 'seq')), may hold values from -0.21875 to 0.21875
- qkv_bias: bfloat16 [2304], P(('dp', 'seq')), may hold values from -3 to 3
- dense_weight: bfloat16 [768, 768], P(('dp', 'seq')), may hold values from -2.5 to 2.5
- dense_bias: bfloat16 [768], P(('dp', 'seq')), may hold values from -3 to 3
- up_weight: bfloat16 [768, 3072], P(('dp', 'seq')), may hold values from -0.21875 to 0.21875
- up_bias: bfloat16 [3072], P(('dp', 'seq')), may hold values from -3 to 3
- down_weight: bfloat16 [3072, 768], P(('dp', 'seq')), may hold values from -0.109375 to 0.109375
- down_bias: bfloat16 [768], P(('dp', 'seq')), may hold values from -3 to 3
Outputs:
- block_out: bfloat16 [4096, 768], P(('dp', 'seq'))
- grad_in: bfloat16 [4096, 768], P(('dp', 'seq'))
- attn_gain_grad: float32 [768], P(('dp', 'seq'))
- attn_shift_grad: float32 [768], P(('dp', 'seq'))
- mlp_gain_grad: float32 [768], P(('dp', 'seq'))
- mlp_shift_grad: float32 [768], P(('dp', 'seq'))
- qkv_weight_grad: float32 [768, 2304], P(('dp', 'seq'))
- qkv_bias_grad: float32 [2304], P(('dp', 'seq'))
- dense_weight_grad: float32 [768, 768], P(('dp', 'seq'))
- dense_bias_grad: float32 [768], P(('dp', 'seq'))
- up_weight_grad: float32 [768, 3072], P(('dp', 'seq'))
- up_bias_grad: float32 [3072], P(('dp', 'seq'))
- down_weight_grad: float32 [3072, 768], P(('dp', 'seq'))
- down_bias_grad: float32 [768], P(('dp', 'seq'))
The draws below stay inside these ranges and needn't reach their ends.
Inputs may be any that keep to these rules, and one draw needn't show every extreme that they name: Each row's 4 lengths sum to 512, and one of them is more than 384; in one row all the others are 1.
All inputs are finite; a program needn't handle non-finite values.
Results may differ from the reference program's by a relative error of at most 0.028.
Values may be sent and summed in bfloat16 or wider, within the bound.
No kernel may reach another device: no remote copies, remote signals or barrier semaphores. Data moves between devices by JAX's collectives and lax.ppermute only.
A program may use at most 192 MiB of HBM per device.

```python
import jax
import jax.numpy as jnp
from jax import lax

D = 768
HEADS = 12
HEAD_DIM = 64
ROT = 16
FF = 3072
TOK_DEV = 128
NSEG = 4
GROUP = 512
TOKENS = 4096
N_DP = 8


def draw_lengths(key, part):
    key = jax.random.fold_in(key, 11)
    key_one, key_two, key_three, key_four = jax.random.split(key, 4)
    remainder = jax.random.randint(key_one, (N_DP,), NSEG - 1, TOK_DEV)
    pinned = jax.random.randint(key_four, (), 0, N_DP)
    remainder = jnp.where(jnp.arange(N_DP, dtype=jnp.int32) == pinned, NSEG - 1, remainder).astype(jnp.int32)
    portions = jax.random.randint(key_two, (N_DP, NSEG - 1), 1, 64)
    spare = remainder - (NSEG - 1)
    shares = 1 + spare[:, None] * portions // jnp.sum(portions, axis=1, keepdims=True)
    closing = remainder - jnp.sum(shares[:, :-1], axis=1)
    shorts = jnp.concatenate([shares[:, :-1], closing[:, None]], axis=1)
    longest = GROUP - remainder
    where_long = jax.random.randint(key_three, (N_DP, 1), 0, NSEG)
    columns = jnp.arange(NSEG, dtype=jnp.int32)[None, :]
    source = jnp.clip(columns - (columns > where_long).astype(jnp.int32), 0, NSEG - 2)
    picked = jnp.take_along_axis(shorts, jnp.broadcast_to(source, (N_DP, NSEG)), axis=1)
    result = jnp.where(columns == where_long, longest[:, None], picked)
    return result.astype(jnp.int32)


def steps_of(own_key, shape, cuts, low, high):
    def one(dim, shards_of):
        heights = jax.random.uniform(jax.random.fold_in(jax.random.fold_in(own_key, 6), dim), (shards_of,), jnp.float32, low / len(cuts), high / len(cuts))
        return jnp.repeat(jnp.exp(heights), shape[dim] // shards_of).reshape((-1,) + (1,) * (len(shape) - dim - 1))

    loudness = one(*cuts[0])
    for cut in cuts[1:]:
        loudness = loudness * one(*cut)
    return loudness


def centred(own_key, dims, scale, most, cuts=(), kind=jnp.bfloat16):
    entries = jax.random.normal(own_key, dims, jnp.float32) * scale
    if len(cuts) > 0:
        entries = steps_of(own_key, dims, cuts, -0.22, 0.18) * entries
    return jnp.clip(entries, min=-most, max=most).astype(kind)


def setup_inputs(seed: int = 0) -> dict:
    key_of = jax.random.split(jax.random.key(seed), 16)
    hidden_in = centred(key_of[0], (TOKENS, D), 1.0, 6.0, ((0, 32),))
    lengths = draw_lengths(jax.random.fold_in(key_of[15], 71), 0)
    grad_out = centred(key_of[2], (TOKENS, D), 1.0, 6.0, ((0, 32),))
    attn_gain = jnp.clip(1.0 + 0.1 * jax.random.normal(key_of[3], (D,), jnp.float32), 0.5, 1.5).astype(jnp.bfloat16)
    attn_shift = centred(key_of[4], (D,), 0.3, 3.0, ((0, 32),))
    mlp_gain = jnp.clip(1.0 + 0.1 * jax.random.normal(key_of[5], (D,), jnp.float32), 0.5, 1.5).astype(jnp.bfloat16)
    mlp_shift = centred(key_of[6], (D,), 0.3, 3.0, ((0, 32),))
    qkv_weight = centred(key_of[7], (D, 3 * D), D ** -0.5, 0.21875, ((0, 32),))
    qkv_bias = centred(key_of[8], (3 * D,), 0.3, 3.0, ((0, 32),))
    dense_weight = centred(key_of[9], (D, D), (max(1, 4 * D // GROUP)) ** -0.5, 2.5, ((0, 32),))
    dense_bias = centred(key_of[10], (D,), 0.3, 3.0, ((0, 32),))
    up_weight = centred(key_of[11], (D, FF), D ** -0.5, 0.21875, ((0, 32),))
    up_bias = centred(key_of[12], (FF,), 0.3, 3.0, ((0, 32),))
    down_weight = centred(key_of[13], (FF, D), FF ** -0.5, 0.109375, ((0, 32),))
    down_bias = centred(key_of[14], (D,), 0.3, 3.0, ((0, 32),))
    return {"hidden_in": hidden_in, "lengths": lengths, "grad_out": grad_out, "attn_gain": attn_gain, "attn_shift": attn_shift, "mlp_gain": mlp_gain, "mlp_shift": mlp_shift, "qkv_weight": qkv_weight, "qkv_bias": qkv_bias, "dense_weight": dense_weight, "dense_bias": dense_bias, "up_weight": up_weight, "up_bias": up_bias, "down_weight": down_weight, "down_bias": down_bias}


HIGH = lax.Precision.HIGHEST
EPS = 1e-05
NEGATIVE = -1e+30

@jax.custom_vjp
def low(v):
    return lax.optimization_barrier(v.astype(jnp.bfloat16)).astype(jnp.float32)

@jax.custom_vjp
def low_back(v):
    return v

def low_keep(v):
    return (low(v), None)

def low_pass(kept, grad):
    return (grad,)

def back_keep(v):
    return (v, None)

def back_low(kept, grad):
    return (low(grad),)
low.defvjp(low_keep, low_pass)
low_back.defvjp(back_keep, back_low)

def layer_norm(values, gain, shift):
    center = lax.optimization_barrier(jnp.mean(values, axis=-1, keepdims=True))
    centered = values - center
    spread = lax.optimization_barrier(jnp.mean(centered * centered, axis=-1, keepdims=True))
    return centered * lax.rsqrt(spread + EPS) * gain + shift

def frequencies():
    steps = jnp.arange(ROT // 2, dtype=jnp.float32)
    return jnp.power(jnp.float32(10000.0), -(2.0 * steps) / ROT)

def rotate(values, cosine, sine, sign):
    half = ROT // 2
    first = values[..., :half]
    second = values[..., half:ROT]
    turned_one = first * cosine - sign * second * sine
    turned_two = second * cosine + sign * first * sine
    return jnp.concatenate([turned_one, turned_two, values[..., ROT:]], axis=-1)

def place(row_lengths, index):
    ends = jnp.cumsum(row_lengths).astype(jnp.int32)
    after = (index[:, None] >= ends[None, :]).astype(jnp.int32)
    segment = lax.optimization_barrier(jnp.sum(after, axis=1)).astype(jnp.int32)
    start = lax.optimization_barrier(jnp.sum(after * row_lengths[None, :], axis=1)).astype(jnp.int32)
    return (segment, index - start)

def group_attention(queries, keys_all, values_all, segment):
    block = min(GROUP, 512)
    count = GROUP // block
    key_index = jnp.arange(GROUP, dtype=jnp.int32)
    scale = HEAD_DIM ** (-0.5)

    def one_block(inputs):
        query_block, query_segment, query_index = inputs
        scores = jnp.einsum('qhd,khd->hqk', query_block, keys_all, precision=HIGH) * scale
        scores = low_back(scores)
        allowed = (query_segment[:, None] == segment[None, :]) & (key_index[None, :] <= query_index[:, None])
        scores = jnp.where(allowed[None], scores, NEGATIVE)
        probs = jax.nn.softmax(scores, axis=-1)
        return jnp.einsum('hqk,khd->qhd', low(probs), values_all, precision=HIGH)
    blocks = (queries.reshape(count, block, HEADS, HEAD_DIM), segment.reshape(count, block), key_index.reshape(count, block))
    result = lax.map(jax.checkpoint(one_block), blocks)
    return result.reshape(GROUP, HEADS, HEAD_DIM)

def reference(hidden_in, lengths, grad_out, attn_gain, attn_shift, mlp_gain, mlp_shift, qkv_weight, qkv_bias, dense_weight, dense_bias, up_weight, up_bias, down_weight, down_bias):

    def forward(hidden, a_gain, a_shift, m_gain, m_shift, w_qkv, b_qkv, w_dense, b_dense, w_up, b_up, w_down, b_down):
        attn_in = low(layer_norm(hidden, a_gain, a_shift))
        joined = low_back(jnp.dot(attn_in, w_qkv, precision=HIGH) + b_qkv)
        joined = joined.reshape(N_DP, GROUP, 3, HEADS, HEAD_DIM)

        def per_group(inputs):
            group_qkv, row_lengths = inputs
            segment, position = place(row_lengths, jnp.arange(GROUP, dtype=jnp.int32))
            angles = position.astype(jnp.float32)[:, None] * frequencies()[None, :]
            cosine = jnp.cos(angles)[:, None, :]
            sine = jnp.sin(angles)[:, None, :]
            queries = low(rotate(group_qkv[:, 0], cosine, sine, 1.0))
            keys_all = low(rotate(group_qkv[:, 1], cosine, sine, 1.0))
            values_all = low(group_qkv[:, 2])
            return group_attention(queries, keys_all, values_all, segment)
        attended = lax.map(per_group, (joined, lengths)).reshape(TOKENS, D)
        attended = low_back(low(attended))
        attn_out = jnp.dot(attended, w_dense, precision=HIGH) + b_dense
        mlp_in = low(layer_norm(hidden, m_gain, m_shift))
        upper = low_back(jnp.dot(mlp_in, w_up, precision=HIGH) + b_up)
        act = low(jax.nn.gelu(upper, approximate=False))
        mlp_out = jnp.dot(act, w_down, precision=HIGH) + b_down
        return hidden + attn_out + mlp_out
    inputs = [hidden_in, attn_gain, attn_shift, mlp_gain, mlp_shift, qkv_weight, qkv_bias, dense_weight, dense_bias, up_weight, up_bias, down_weight, down_bias]
    inputs = [item.astype(jnp.float32) for item in inputs]
    result, pullback = jax.vjp(forward, *inputs)
    grads = pullback(grad_out.astype(jnp.float32))
    return (result.astype(jnp.bfloat16), grads[0].astype(jnp.bfloat16), grads[1], grads[2], grads[3], grads[4], grads[5], grads[6], grads[7], grads[8], grads[9], grads[10], grads[11], grads[12])
```

```python
import jax
import jax.numpy as jnp
from jax import lax
from jax.sharding import PartitionSpec as P

HEADS = 12
HEAD_DIM = 64
ROT = 16
EPS = 1e-05
NEGATIVE = -1e30
BF = jnp.bfloat16
F32 = jnp.float32


def dot(spec, a, b):
    return jnp.einsum(spec, a, b, preferred_element_type=F32)


def frequencies():
    steps = jnp.arange(ROT // 2, dtype=F32)
    return jnp.power(F32(10000.0), -(2.0 * steps) / ROT)


def rotate(values, cosine, sine, sign):
    half = ROT // 2
    first = values[..., :half]
    second = values[..., half:ROT]
    turned_one = first * cosine - sign * second * sine
    turned_two = second * cosine + sign * first * sine
    return jnp.concatenate([turned_one, turned_two, values[..., ROT:]], axis=-1)


def place(row_lengths, index):
    ends = jnp.cumsum(row_lengths)
    after = (index[:, None] >= ends[None, :]).astype(jnp.int32)
    segment = jnp.sum(after, axis=1)
    start = jnp.sum(after * row_lengths[None, :], axis=1)
    return (segment, index - start)


def pick(values, index):
    return lax.dynamic_index_in_dim(values, index, 0, keepdims=False)


def seq_exchange(blocks):
    n = lax.axis_size("seq")
    if n != 4:
        return lax.all_to_all(blocks, "seq", 0, 0)
    me = lax.axis_index("seq")
    got = [pick(blocks, me)]
    for other in (1, 2, 3):
        pairs = [(i, i ^ other) for i in range(n)]
        got.append(lax.ppermute(pick(blocks, me ^ other), "seq", pairs))
    return jnp.stack(
        [
            jnp.where(
                me < 2,
                jnp.where(me == 0, got[j], got[j ^ 1]),
                jnp.where(me == 2, got[j ^ 2], got[j ^ 3]),
            )
            for j in range(n)
        ]
    )


CHIP_SWAP = [(0, 2), (2, 0), (1, 3), (3, 1)]
CORE_SWAP = [(0, 1), (1, 0), (2, 3), (3, 2)]


def seq_gather(values):
    n = lax.axis_size("seq")
    if n != 4:
        return lax.all_gather(values, "seq", axis=0, tiled=True)
    me = lax.axis_index("seq")
    chip, core = me // 2, me % 2
    far = lax.ppermute(values, "seq", CHIP_SWAP)
    mine = jnp.stack([jnp.where(chip == 0, values, far), jnp.where(chip == 0, far, values)])
    other = lax.ppermute(mine, "seq", CORE_SWAP)
    full = jnp.stack([jnp.where(core == 0, mine, other), jnp.where(core == 0, other, mine)], axis=1)
    return full.reshape((n * values.shape[0],) + values.shape[1:])


def seq_reduce(values):
    n = lax.axis_size("seq")
    if n != 4:
        return lax.psum_scatter(values.astype(BF), "seq", scatter_dimension=0, tiled=True).astype(F32)
    me = lax.axis_index("seq")
    chip, core = me // 2, me % 2
    rows = values.shape[0] // n
    parts = values.reshape((2, 2, rows) + values.shape[1:])
    keep = lax.dynamic_index_in_dim(parts, core, 1, keepdims=False)
    give = lax.dynamic_index_in_dim(parts, 1 - core, 1, keepdims=False).astype(BF)
    both = keep.astype(F32) + lax.ppermute(give, "seq", CORE_SWAP).astype(F32)
    far = lax.ppermute(pick(both, 1 - chip).astype(BF), "seq", CHIP_SWAP)
    return pick(both, chip) + far.astype(F32)


SIDE_SWAP = [(i, i ^ 1) for i in range(8)]


def up_pairs(*places):
    return [(2 * p + y, 2 * p + 2 + y) for p in places for y in (0, 1)]


def down_pairs(*places):
    return [(2 * p + y, 2 * p - 2 + y) for p in places for y in (0, 1)]


def dp_gather(block):
    n = lax.axis_size("dp")
    if n != 8:
        return lax.all_gather(block, "dp", axis=0)
    me = lax.axis_index("dp")
    line, side = me // 2, me % 2

    def send(values, pairs):
        return lax.ppermute(values, "dp", pairs)

    up1 = send(block, up_pairs(0, 1, 2))
    down1 = send(block, down_pairs(1, 2, 3))
    side0 = send(block, SIDE_SWAP)
    up2 = send(up1, up_pairs(1, 2))
    down2 = send(down1, down_pairs(2, 1))
    first = jnp.where(line == 0, down1, up1)
    side1 = send(first, SIDE_SWAP)
    second = jnp.where(line < 2, down2, up2)
    end3 = send(second, up_pairs(2) + down_pairs(1))
    side2 = send(second, SIDE_SWAP)
    third = jnp.where((line == 0) | (line == 3), end3, down1)
    side3 = send(third, SIDE_SWAP)
    source1 = jnp.where(line == 0, 1, line - 1)
    source2 = jnp.where(line < 2, line + 2, line - 2)
    source3 = jnp.where(line == 0, 3, jnp.where(line == 3, 0, line + 1))
    full = jnp.zeros((4, 2) + block.shape, block.dtype)
    zero = jnp.int32(0)
    for where, near, far in (
        (line, block, side0),
        (source1, first, side1),
        (source2, second, side2),
        (source3, third, side3),
    ):
        pair = jnp.stack([jnp.where(side == 0, near, far), jnp.where(side == 0, far, near)])
        full = lax.dynamic_update_slice(full, pair[None], (where, zero, zero, zero))
    return full.reshape((n,) + block.shape)


def dp_reduce(block_of):
    n = lax.axis_size("dp")
    if n != 8:
        blocks = jnp.stack([block_of(jnp.int32(i)).astype(BF) for i in range(n)])
        return lax.psum_scatter(blocks, "dp", scatter_dimension=0).astype(F32)
    me = lax.axis_index("dp")
    line, side = me // 2, me % 2

    def send(values, pairs):
        return lax.ppermute(values.astype(BF), "dp", pairs).astype(F32)

    ahead = line < 2

    def over_side(target):
        moved = send(block_of(2 * target + 1 - side), SIDE_SWAP)
        return block_of(2 * target + side).astype(F32) + moved

    sum_a = over_side(jnp.where(ahead, 3, 0))
    sum_b = over_side(jnp.where(ahead, 2, 1))
    sum_c = over_side(jnp.where(ahead, 1 - line, 5 - line))
    sum_d = over_side(line)
    sum_a = sum_a + send(sum_a, up_pairs(0) + down_pairs(3))
    end = (line == 0) | (line == 3)
    second = jnp.where(end, sum_b, sum_a)
    up2 = send(second, up_pairs(0, 1))
    down2 = send(second, down_pairs(3, 2))
    sum_b = sum_b + jnp.where(ahead, up2, down2)
    sum_c = sum_c + jnp.where(ahead, down2, up2)
    up3 = send(jnp.where(line == 1, sum_b, sum_c), up_pairs(0, 1, 2))
    down3 = send(jnp.where(line == 2, sum_b, sum_c), down_pairs(3, 2, 1))
    return sum_d + up3 + down3


def attention(queries, keys, values, d_out, segment, scale):
    tokens = queries.shape[1]
    index = jnp.arange(tokens, dtype=jnp.int32)
    allowed = (segment[:, None] == segment[None, :]) & (index[None, :] <= index[:, None])
    scores = dot("htd,hnd->htn", queries, keys) * scale
    masked = jnp.where(allowed[None], scores, NEGATIVE)
    top = jnp.max(masked, axis=-1, keepdims=True)
    weights = jnp.where(allowed[None], jnp.exp(masked - top), 0.0)
    probs = weights / jnp.sum(weights, axis=-1, keepdims=True)
    probs_r = probs.astype(BF)
    attended = dot("htn,hnd->htd", probs_r, values)
    d_probs = dot("htd,hnd->htn", d_out, values)
    delta = jnp.sum(probs * d_probs, axis=-1, keepdims=True)
    d_scores = (probs * (d_probs - delta)).astype(BF)
    d_queries = dot("htn,hnd->htd", d_scores, keys) * scale
    d_keys = dot("htn,htd->hnd", d_scores, queries) * scale
    d_values = dot("htn,htd->hnd", probs_r, d_out)
    return attended, d_queries, d_keys, d_values


def per_device(
    hidden_in,
    lengths,
    grad_out,
    attn_gain,
    attn_shift,
    mlp_gain,
    mlp_shift,
    qkv_weight,
    qkv_bias,
    dense_weight,
    dense_bias,
    up_weight,
    up_bias,
    down_weight,
    down_bias,
):
    n_dp, n_seq = lax.axis_size("dp"), lax.axis_size("seq")
    me = lax.axis_index("seq")
    rows, width = hidden_in.shape
    group = rows * n_seq
    scale = HEAD_DIM ** (-0.5)
    hidden_units = up_weight.shape[1]
    own_units = hidden_units // n_seq
    deep = width // (n_dp * n_seq)
    unit_rows = hidden_units // (n_dp * n_seq)
    heads = -(-HEADS // n_seq)
    own = heads * HEAD_DIM
    spare = heads * n_seq - HEADS

    def by_head(values):
        lead = values.shape[:-1]
        split = values.reshape(lead + (3, HEADS, HEAD_DIM))
        if spare:
            split = jnp.pad(split, [(0, 0)] * (len(lead) + 1) + [(0, spare), (0, 0)])
        split = split.reshape(lead + (3, n_seq, own))
        return jnp.moveaxis(split, -2, 0).reshape((n_seq,) + lead + (3 * own,))

    def from_heads(blocks):
        lead = blocks.shape[1:-1]
        split = jnp.moveaxis(blocks.reshape((n_seq,) + lead + (3, own)), 0, -2)
        split = split.reshape(lead + (3, HEADS + spare, HEAD_DIM))[..., :HEADS, :]
        return split.reshape(lead + (3 * width,))

    vectors = (attn_gain, attn_shift, mlp_gain, mlp_shift, qkv_bias, dense_bias, up_bias, down_bias)
    sizes = [v.shape[0] for v in vectors]
    length = sum(sizes)
    wide = own_units + 3 * own
    up_blocks = jnp.moveaxis(up_weight.reshape(deep, n_dp, n_seq, unit_rows), 2, 0)
    up_blocks = up_blocks.reshape(n_seq, deep, own_units)
    vector = jnp.pad(jnp.concatenate(vectors), (0, wide - length))
    blocks = jnp.concatenate(
        [
            jnp.concatenate([up_blocks, by_head(qkv_weight)], axis=2),
            jnp.broadcast_to(vector, (n_seq, 1, wide)),
        ],
        axis=1,
    )
    got = seq_exchange(blocks)
    up_piece = got[:, :deep, :own_units].reshape(n_seq * deep, own_units)
    qkv_piece = got[:, :deep, own_units:].reshape(n_seq * deep, 3 * own)
    group_vector = got[:, deep, :length]

    hidden_group = seq_gather(hidden_in)
    grad_group = seq_gather(grad_out)

    up_rows = n_seq * deep * own_units // width
    mlp_all = dp_gather(jnp.concatenate([up_piece.reshape(up_rows, width), down_weight], axis=0))
    qkv_all = dp_gather(qkv_piece)
    vec_rows = -(-n_seq * length // width)
    vec_piece = jnp.pad(group_vector.reshape(-1), (0, vec_rows * width - n_seq * length))
    dense_all = dp_gather(jnp.concatenate([dense_weight, vec_piece.reshape(vec_rows, width)], axis=0))
    up_full = mlp_all[:, :up_rows].reshape(width, own_units)
    down_full = mlp_all[:, up_rows:].reshape(own_units, width)
    qkv_full = qkv_all.reshape(width, 3 * own)
    dense_rows = dense_all[:, :deep].reshape(n_dp * deep, width)
    every = dense_all[:, deep:].reshape(n_dp, vec_rows * width)[:, : n_seq * length]
    every = every.reshape(n_dp * n_seq, length).astype(F32)
    whole = []
    start = 0
    for size in sizes:
        whole.append(every[:, start : start + size].reshape(-1))
        start += size
    f_attn_gain, f_attn_shift, f_mlp_gain, f_mlp_shift, f_qkv_bias, f_dense_bias, f_up_bias, f_down_bias = whole
    own_qkv_bias = pick(by_head(f_qkv_bias), me)
    own_up_bias = lax.dynamic_index_in_dim(
        f_up_bias.reshape(n_dp, n_seq, unit_rows), me, 1, keepdims=False
    ).reshape(-1)

    row_lengths = lengths[0]
    index = jnp.arange(group, dtype=jnp.int32)
    segment, position = place(row_lengths, index)
    angles = position.astype(F32)[:, None] * frequencies()[None, :]
    cosine = jnp.cos(angles)[:, None, :]
    sine = jnp.sin(angles)[:, None, :]

    tokens = hidden_group.astype(F32)
    center = jnp.mean(tokens, axis=-1, keepdims=True)
    centered = tokens - center
    spread = jnp.mean(centered * centered, axis=-1, keepdims=True)
    unit = centered * lax.rsqrt(spread + EPS)
    attn_in = (unit * f_attn_gain + f_attn_shift).astype(BF)
    mlp_in = (unit * f_mlp_gain + f_mlp_shift).astype(BF)

    upper = dot("td,df->tf", mlp_in, up_full) + own_up_bias
    cdf = 0.5 * (1.0 + lax.erf(upper * F32(0.7071067811865476)))
    pdf = jnp.exp(-0.5 * upper * upper) * F32(0.3989422804014327)
    act = (upper * cdf).astype(BF)
    d_act = dot("td,fd->tf", grad_group, down_full)
    d_up = (d_act * (cdf + upper * pdf)).astype(BF)
    down_grad = dot("tf,td->fd", act, grad_group).astype(BF).reshape(n_dp, unit_rows, width)
    up_grad = dot("td,tf->df", mlp_in, d_up).astype(BF).reshape(n_dp, up_rows, width)
    mlp_out = dot("tf,fd->td", act, down_full)
    d_mlp_in = dot("tf,df->td", d_up, up_full)
    mlp_sum = dp_reduce(lambda i: jnp.concatenate([pick(up_grad, i), pick(down_grad, i)], axis=0))

    joined = dot("td,de->te", attn_in, qkv_full) + own_qkv_bias
    joined = joined.reshape(group, 3, heads, HEAD_DIM)
    queries = jnp.moveaxis(rotate(joined[:, 0], cosine, sine, 1.0).astype(BF), 1, 0)
    keys = jnp.moveaxis(rotate(joined[:, 1], cosine, sine, 1.0).astype(BF), 1, 0)
    values = jnp.moveaxis(joined[:, 2].astype(BF), 1, 0)
    feature_rows = n_dp * deep
    per_line = n_seq * deep
    direct = spare == 0 and own % per_line == 0
    d_rows = dot("fe,te->ft", dense_rows, grad_group).astype(BF)
    if direct:
        runs = own // per_line
        moved = seq_exchange(d_rows.reshape(n_seq, runs * deep, group))
        moved = moved.reshape(n_seq, runs, deep, group)
        d_attended = jnp.moveaxis(moved, 0, 1).reshape(heads, HEAD_DIM, group)
    else:
        moved = lax.all_gather(d_rows.reshape(n_dp, deep, group), "seq", axis=1)
        moved = moved.reshape(width, group)
        moved = jnp.pad(moved, ((0, spare * HEAD_DIM), (0, 0)))
        d_attended = pick(moved.reshape(n_seq, heads, HEAD_DIM, group), me)
    d_attended = jnp.swapaxes(d_attended, 1, 2)
    attended, d_queries, d_keys, d_values = attention(queries, keys, values, d_attended, segment, scale)
    attended = jnp.swapaxes(attended.astype(BF), 1, 2).reshape(own, group)
    if direct:
        given = jnp.moveaxis(attended.reshape(runs, n_seq, deep, group), 1, 0)
        rows_attended = seq_exchange(given.reshape(n_seq, runs * deep, group)).reshape(feature_rows, group)
    else:
        given = lax.all_gather(attended, "seq", axis=0, tiled=True)[:width]
        rows_attended = lax.dynamic_index_in_dim(
            given.reshape(n_dp, n_seq, deep, group), me, 1, keepdims=False
        ).reshape(feature_rows, group)
    attn_out = dot("ft,fe->te", rows_attended, dense_rows)
    dense_grad = dot("ft,te->fe", rows_attended, grad_group).reshape(n_dp, deep, width)
    d_queries = rotate(jnp.moveaxis(d_queries, 0, 1), cosine, sine, -1.0)
    d_keys = rotate(jnp.moveaxis(d_keys, 0, 1), cosine, sine, -1.0)
    d_joined = jnp.stack([d_queries, d_keys, jnp.moveaxis(d_values, 0, 1)], axis=1)
    d_joined = d_joined.astype(BF).reshape(group, 3 * own)
    qkv_grad = dot("td,te->de", attn_in, d_joined).astype(BF).reshape(n_dp, n_seq * deep, 3 * own)
    d_attn_in = dot("te,de->td", d_joined, qkv_full)

    mine = jnp.arange(n_seq) == me
    qkv_bias_grad = jnp.sum(d_joined.astype(F32), axis=0)
    qkv_bias_grad = from_heads(jnp.where(mine[:, None], qkv_bias_grad[None], 0.0))
    up_bias_grad = jnp.sum(d_up.astype(F32), axis=0).reshape(n_dp, 1, unit_rows)
    up_bias_grad = jnp.where(mine[None, :, None], up_bias_grad, 0.0)
    bias_sum = jnp.sum(grad_out.astype(F32), axis=0)
    terms = (
        jnp.sum(d_attn_in * unit, axis=0),
        jnp.sum(d_attn_in, axis=0),
        jnp.sum(d_mlp_in * unit, axis=0),
        jnp.sum(d_mlp_in, axis=0),
        qkv_bias_grad,
        bias_sum,
        up_bias_grad,
        bias_sum,
    )
    terms = [t.reshape(n_dp, n_seq, size) for t, size in zip(terms, sizes)]
    terms = jnp.concatenate(terms, axis=2).reshape(n_dp, n_seq * length)
    terms = jnp.pad(terms, ((0, 0), (0, vec_rows * width - n_seq * length)))
    terms = terms.reshape(n_dp, vec_rows, width)
    dense_terms = jnp.concatenate([dense_grad, terms], axis=1).astype(BF)
    qkv_sum = dp_reduce(lambda i: pick(qkv_grad, i))
    dense_sum = dp_reduce(lambda i: pick(dense_terms, i))

    block_out = hidden_in.astype(F32) + f_dense_bias + f_down_bias + seq_reduce(attn_out + mlp_out)
    upstream = seq_reduce(d_attn_in * f_attn_gain + d_mlp_in * f_mlp_gain)
    x = hidden_in.astype(F32)
    centered = x - jnp.mean(x, axis=-1, keepdims=True)
    inverse = lax.rsqrt(jnp.mean(centered * centered, axis=-1, keepdims=True) + EPS)
    own_unit = centered * inverse
    inner = (
        upstream
        - jnp.mean(upstream, axis=-1, keepdims=True)
        - own_unit * jnp.mean(upstream * own_unit, axis=-1, keepdims=True)
    )
    grad_in = grad_out.astype(F32) + inverse * inner

    vec_sum = dense_sum[deep:].reshape(-1)[: n_seq * length].reshape(n_seq, 1, length)
    vec_sum = jnp.pad(vec_sum, ((0, 0), (0, 0), (0, wide - length)))
    back = jnp.concatenate(
        [
            jnp.concatenate(
                [
                    mlp_sum[:up_rows].reshape(n_seq, deep, own_units),
                    qkv_sum.reshape(n_seq, deep, 3 * own),
                ],
                axis=2,
            ),
            vec_sum,
        ],
        axis=1,
    )
    back = seq_exchange(back.astype(BF)).astype(F32)
    up_own = jnp.moveaxis(back[:, :deep, :own_units].reshape(n_seq, deep, n_dp, unit_rows), 0, 2)
    qkv_own = from_heads(back[:, :deep, own_units:])
    vec_own = jnp.sum(back[:, deep, :length], axis=0)
    owned = []
    start = 0
    for size in sizes:
        owned.append(vec_own[start : start + size])
        start += size
    return (
        block_out.astype(BF),
        grad_in.astype(BF),
        owned[0],
        owned[1],
        owned[2],
        owned[3],
        qkv_own,
        owned[4],
        dense_sum[:deep],
        owned[5],
        up_own.reshape(deep, hidden_units),
        owned[6],
        mlp_sum[up_rows:],
        owned[7],
    )


def solution(mesh):
    both = ("dp", "seq")
    matrix, vector = P(both, None), P(both)
    params = (vector, vector, vector, vector, matrix, vector, matrix, vector, matrix, vector, matrix, vector)
    return jax.shard_map(
        per_device,
        mesh=mesh,
        in_specs=(matrix, P("dp", None), matrix) + params,
        out_specs=(matrix, matrix) + params,
        check_vma=False,
    )
```

```python
import jax
import jax.numpy as jnp
from jax import lax
from jax.sharding import PartitionSpec as P

HEADS = 12
HEAD_DIM = 64
ROT = 16
EPS = 1e-05
NEGATIVE = -1e30
BF = jnp.bfloat16
F32 = jnp.float32


def dot(spec, a, b):
    return jnp.einsum(spec, a, b, preferred_element_type=F32)


def frequencies():
    steps = jnp.arange(ROT // 2, dtype=F32)
    return jnp.power(F32(10000.0), -(2.0 * steps) / ROT)


def rotate(values, cosine, sine, sign):
    half = ROT // 2
    first = values[..., :half]
    second = values[..., half:ROT]
    turned_one = first * cosine - sign * second * sine
    turned_two = second * cosine + sign * first * sine
    return jnp.concatenate([turned_one, turned_two, values[..., ROT:]], axis=-1)


def place(row_lengths, index):
    ends = jnp.cumsum(row_lengths)
    after = (index[:, None] >= ends[None, :]).astype(jnp.int32)
    segment = jnp.sum(after, axis=1)
    start = jnp.sum(after * row_lengths[None, :], axis=1)
    return (segment, index - start)


def pick(values, index):
    return lax.dynamic_index_in_dim(values, index, 0, keepdims=False)


CHIP_SWAP = [(0, 2), (2, 0), (1, 3), (3, 1)]
CORE_SWAP = [(0, 1), (1, 0), (2, 3), (3, 2)]


def in_order(second, mine, other, axis=0):
    return jnp.stack([jnp.where(second, other, mine), jnp.where(second, mine, other)], axis=axis)


def seq_exchange(blocks):
    n = lax.axis_size("seq")
    if n != 4:
        return lax.all_to_all(blocks, "seq", 0, 0)
    me = lax.axis_index("seq")
    chip, core = me // 2, me % 2
    halves = blocks.reshape((2, 2) + blocks.shape[1:])
    far = lax.ppermute(pick(halves, 1 - chip), "seq", CHIP_SWAP)
    by_chip = in_order(chip == 1, pick(halves, chip), far, axis=1)
    other = lax.ppermute(pick(by_chip, 1 - core), "seq", CORE_SWAP)
    return in_order(core == 1, pick(by_chip, core), other, axis=1).reshape(blocks.shape)


def seq_gather(values):
    n = lax.axis_size("seq")
    if n != 4:
        return lax.all_gather(values, "seq", axis=0)
    me = lax.axis_index("seq")
    chip, core = me // 2, me % 2
    far = lax.ppermute(values, "seq", CHIP_SWAP)
    mine = in_order(chip == 1, values, far)
    other = lax.ppermute(mine, "seq", CORE_SWAP)
    return in_order(core == 1, mine, other, axis=1).reshape((n,) + values.shape)


def seq_reduce(values):
    n = lax.axis_size("seq")
    if n != 4:
        return lax.psum_scatter(values.astype(BF), "seq", scatter_dimension=0).astype(F32)
    me = lax.axis_index("seq")
    chip, core = me // 2, me % 2
    parts = values.reshape((2, 2) + values.shape[1:])
    keep = lax.dynamic_index_in_dim(parts, core, 1, keepdims=False)
    give = lax.dynamic_index_in_dim(parts, 1 - core, 1, keepdims=False).astype(BF)
    both = keep.astype(F32) + lax.ppermute(give, "seq", CORE_SWAP).astype(F32)
    far = lax.ppermute(pick(both, 1 - chip).astype(BF), "seq", CHIP_SWAP)
    return pick(both, chip) + far.astype(F32)


SIDE_SWAP = [(i, i ^ 1) for i in range(8)]


def along(step):
    return [(i, (i + 2 * step) % 8) for i in range(8)]


def dp_gather(block):
    n = lax.axis_size("dp")
    if n != 8:
        return lax.all_gather(block, "dp", axis=0)
    me = lax.axis_index("dp")
    line, side = me // 2, me % 2
    near1 = lax.ppermute(block, "dp", along(1))
    near3 = lax.ppermute(block, "dp", along(3))
    near2 = lax.ppermute(block, "dp", along(2))
    far0 = lax.ppermute(block, "dp", SIDE_SWAP)
    far13 = lax.ppermute(jnp.stack([near1, near3]), "dp", SIDE_SWAP)
    far2 = lax.ppermute(near2, "dp", SIDE_SWAP)
    full = jnp.zeros((4, 2) + block.shape, block.dtype)
    zero = jnp.int32(0)
    for step, near, far in ((0, block, far0), (1, near1, far13[0]), (3, near3, far13[1]), (2, near2, far2)):
        pair = in_order(side == 1, near, far)
        full = lax.dynamic_update_slice(full, pair[None], ((line - step) % 4, zero, zero, zero))
    return full.reshape((n,) + block.shape)


def dp_reduce(block_of):
    n = lax.axis_size("dp")
    if n != 8:
        blocks = jnp.stack([block_of(jnp.int32(i)).astype(BF) for i in range(n)])
        return lax.psum_scatter(blocks, "dp", scatter_dimension=0).astype(F32)
    me = lax.axis_index("dp")
    line, side = me // 2, me % 2

    def over_side(*steps):
        targets = [2 * ((line + step) % 4) for step in steps]
        moved = lax.ppermute(jnp.stack([block_of(t + 1 - side) for t in targets]), "dp", SIDE_SWAP)
        return [block_of(t + side).astype(F32) + moved[j].astype(F32) for j, t in enumerate(targets)]

    (sum2,) = over_side(2)
    sum1, sum3 = over_side(1, 3)
    (sum0,) = over_side(0)
    got2 = lax.ppermute(sum2.astype(BF), "dp", along(2)).astype(F32)
    got1 = lax.ppermute(sum1.astype(BF), "dp", along(1)).astype(F32)
    got3 = lax.ppermute(sum3.astype(BF), "dp", along(3)).astype(F32)
    return sum0 + got1 + got2 + got3


def attention(queries, keys, values, d_out, segment, scale):
    tokens = queries.shape[1]
    index = jnp.arange(tokens, dtype=jnp.int32)
    allowed = (segment[:, None] == segment[None, :]) & (index[None, :] <= index[:, None])
    scores = dot("htd,hnd->htn", queries, keys) * scale
    masked = jnp.where(allowed[None], scores, NEGATIVE)
    top = jnp.max(masked, axis=-1, keepdims=True)
    weights = jnp.where(allowed[None], jnp.exp(masked - top), 0.0)
    probs = weights / jnp.sum(weights, axis=-1, keepdims=True)
    probs_r = probs.astype(BF)
    attended = dot("htn,hnd->htd", probs_r, values)
    d_probs = dot("htd,hnd->htn", d_out, values)
    delta = jnp.sum(probs * d_probs, axis=-1, keepdims=True)
    d_scores = (probs * (d_probs - delta)).astype(BF)
    d_queries = dot("htn,hnd->htd", d_scores, keys) * scale
    d_keys = dot("htn,htd->hnd", d_scores, queries) * scale
    d_values = dot("htn,htd->hnd", probs_r, d_out)
    return attended, d_queries, d_keys, d_values


def per_device(
    hidden_in,
    lengths,
    grad_out,
    attn_gain,
    attn_shift,
    mlp_gain,
    mlp_shift,
    qkv_weight,
    qkv_bias,
    dense_weight,
    dense_bias,
    up_weight,
    up_bias,
    down_weight,
    down_bias,
):
    n_dp, n_seq = lax.axis_size("dp"), lax.axis_size("seq")
    me = lax.axis_index("seq")
    rows, width = hidden_in.shape
    group = rows * n_seq
    scale = HEAD_DIM ** (-0.5)
    hidden_units = up_weight.shape[1]
    own_units = hidden_units // n_seq
    deep = width // (n_dp * n_seq)
    unit_rows = hidden_units // (n_dp * n_seq)
    heads = -(-HEADS // n_seq)
    own = heads * HEAD_DIM
    spare = heads * n_seq - HEADS

    def by_head(values):
        lead = values.shape[:-1]
        split = values.reshape(lead + (3, HEADS, HEAD_DIM))
        if spare:
            split = jnp.pad(split, [(0, 0)] * (len(lead) + 1) + [(0, spare), (0, 0)])
        split = split.reshape(lead + (3, n_seq, own))
        return jnp.moveaxis(split, -2, 0).reshape((n_seq,) + lead + (3 * own,))

    def from_heads(blocks):
        lead = blocks.shape[1:-1]
        split = jnp.moveaxis(blocks.reshape((n_seq,) + lead + (3, own)), 0, -2)
        split = split.reshape(lead + (3, HEADS + spare, HEAD_DIM))[..., :HEADS, :]
        return split.reshape(lead + (3 * width,))

    vectors = (attn_gain, attn_shift, mlp_gain, mlp_shift, qkv_bias, dense_bias, up_bias, down_bias)
    sizes = [v.shape[0] for v in vectors]
    length = sum(sizes)
    wide = own_units + 3 * own
    up_blocks = jnp.moveaxis(up_weight.reshape(deep, n_dp, n_seq, unit_rows), 2, 0)
    up_blocks = up_blocks.reshape(n_seq, deep, own_units)
    vector = jnp.pad(jnp.concatenate(vectors), (0, wide - length))
    blocks = jnp.concatenate(
        [
            jnp.concatenate([up_blocks, by_head(qkv_weight)], axis=2),
            jnp.broadcast_to(vector, (n_seq, 1, wide)),
        ],
        axis=1,
    )
    got = seq_exchange(blocks)
    per_line = n_seq * deep
    up_rows = per_line * own_units // width
    up_piece = got[:, :deep, :own_units].reshape(up_rows, width)
    qkv_piece = got[:, :deep, own_units:].reshape(per_line, 3 * own)
    group_vector = got[:, deep, :length]

    both = seq_gather(jnp.concatenate([hidden_in, grad_out], axis=0))
    hidden_group = both[:, :rows].reshape(group, width)
    grad_group = both[:, rows:].reshape(group, width)

    def beside(values):
        lead = values.shape[:-2]
        split = values.reshape(lead + (deep, n_seq, width // n_seq))
        return jnp.swapaxes(split, -3, -2).reshape(lead + (per_line, width // n_seq))

    def from_beside(values):
        lead = values.shape[:-2]
        split = values.reshape(lead + (n_seq, deep, width // n_seq))
        return jnp.swapaxes(split, -3, -2).reshape(lead + (deep, width))

    attn_wide = 3 * own + width // n_seq
    vec_rows = -(-n_seq * length // attn_wide)
    vec_rows += -vec_rows % 8
    vec_piece = jnp.pad(group_vector.reshape(-1), (0, vec_rows * attn_wide - n_seq * length))
    attn_piece = jnp.concatenate([qkv_piece, beside(dense_weight)], axis=1)
    attn_piece = jnp.concatenate([attn_piece, vec_piece.reshape(vec_rows, attn_wide)], axis=0)
    attn_all = dp_gather(attn_piece)
    mlp_all = dp_gather(jnp.concatenate([up_piece, down_weight], axis=0))
    qkv_full = attn_all[:, :per_line, : 3 * own].reshape(width, 3 * own)
    dense_rows = from_beside(attn_all[:, :per_line, 3 * own :]).reshape(n_dp * deep, width)
    up_full = mlp_all[:, :up_rows].reshape(width, own_units)
    down_full = mlp_all[:, up_rows:].reshape(own_units, width)
    every = attn_all[:, per_line:].reshape(n_dp, vec_rows * attn_wide)[:, : n_seq * length]
    every = every.reshape(n_dp * n_seq, length).astype(F32)
    whole = []
    start = 0
    for size in sizes:
        whole.append(every[:, start : start + size].reshape(-1))
        start += size
    f_attn_gain, f_attn_shift, f_mlp_gain, f_mlp_shift, f_qkv_bias, f_dense_bias, f_up_bias, f_down_bias = whole
    own_qkv_bias = pick(by_head(f_qkv_bias), me)
    own_up_bias = lax.dynamic_index_in_dim(
        f_up_bias.reshape(n_dp, n_seq, unit_rows), me, 1, keepdims=False
    ).reshape(-1)

    row_lengths = lengths[0]
    index = jnp.arange(group, dtype=jnp.int32)
    segment, position = place(row_lengths, index)
    angles = position.astype(F32)[:, None] * frequencies()[None, :]
    cosine = jnp.cos(angles)[:, None, :]
    sine = jnp.sin(angles)[:, None, :]

    tokens = hidden_group.astype(F32)
    center = jnp.mean(tokens, axis=-1, keepdims=True)
    centered = tokens - center
    spread = jnp.mean(centered * centered, axis=-1, keepdims=True)
    unit = centered * lax.rsqrt(spread + EPS)
    attn_in = (unit * f_attn_gain + f_attn_shift).astype(BF)
    mlp_in = (unit * f_mlp_gain + f_mlp_shift).astype(BF)

    joined = dot("td,de->te", attn_in, qkv_full) + own_qkv_bias
    joined = joined.reshape(group, 3, heads, HEAD_DIM)
    queries = jnp.moveaxis(rotate(joined[:, 0], cosine, sine, 1.0).astype(BF), 1, 0)
    keys = jnp.moveaxis(rotate(joined[:, 1], cosine, sine, 1.0).astype(BF), 1, 0)
    values = jnp.moveaxis(joined[:, 2].astype(BF), 1, 0)
    feature_rows = n_dp * deep
    direct = spare == 0 and own % per_line == 0
    d_rows = dot("fe,te->ft", dense_rows, grad_group).astype(BF)
    if direct:
        runs = own // per_line
        moved = seq_exchange(d_rows.reshape(n_seq, runs * deep, group))
        moved = moved.reshape(n_seq, runs, deep, group)
        d_attended = jnp.moveaxis(moved, 0, 1).reshape(heads, HEAD_DIM, group)
    else:
        moved = lax.all_gather(d_rows.reshape(n_dp, deep, group), "seq", axis=1)
        moved = moved.reshape(width, group)
        moved = jnp.pad(moved, ((0, spare * HEAD_DIM), (0, 0)))
        d_attended = pick(moved.reshape(n_seq, heads, HEAD_DIM, group), me)
    d_attended = jnp.swapaxes(d_attended, 1, 2)
    attended, d_queries, d_keys, d_values = attention(queries, keys, values, d_attended, segment, scale)
    attended = jnp.swapaxes(attended.astype(BF), 1, 2).reshape(own, group)
    if direct:
        given = jnp.moveaxis(attended.reshape(runs, n_seq, deep, group), 1, 0)
        rows_attended = seq_exchange(given.reshape(n_seq, runs * deep, group)).reshape(feature_rows, group)
    else:
        given = lax.all_gather(attended, "seq", axis=0, tiled=True)[:width]
        rows_attended = lax.dynamic_index_in_dim(
            given.reshape(n_dp, n_seq, deep, group), me, 1, keepdims=False
        ).reshape(feature_rows, group)
    attn_out = dot("ft,fe->te", rows_attended, dense_rows)
    dense_grad = dot("ft,te->fe", rows_attended, grad_group).astype(BF).reshape(n_dp, deep, width)
    d_queries = rotate(jnp.moveaxis(d_queries, 0, 1), cosine, sine, -1.0)
    d_keys = rotate(jnp.moveaxis(d_keys, 0, 1), cosine, sine, -1.0)
    d_joined = jnp.stack([d_queries, d_keys, jnp.moveaxis(d_values, 0, 1)], axis=1)
    d_joined = d_joined.astype(BF).reshape(group, 3 * own)
    qkv_grad = dot("td,te->de", attn_in, d_joined).astype(BF).reshape(n_dp, n_seq * deep, 3 * own)
    d_attn_in = dot("te,de->td", d_joined, qkv_full)
    attn_terms = jnp.concatenate([qkv_grad, beside(dense_grad)], axis=2)
    attn_sum = dp_reduce(lambda i: pick(attn_terms, i))

    upper = dot("td,df->tf", mlp_in, up_full) + own_up_bias
    cdf = 0.5 * (1.0 + lax.erf(upper * F32(0.7071067811865476)))
    pdf = jnp.exp(-0.5 * upper * upper) * F32(0.3989422804014327)
    act = (upper * cdf).astype(BF)
    d_act = dot("td,fd->tf", grad_group, down_full)
    d_up = (d_act * (cdf + upper * pdf)).astype(BF)
    down_grad = dot("tf,td->fd", act, grad_group).astype(BF).reshape(n_dp, unit_rows, width)
    up_grad = dot("td,tf->df", mlp_in, d_up).astype(BF).reshape(n_dp, up_rows, width)
    mlp_out = dot("tf,fd->td", act, down_full)
    d_mlp_in = dot("tf,df->td", d_up, up_full)

    mine = jnp.arange(n_seq) == me
    qkv_bias_grad = jnp.sum(d_joined.astype(F32), axis=0)
    qkv_bias_grad = from_heads(jnp.where(mine[:, None], qkv_bias_grad[None], 0.0))
    up_bias_grad = jnp.sum(d_up.astype(F32), axis=0).reshape(n_dp, 1, unit_rows)
    up_bias_grad = jnp.where(mine[None, :, None], up_bias_grad, 0.0)
    bias_sum = jnp.sum(grad_out.astype(F32), axis=0)
    terms = (
        jnp.sum(d_attn_in * unit, axis=0),
        jnp.sum(d_attn_in, axis=0),
        jnp.sum(d_mlp_in * unit, axis=0),
        jnp.sum(d_mlp_in, axis=0),
        qkv_bias_grad,
        bias_sum,
        up_bias_grad,
        bias_sum,
    )
    terms = [t.reshape(n_dp, n_seq, size) for t, size in zip(terms, sizes)]
    terms = jnp.concatenate(terms, axis=2).reshape(n_dp, n_seq * length)
    tail_rows = -(-n_seq * length // width)
    tail_rows += -tail_rows % 8
    terms = jnp.pad(terms, ((0, 0), (0, tail_rows * width - n_seq * length)))
    terms = terms.reshape(n_dp, tail_rows, width).astype(BF)
    mlp_sum = dp_reduce(lambda i: jnp.concatenate([pick(up_grad, i), pick(down_grad, i), pick(terms, i)], axis=0))

    upstream = d_attn_in * f_attn_gain + d_mlp_in * f_mlp_gain
    pair = jnp.concatenate([(attn_out + mlp_out).astype(BF), upstream.astype(BF)], axis=1)
    pair = seq_reduce(pair.reshape(n_seq, rows, 2 * width))
    block_out = hidden_in.astype(F32) + f_dense_bias + f_down_bias + pair[:, :width]
    upstream = pair[:, width:]
    x = hidden_in.astype(F32)
    centered = x - jnp.mean(x, axis=-1, keepdims=True)
    inverse = lax.rsqrt(jnp.mean(centered * centered, axis=-1, keepdims=True) + EPS)
    own_unit = centered * inverse
    inner = (
        upstream
        - jnp.mean(upstream, axis=-1, keepdims=True)
        - own_unit * jnp.mean(upstream * own_unit, axis=-1, keepdims=True)
    )
    grad_in = grad_out.astype(F32) + inverse * inner

    qkv_back = attn_sum[:, : 3 * own].reshape(n_seq, deep, 3 * own).astype(BF)
    qkv_own = from_heads(seq_exchange(qkv_back).astype(F32))
    dense_own = from_beside(attn_sum[:, 3 * own :])
    vec_sum = mlp_sum[up_rows + unit_rows :].reshape(-1)[: n_seq * length].reshape(n_seq, 1, length)
    vec_sum = jnp.pad(vec_sum, ((0, 0), (0, 0), (0, -length % own_units)))
    vec_sum = vec_sum.reshape(n_seq, -1, own_units)
    back = jnp.concatenate([mlp_sum[:up_rows].reshape(n_seq, deep, own_units), vec_sum], axis=1)
    back = seq_exchange(back.astype(BF)).astype(F32)
    up_own = jnp.moveaxis(back[:, :deep].reshape(n_seq, deep, n_dp, unit_rows), 0, 2)
    vec_own = jnp.sum(back[:, deep:].reshape(n_seq, -1), axis=0)
    owned = []
    start = 0
    for size in sizes:
        owned.append(vec_own[start : start + size])
        start += size
    return (
        block_out.astype(BF),
        grad_in.astype(BF),
        owned[0],
        owned[1],
        owned[2],
        owned[3],
        qkv_own,
        owned[4],
        dense_own,
        owned[5],
        up_own.reshape(deep, hidden_units),
        owned[6],
        mlp_sum[up_rows : up_rows + unit_rows],
        owned[7],
    )


def solution(mesh):
    both = ("dp", "seq")
    matrix, vector = P(both, None), P(both)
    params = (vector, vector, vector, vector, matrix, vector, matrix, vector, matrix, vector, matrix, vector)
    return jax.shard_map(
        per_device,
        mesh=mesh,
        in_specs=(matrix, P("dp", None), matrix) + params,
        out_specs=(matrix, matrix) + params,
        check_vma=False,
    )
```

```python
import functools

import jax
import jax.numpy as jnp
from jax import lax
from jax.experimental import pallas as pl
from jax.experimental.pallas import tpu as pltpu
from jax.sharding import PartitionSpec as P

HEADS = 12
HEAD_DIM = 64
ROT = 16
EPS = 1e-05
NEGATIVE = -1e30
BF = jnp.bfloat16
F32 = jnp.float32


def dot(spec, a, b):
    return jnp.einsum(spec, a, b, preferred_element_type=F32)


def frequencies():
    steps = jnp.arange(ROT // 2, dtype=F32)
    return jnp.power(F32(10000.0), -(2.0 * steps) / ROT)


def rotate(values, cosine, sine, sign):
    half = ROT // 2
    first = values[..., :half]
    second = values[..., half:ROT]
    turned_one = first * cosine - sign * second * sine
    turned_two = second * cosine + sign * first * sine
    return jnp.concatenate([turned_one, turned_two, values[..., ROT:]], axis=-1)


def place(row_lengths, index):
    ends = jnp.cumsum(row_lengths)
    after = (index[:, None] >= ends[None, :]).astype(jnp.int32)
    segment = jnp.sum(after, axis=1)
    start = jnp.sum(after * row_lengths[None, :], axis=1)
    return (segment, index - start)


def pick(values, index):
    return lax.dynamic_index_in_dim(values, index, 0, keepdims=False)


CHIP_SWAP = [(0, 2), (2, 0), (1, 3), (3, 1)]
CORE_SWAP = [(0, 1), (1, 0), (2, 3), (3, 2)]


def in_order(second, mine, other, axis=0):
    return jnp.stack([jnp.where(second, other, mine), jnp.where(second, mine, other)], axis=axis)


def seq_exchange(blocks):
    n = lax.axis_size("seq")
    if n != 4:
        return lax.all_to_all(blocks, "seq", 0, 0)
    me = lax.axis_index("seq")
    chip, core = me // 2, me % 2
    halves = blocks.reshape((2, 2) + blocks.shape[1:])
    far = lax.ppermute(pick(halves, 1 - chip), "seq", CHIP_SWAP)
    by_chip = in_order(chip == 1, pick(halves, chip), far, axis=1)
    other = lax.ppermute(pick(by_chip, 1 - core), "seq", CORE_SWAP)
    return in_order(core == 1, pick(by_chip, core), other, axis=1).reshape(blocks.shape)


def seq_gather(values):
    n = lax.axis_size("seq")
    if n != 4:
        return lax.all_gather(values, "seq", axis=0)
    me = lax.axis_index("seq")
    chip, core = me // 2, me % 2
    far = lax.ppermute(values, "seq", CHIP_SWAP)
    mine = in_order(chip == 1, values, far)
    other = lax.ppermute(mine, "seq", CORE_SWAP)
    return in_order(core == 1, mine, other, axis=1).reshape((n,) + values.shape)


def seq_reduce(values):
    n = lax.axis_size("seq")
    if n != 4:
        return lax.psum_scatter(values.astype(BF), "seq", scatter_dimension=0).astype(F32)
    me = lax.axis_index("seq")
    chip, core = me // 2, me % 2
    parts = values.reshape((2, 2) + values.shape[1:])
    keep = lax.dynamic_index_in_dim(parts, core, 1, keepdims=False)
    give = lax.dynamic_index_in_dim(parts, 1 - core, 1, keepdims=False).astype(BF)
    both = keep.astype(F32) + lax.ppermute(give, "seq", CORE_SWAP).astype(F32)
    far = lax.ppermute(pick(both, 1 - chip).astype(BF), "seq", CHIP_SWAP)
    return pick(both, chip) + far.astype(F32)


SIDE_SWAP = [(i, i ^ 1) for i in range(8)]


def along(step):
    return [(i, (i + 2 * step) % 8) for i in range(8)]


def dp_gather(block):
    n = lax.axis_size("dp")
    if n != 8:
        return lax.all_gather(block, "dp", axis=0)
    me = lax.axis_index("dp")
    line, side = me // 2, me % 2
    near1 = lax.ppermute(block, "dp", along(1))
    near3 = lax.ppermute(block, "dp", along(3))
    near2 = lax.ppermute(block, "dp", along(2))
    far0 = lax.ppermute(block, "dp", SIDE_SWAP)
    far13 = lax.ppermute(jnp.stack([near1, near3]), "dp", SIDE_SWAP)
    far2 = lax.ppermute(near2, "dp", SIDE_SWAP)
    full = jnp.zeros((4, 2) + block.shape, block.dtype)
    zero = jnp.int32(0)
    for step, near, far in ((0, block, far0), (1, near1, far13[0]), (3, near3, far13[1]), (2, near2, far2)):
        pair = in_order(side == 1, near, far)
        full = lax.dynamic_update_slice(full, pair[None], ((line - step) % 4, zero, zero, zero))
    return full.reshape((n,) + block.shape)


def dp_reduce(block_of):
    n = lax.axis_size("dp")
    if n != 8:
        blocks = jnp.stack([block_of(jnp.int32(i)).astype(BF) for i in range(n)])
        return lax.psum_scatter(blocks, "dp", scatter_dimension=0).astype(F32)
    me = lax.axis_index("dp")
    line, side = me // 2, me % 2

    def over_side(*steps):
        targets = [2 * ((line + step) % 4) for step in steps]
        moved = lax.ppermute(jnp.stack([block_of(t + 1 - side) for t in targets]), "dp", SIDE_SWAP)
        return [block_of(t + side).astype(F32) + moved[j].astype(F32) for j, t in enumerate(targets)]

    (sum2,) = over_side(2)
    sum1, sum3 = over_side(1, 3)
    (sum0,) = over_side(0)
    got2 = lax.ppermute(sum2.astype(BF), "dp", along(2)).astype(F32)
    got1 = lax.ppermute(sum1.astype(BF), "dp", along(1)).astype(F32)
    got3 = lax.ppermute(sum3.astype(BF), "dp", along(3)).astype(F32)
    return sum0 + got1 + got2 + got3


def attention(queries, keys, values, d_out, segment, scale):
    tokens = queries.shape[1]
    index = jnp.arange(tokens, dtype=jnp.int32)
    allowed = (segment[:, None] == segment[None, :]) & (index[None, :] <= index[:, None])
    scores = dot("htd,hnd->htn", queries, keys) * scale
    masked = jnp.where(allowed[None], scores, NEGATIVE)
    top = jnp.max(masked, axis=-1, keepdims=True)
    weights = jnp.where(allowed[None], jnp.exp(masked - top), 0.0)
    probs = weights / jnp.sum(weights, axis=-1, keepdims=True)
    probs_r = probs.astype(BF)
    attended = dot("htn,hnd->htd", probs_r, values)
    d_probs = dot("htd,hnd->htn", d_out, values)
    delta = jnp.sum(probs * d_probs, axis=-1, keepdims=True)
    d_scores = (probs * (d_probs - delta)).astype(BF)
    d_queries = dot("htn,hnd->htd", d_scores, keys) * scale
    d_keys = dot("htn,htd->hnd", d_scores, queries) * scale
    d_values = dot("htn,htd->hnd", probs_r, d_out)
    return attended, d_queries, d_keys, d_values


def general_device(
    hidden_in,
    lengths,
    grad_out,
    attn_gain,
    attn_shift,
    mlp_gain,
    mlp_shift,
    qkv_weight,
    qkv_bias,
    dense_weight,
    dense_bias,
    up_weight,
    up_bias,
    down_weight,
    down_bias,
):
    n_dp, n_seq = lax.axis_size("dp"), lax.axis_size("seq")
    me = lax.axis_index("seq")
    rows, width = hidden_in.shape
    group = rows * n_seq
    scale = HEAD_DIM ** (-0.5)
    hidden_units = up_weight.shape[1]
    own_units = hidden_units // n_seq
    deep = width // (n_dp * n_seq)
    unit_rows = hidden_units // (n_dp * n_seq)
    heads = -(-HEADS // n_seq)
    own = heads * HEAD_DIM
    spare = heads * n_seq - HEADS

    def by_head(values):
        lead = values.shape[:-1]
        split = values.reshape(lead + (3, HEADS, HEAD_DIM))
        if spare:
            split = jnp.pad(split, [(0, 0)] * (len(lead) + 1) + [(0, spare), (0, 0)])
        split = split.reshape(lead + (3, n_seq, own))
        return jnp.moveaxis(split, -2, 0).reshape((n_seq,) + lead + (3 * own,))

    def from_heads(blocks):
        lead = blocks.shape[1:-1]
        split = jnp.moveaxis(blocks.reshape((n_seq,) + lead + (3, own)), 0, -2)
        split = split.reshape(lead + (3, HEADS + spare, HEAD_DIM))[..., :HEADS, :]
        return split.reshape(lead + (3 * width,))

    vectors = (attn_gain, attn_shift, mlp_gain, mlp_shift, qkv_bias, dense_bias, up_bias, down_bias)
    sizes = [v.shape[0] for v in vectors]
    length = sum(sizes)
    wide = own_units + 3 * own
    up_blocks = jnp.moveaxis(up_weight.reshape(deep, n_dp, n_seq, unit_rows), 2, 0)
    up_blocks = up_blocks.reshape(n_seq, deep, own_units)
    vector = jnp.pad(jnp.concatenate(vectors), (0, wide - length))
    blocks = jnp.concatenate(
        [
            jnp.concatenate([up_blocks, by_head(qkv_weight)], axis=2),
            jnp.broadcast_to(vector, (n_seq, 1, wide)),
        ],
        axis=1,
    )
    got = seq_exchange(blocks)
    per_line = n_seq * deep
    up_rows = per_line * own_units // width
    up_piece = got[:, :deep, :own_units].reshape(up_rows, width)
    qkv_piece = got[:, :deep, own_units:].reshape(per_line, 3 * own)
    group_vector = got[:, deep, :length]

    both = seq_gather(jnp.concatenate([hidden_in, grad_out], axis=0))
    hidden_group = both[:, :rows].reshape(group, width)
    grad_group = both[:, rows:].reshape(group, width)

    def beside(values):
        lead = values.shape[:-2]
        split = values.reshape(lead + (deep, n_seq, width // n_seq))
        return jnp.swapaxes(split, -3, -2).reshape(lead + (per_line, width // n_seq))

    def from_beside(values):
        lead = values.shape[:-2]
        split = values.reshape(lead + (n_seq, deep, width // n_seq))
        return jnp.swapaxes(split, -3, -2).reshape(lead + (deep, width))

    attn_wide = 3 * own + width // n_seq
    vec_rows = -(-n_seq * length // attn_wide)
    vec_rows += -vec_rows % 8
    vec_piece = jnp.pad(group_vector.reshape(-1), (0, vec_rows * attn_wide - n_seq * length))
    attn_piece = jnp.concatenate([qkv_piece, beside(dense_weight)], axis=1)
    attn_piece = jnp.concatenate([attn_piece, vec_piece.reshape(vec_rows, attn_wide)], axis=0)
    attn_all = dp_gather(attn_piece)
    mlp_all = dp_gather(jnp.concatenate([up_piece, down_weight], axis=0))
    qkv_full = attn_all[:, :per_line, : 3 * own].reshape(width, 3 * own)
    dense_rows = from_beside(attn_all[:, :per_line, 3 * own :]).reshape(n_dp * deep, width)
    up_full = mlp_all[:, :up_rows].reshape(width, own_units)
    down_full = mlp_all[:, up_rows:].reshape(own_units, width)
    every = attn_all[:, per_line:].reshape(n_dp, vec_rows * attn_wide)[:, : n_seq * length]
    every = every.reshape(n_dp * n_seq, length).astype(F32)
    whole = []
    start = 0
    for size in sizes:
        whole.append(every[:, start : start + size].reshape(-1))
        start += size
    f_attn_gain, f_attn_shift, f_mlp_gain, f_mlp_shift, f_qkv_bias, f_dense_bias, f_up_bias, f_down_bias = whole
    own_qkv_bias = pick(by_head(f_qkv_bias), me)
    own_up_bias = lax.dynamic_index_in_dim(
        f_up_bias.reshape(n_dp, n_seq, unit_rows), me, 1, keepdims=False
    ).reshape(-1)

    row_lengths = lengths[0]
    index = jnp.arange(group, dtype=jnp.int32)
    segment, position = place(row_lengths, index)
    angles = position.astype(F32)[:, None] * frequencies()[None, :]
    cosine = jnp.cos(angles)[:, None, :]
    sine = jnp.sin(angles)[:, None, :]

    tokens = hidden_group.astype(F32)
    center = jnp.mean(tokens, axis=-1, keepdims=True)
    centered = tokens - center
    spread = jnp.mean(centered * centered, axis=-1, keepdims=True)
    unit = centered * lax.rsqrt(spread + EPS)
    attn_in = (unit * f_attn_gain + f_attn_shift).astype(BF)
    mlp_in = (unit * f_mlp_gain + f_mlp_shift).astype(BF)

    joined = dot("td,de->te", attn_in, qkv_full) + own_qkv_bias
    joined = joined.reshape(group, 3, heads, HEAD_DIM)
    queries = jnp.moveaxis(rotate(joined[:, 0], cosine, sine, 1.0).astype(BF), 1, 0)
    keys = jnp.moveaxis(rotate(joined[:, 1], cosine, sine, 1.0).astype(BF), 1, 0)
    values = jnp.moveaxis(joined[:, 2].astype(BF), 1, 0)
    feature_rows = n_dp * deep
    direct = spare == 0 and own % per_line == 0
    d_rows = dot("fe,te->ft", dense_rows, grad_group).astype(BF)
    if direct:
        runs = own // per_line
        moved = seq_exchange(d_rows.reshape(n_seq, runs * deep, group))
        moved = moved.reshape(n_seq, runs, deep, group)
        d_attended = jnp.moveaxis(moved, 0, 1).reshape(heads, HEAD_DIM, group)
    else:
        moved = lax.all_gather(d_rows.reshape(n_dp, deep, group), "seq", axis=1)
        moved = moved.reshape(width, group)
        moved = jnp.pad(moved, ((0, spare * HEAD_DIM), (0, 0)))
        d_attended = pick(moved.reshape(n_seq, heads, HEAD_DIM, group), me)
    d_attended = jnp.swapaxes(d_attended, 1, 2)
    attended, d_queries, d_keys, d_values = attention(queries, keys, values, d_attended, segment, scale)
    attended = jnp.swapaxes(attended.astype(BF), 1, 2).reshape(own, group)
    if direct:
        given = jnp.moveaxis(attended.reshape(runs, n_seq, deep, group), 1, 0)
        rows_attended = seq_exchange(given.reshape(n_seq, runs * deep, group)).reshape(feature_rows, group)
    else:
        given = lax.all_gather(attended, "seq", axis=0, tiled=True)[:width]
        rows_attended = lax.dynamic_index_in_dim(
            given.reshape(n_dp, n_seq, deep, group), me, 1, keepdims=False
        ).reshape(feature_rows, group)
    attn_out = dot("ft,fe->te", rows_attended, dense_rows)
    dense_grad = dot("ft,te->fe", rows_attended, grad_group).astype(BF).reshape(n_dp, deep, width)
    d_queries = rotate(jnp.moveaxis(d_queries, 0, 1), cosine, sine, -1.0)
    d_keys = rotate(jnp.moveaxis(d_keys, 0, 1), cosine, sine, -1.0)
    d_joined = jnp.stack([d_queries, d_keys, jnp.moveaxis(d_values, 0, 1)], axis=1)
    d_joined = d_joined.astype(BF).reshape(group, 3 * own)
    qkv_grad = dot("td,te->de", attn_in, d_joined).astype(BF).reshape(n_dp, n_seq * deep, 3 * own)
    d_attn_in = dot("te,de->td", d_joined, qkv_full)
    attn_terms = jnp.concatenate([qkv_grad, beside(dense_grad)], axis=2)
    attn_sum = dp_reduce(lambda i: pick(attn_terms, i))

    upper = dot("td,df->tf", mlp_in, up_full) + own_up_bias
    cdf = 0.5 * (1.0 + lax.erf(upper * F32(0.7071067811865476)))
    pdf = jnp.exp(-0.5 * upper * upper) * F32(0.3989422804014327)
    act = (upper * cdf).astype(BF)
    d_act = dot("td,fd->tf", grad_group, down_full)
    d_up = (d_act * (cdf + upper * pdf)).astype(BF)
    down_grad = dot("tf,td->fd", act, grad_group).astype(BF).reshape(n_dp, unit_rows, width)
    up_grad = dot("td,tf->df", mlp_in, d_up).astype(BF).reshape(n_dp, up_rows, width)
    mlp_out = dot("tf,fd->td", act, down_full)
    d_mlp_in = dot("tf,df->td", d_up, up_full)

    mine = jnp.arange(n_seq) == me
    qkv_bias_grad = jnp.sum(d_joined.astype(F32), axis=0)
    qkv_bias_grad = from_heads(jnp.where(mine[:, None], qkv_bias_grad[None], 0.0))
    up_bias_grad = jnp.sum(d_up.astype(F32), axis=0).reshape(n_dp, 1, unit_rows)
    up_bias_grad = jnp.where(mine[None, :, None], up_bias_grad, 0.0)
    bias_sum = jnp.sum(grad_out.astype(F32), axis=0)
    terms = (
        jnp.sum(d_attn_in * unit, axis=0),
        jnp.sum(d_attn_in, axis=0),
        jnp.sum(d_mlp_in * unit, axis=0),
        jnp.sum(d_mlp_in, axis=0),
        qkv_bias_grad,
        bias_sum,
        up_bias_grad,
        bias_sum,
    )
    terms = [t.reshape(n_dp, n_seq, size) for t, size in zip(terms, sizes)]
    terms = jnp.concatenate(terms, axis=2).reshape(n_dp, n_seq * length)
    tail_rows = -(-n_seq * length // width)
    tail_rows += -tail_rows % 8
    terms = jnp.pad(terms, ((0, 0), (0, tail_rows * width - n_seq * length)))
    terms = terms.reshape(n_dp, tail_rows, width).astype(BF)
    mlp_sum = dp_reduce(lambda i: jnp.concatenate([pick(up_grad, i), pick(down_grad, i), pick(terms, i)], axis=0))

    upstream = d_attn_in * f_attn_gain + d_mlp_in * f_mlp_gain
    pair = jnp.concatenate([(attn_out + mlp_out).astype(BF), upstream.astype(BF)], axis=1)
    pair = seq_reduce(pair.reshape(n_seq, rows, 2 * width))
    block_out = hidden_in.astype(F32) + f_dense_bias + f_down_bias + pair[:, :width]
    upstream = pair[:, width:]
    x = hidden_in.astype(F32)
    centered = x - jnp.mean(x, axis=-1, keepdims=True)
    inverse = lax.rsqrt(jnp.mean(centered * centered, axis=-1, keepdims=True) + EPS)
    own_unit = centered * inverse
    inner = (
        upstream
        - jnp.mean(upstream, axis=-1, keepdims=True)
        - own_unit * jnp.mean(upstream * own_unit, axis=-1, keepdims=True)
    )
    grad_in = grad_out.astype(F32) + inverse * inner

    qkv_back = attn_sum[:, : 3 * own].reshape(n_seq, deep, 3 * own).astype(BF)
    qkv_own = from_heads(seq_exchange(qkv_back).astype(F32))
    dense_own = from_beside(attn_sum[:, 3 * own :])
    vec_sum = mlp_sum[up_rows + unit_rows :].reshape(-1)[: n_seq * length].reshape(n_seq, 1, length)
    vec_sum = jnp.pad(vec_sum, ((0, 0), (0, 0), (0, -length % own_units)))
    vec_sum = vec_sum.reshape(n_seq, -1, own_units)
    back = jnp.concatenate([mlp_sum[:up_rows].reshape(n_seq, deep, own_units), vec_sum], axis=1)
    back = seq_exchange(back.astype(BF)).astype(F32)
    up_own = jnp.moveaxis(back[:, :deep].reshape(n_seq, deep, n_dp, unit_rows), 0, 2)
    vec_own = jnp.sum(back[:, deep:].reshape(n_seq, -1), axis=0)
    owned = []
    start = 0
    for size in sizes:
        owned.append(vec_own[start : start + size])
        start += size
    return (
        block_out.astype(BF),
        grad_in.astype(BF),
        owned[0],
        owned[1],
        owned[2],
        owned[3],
        qkv_own,
        owned[4],
        dense_own,
        owned[5],
        up_own.reshape(deep, hidden_units),
        owned[6],
        mlp_sum[up_rows : up_rows + unit_rows],
        owned[7],
    )


SCALE = HEAD_DIM**-0.5


def kernel_call(body, outs, args, scratch=(), megabytes=24, flops=0):
    moved = sum(a.size * a.dtype.itemsize for a in args)
    return pl.pallas_call(
        body,
        out_shape=tuple(jax.ShapeDtypeStruct(shape, kind) for shape, kind in outs),
        scratch_shapes=[pltpu.VMEM(shape, kind) for shape, kind in scratch],
        compiler_params=pltpu.CompilerParams(vmem_limit_bytes=megabytes << 20),
        cost_estimate=pl.CostEstimate(flops=flops, bytes_accessed=moved, transcendentals=0),
    )(*args)


def dot_nn(a, b):
    return lax.dot_general(a, b, (((1,), (0,)), ((), ())), preferred_element_type=F32)


def dot_nt(a, b):
    return lax.dot_general(a, b, (((1,), (1,)), ((), ())), preferred_element_type=F32)


def dot_tn(a, b):
    return lax.dot_general(a, b, (((0,), (0,)), ((), ())), preferred_element_type=F32)


def line_and_side():
    me = lax.axis_index("dp")
    return lax.shift_right_logical(me, 1), lax.bitwise_and(me, 1)


def dp_index(line, step, side):
    return 2 * lax.bitwise_and(line + step, 3) + side


def dp_pieces(block):
    near1 = lax.ppermute(block, "dp", along(1))
    far0 = lax.ppermute(block, "dp", SIDE_SWAP)
    near3 = lax.ppermute(block, "dp", along(3))
    near2 = lax.ppermute(block, "dp", along(2))
    far1 = lax.ppermute(near1, "dp", SIDE_SWAP)
    far3 = lax.ppermute(near3, "dp", SIDE_SWAP)
    far2 = lax.ppermute(near2, "dp", SIDE_SWAP)
    return (block, far0, near1, far1, near3, far3, near2, far2)


def piece_owners():
    line, side = line_and_side()
    return [dp_index(line, step, s) for step in (0, 3, 1, 2) for s in (side, 1 - side)]


def dp_sum(send2, send13, send0, keep2, keep13, keep0):
    moved2 = lax.ppermute(send2, "dp", SIDE_SWAP)
    moved13 = lax.ppermute(send13, "dp", SIDE_SWAP)
    moved0 = lax.ppermute(send0, "dp", SIDE_SWAP)
    sum2 = (keep2.astype(F32) + moved2.astype(F32)).astype(BF)
    sum1 = (keep13[0].astype(F32) + moved13[0].astype(F32)).astype(BF)
    sum3 = (keep13[1].astype(F32) + moved13[1].astype(F32)).astype(BF)
    got2 = lax.ppermute(sum2, "dp", along(2))
    got1 = lax.ppermute(sum1, "dp", along(1))
    got3 = lax.ppermute(sum3, "dp", along(3))
    total = keep0.astype(F32) + moved0.astype(F32)
    return total + got2.astype(F32) + got1.astype(F32) + got3.astype(F32)


def pick_blocks(block_of, send2, send13, send0, keep2, keep13, keep0):
    line, side = line_and_side()
    for far, (r2, r13, r0) in ((True, (send2, send13, send0)), (False, (keep2, keep13, keep0))):
        s = 1 - side if far else side
        r2[...] = block_of(dp_index(line, 2, s))
        r13[0] = block_of(dp_index(line, 1, s))
        r13[1] = block_of(dp_index(line, 3, s))
        r0[...] = block_of(dp_index(line, 0, s))


def pick_shapes(rows, width):
    one, two = ((rows, width), BF), ((2, rows, width), BF)
    return (one, two, one, one, two, one)


def seq_shuffle(blocks):
    got = [blocks[0]]
    for other in (1, 2, 3):
        pairs = [(i, i ^ other) for i in range(4)]
        got.append(lax.ppermute(blocks[other], "seq", pairs))
    return got


def place_kernel(deep, *refs):
    pieces, (dy, weights, dense, vectors), d_blocks, (rows32, d_rows) = refs[:8], refs[8:12], refs[12:16], refs[16:]
    per_line = 4 * deep
    quarter = dy.shape[1] // 4
    own = weights.shape[1] - quarter
    total = jnp.zeros(vectors.shape, F32)
    for piece, owner in zip(pieces, piece_owners()):
        weights[pl.ds(pl.multiple_of(owner * per_line, per_line), per_line), :] = piece[:per_line, :]
        total = total + piece[per_line:, :].astype(F32)
        beside = piece[:per_line, own:].astype(F32)
        for q in range(4):
            rows32[pl.ds(pl.multiple_of(owner * deep, 8), deep), q * quarter : (q + 1) * quarter] = beside[
                q * deep : (q + 1) * deep
            ]
    vectors[...] = total
    dense[...] = rows32[...].astype(BF)
    d_rows[...] = dot_nt(dense[...], dy[...]).astype(BF)
    me = lax.axis_index("seq")
    count = d_blocks[0].shape[0]
    for j in range(4):
        d_blocks[j][...] = d_rows[pl.ds(pl.multiple_of(lax.bitwise_xor(me, j) * count, 16), count), :]


def turn(values, cosine, sine_a, sine_b, sign):
    half = ROT // 2
    ahead = pltpu.roll(values, 128 - half, 1)
    behind = pltpu.roll(values, half, 1)
    return values * cosine + sign * (ahead * sine_a + behind * sine_b)


def project_kernel(unit, weights, vectors, cosine, sine_a, sine_b, attn_in, qk, v):
    gain, shift, bias = vectors[0:1, :], vectors[1:2, :], vectors[6:7, :]
    turned = qk.shape[1]
    size = 128

    def step(i, carry):
        rows = pl.ds(pl.multiple_of(i * size, size), size)
        normed = (unit[rows, :] * gain + shift).astype(BF)
        attn_in[rows, :] = normed
        joined = dot_nn(normed, weights[...]) + bias
        tables = cosine[rows, :], sine_a[rows, :], sine_b[rows, :]
        for c in range(0, turned, 128):
            qk[rows, c : c + 128] = turn(joined[:, c : c + 128], *tables, 1.0).astype(BF)
        v[rows, :] = joined[:, turned : turned + v.shape[1]].astype(BF)
        return carry

    lax.fori_loop(0, unit.shape[0] // size, step, 0)


def attention_kernel(deep, *refs):
    qk, v, d0, d1, d2, d3, seg_column, seg_row, cosine, sine_a, sine_b = refs[:11]
    given, d_joined, (d_t, out_t, dk_t, dv_t, acc) = refs[11:15], refs[15], refs[16:]
    tokens, own = v.shape
    me = lax.axis_index("seq")
    runs = own // (4 * deep)
    for j, ref in enumerate((d0, d1, d2, d3)):
        source = lax.bitwise_xor(me, j)
        block = ref[...].astype(F32)
        for r in range(runs):
            place = pl.multiple_of(r * 4 * deep + source * deep, 8)
            d_t[pl.ds(place, deep), :] = block[r * deep : (r + 1) * deep]
    d_out = jnp.transpose(d_t[...]).astype(BF)
    q_t = jnp.transpose(qk[:, :own].astype(F32)).astype(BF)
    d_tb = d_t[...].astype(BF)
    dk_t[...] = jnp.zeros(dk_t.shape, F32)
    dv_t[...] = jnp.zeros(dv_t.shape, F32)
    size = 256
    for h in range(own // HEAD_DIM):
        lanes = slice(h * HEAD_DIM, (h + 1) * HEAD_DIM)
        q_h = qk[:, lanes]
        k_h = qk[:, own + h * HEAD_DIM : own + (h + 1) * HEAD_DIM]
        v_h = v[:, lanes]
        d_h = d_out[:, lanes]
        for first in range(0, tokens, size):
            rows = slice(first, first + size)
            n = first + size
            scores = dot_nt(q_h[rows], k_h[:n]) * SCALE
            query = lax.broadcasted_iota(jnp.int32, (size, n), 0) + first
            key = lax.broadcasted_iota(jnp.int32, (size, n), 1)
            allowed = (seg_column[rows, :] == seg_row[:, :n]) & (key <= query)
            scores = jnp.where(allowed, scores, NEGATIVE)
            weights = jnp.where(allowed, jnp.exp(scores - jnp.max(scores, axis=1, keepdims=True)), 0.0)
            probs = weights * (1.0 / jnp.sum(weights, axis=1, keepdims=True))
            probs_r = probs.astype(BF)
            out_t[lanes, rows] = jnp.transpose(dot_nn(probs_r, v_h[:n]))
            d_probs = dot_nt(d_h[rows], v_h[:n])
            delta = jnp.sum(probs * d_probs, axis=1, keepdims=True)
            d_scores = (probs * (d_probs - delta)).astype(BF)
            acc[rows, lanes] = dot_nn(d_scores, k_h[:n]) * SCALE
            dk_t[lanes, :n] += dot_nn(q_t[lanes, rows], d_scores)
            dv_t[lanes, :n] += dot_nn(d_tb[lanes, rows], probs_r)
    acc[:, own : 2 * own] = jnp.transpose(dk_t[...]) * SCALE
    for c in range(0, 2 * own, 128):
        turned = turn(acc[:, c : c + 128], cosine[...], sine_a[...], sine_b[...], -1.0)
        d_joined[:, c : c + 128] = turned.astype(BF)
    d_joined[:, 2 * own : 3 * own] = jnp.transpose(dv_t[...]).astype(BF)
    d_joined[:, 3 * own :] = jnp.zeros((tokens, d_joined.shape[1] - 3 * own), BF)
    for j in range(4):
        target = lax.bitwise_xor(me, j)
        parts = [out_t[pl.ds(pl.multiple_of(r * 4 * deep + target * deep, 8), deep), :] for r in range(runs)]
        given[j][...] = jnp.concatenate(parts, axis=0).astype(BF)


def attention_grads_kernel(deep, *refs):
    r0, r1, r2, r3, dense, dy, attn_in, d_joined, weights, unit, vectors = refs[:11]
    picks, (attn_out, scaled, sums), (rows_t, grads) = refs[11:17], refs[17:20], refs[20:]
    me = lax.axis_index("seq")
    count = r0.shape[0]
    width = dy.shape[1]
    quarter = width // 4
    own = width - quarter
    for j, ref in enumerate((r0, r1, r2, r3)):
        rows_t[pl.ds(pl.multiple_of(lax.bitwise_xor(me, j) * count, 16), count), :] = ref[...]
    size = 128
    for c in range(0, width, size):
        grads[c : c + size, :] = dot_tn(attn_in[:, c : c + size], d_joined[...])
    dense_grad = dot_nn(rows_t[...], dy[...])
    for p in range(8):
        for q in range(4):
            start = p * 4 * deep + q * deep
            grads[start : start + deep, own:] = dense_grad[p * deep : (p + 1) * deep, q * quarter : (q + 1) * quarter]
    per_line = 4 * deep

    def block_of(index):
        return grads[pl.ds(pl.multiple_of(index * per_line, per_line), per_line), :].astype(BF)

    pick_blocks(block_of, *picks)
    attended = jnp.transpose(rows_t[...].astype(F32)).astype(BF)
    gain = vectors[0:1, :]
    tokens = dy.shape[0]
    sums[...] = jnp.zeros(sums.shape, F32)
    for c in range(0, tokens, size):
        rows = slice(c, c + size)
        attn_out[rows, :] = dot_nn(attended[rows], dense[...])
        back = dot_nt(d_joined[rows, :], weights[...])
        scaled[rows, :] = back * gain
        sums[0:1, :] += jnp.sum(back * unit[rows, :], axis=0, keepdims=True)
        sums[1:2, :] += jnp.sum(back, axis=0, keepdims=True)
        sums[5:6, :] += jnp.sum(d_joined[rows, :].astype(F32), axis=0, keepdims=True)


def mlp_kernel(per_line, *refs):
    pieces, (unit, dy, vectors, attn_out, scaled, sums_in) = refs[:8], refs[8:14]
    picks, (give, keep), scratch = refs[14:20], refs[20:22], refs[22:]
    up, down, mlp_in, act, d_up, up_grad, down_grad, pair, sums = scratch
    for piece, owner in zip(pieces, piece_owners()):
        rows = pl.ds(pl.multiple_of(owner * per_line, per_line), per_line)
        up[rows, :] = piece[:per_line, :]
        down[rows, :] = piece[per_line:, :]
    gain, shift, bias = vectors[2:3, :], vectors[3:4, :], vectors[7:8, :]
    sums[...] = sums_in[...]
    tokens, width = dy.shape
    size = tokens // 4

    def step(i, carry):
        rows = pl.ds(pl.multiple_of(i * size, size), size)
        u = unit[rows, :]
        normed = (u * gain + shift).astype(BF)
        mlp_in[rows, :] = normed
        upper = dot_nn(normed, up[...]) + bias
        cdf = 0.5 * (1.0 + lax.erf(upper * 0.7071067811865476))
        pdf = jnp.exp(-0.5 * upper * upper) * 0.3989422804014327
        act_rows = (upper * cdf).astype(BF)
        act[rows, :] = act_rows
        g = dy[rows, :]
        d_rows = (dot_nt(g, down[...]) * (cdf + upper * pdf)).astype(BF)
        d_up[rows, :] = d_rows
        pair[i, :, :width] = dot_nn(act_rows, down[...]) + attn_out[rows, :]
        back = dot_nt(d_rows, up[...])
        pair[i, :, width:] = back * gain + scaled[rows, :]
        sums[2:3, :] += jnp.sum(back * u, axis=0, keepdims=True)
        sums[3:4, :] += jnp.sum(back, axis=0, keepdims=True)
        sums[4:5, :] += 0.25 * jnp.sum(g.astype(F32), axis=0, keepdims=True)
        sums[6:7, :] += jnp.sum(d_rows.astype(F32), axis=0, keepdims=True)
        return carry

    lax.fori_loop(0, 4, step, 0)
    core = lax.bitwise_and(lax.axis_index("seq"), 1)
    for chip in range(2):
        give[chip] = pair[2 * chip + 1 - core].astype(BF)
        keep[chip] = pair[2 * chip + core]
    for c in range(0, width, 128):
        up_grad[c : c + 128, :] = dot_tn(mlp_in[:, c : c + 128], d_up[...]).astype(BF)
        down_grad[c : c + 128, :] = dot_tn(act[:, c : c + 128], dy[...]).astype(BF)
    tail = sums[...].astype(BF)

    def block_of(index):
        rows = pl.ds(pl.multiple_of(index * per_line, per_line), per_line)
        return jnp.concatenate([up_grad[rows, :], down_grad[rows, :], tail], axis=0)

    pick_blocks(block_of, *picks)


def line_device(
    hidden_in,
    lengths,
    grad_out,
    attn_gain,
    attn_shift,
    mlp_gain,
    mlp_shift,
    qkv_weight,
    qkv_bias,
    dense_weight,
    dense_bias,
    up_weight,
    up_bias,
    down_weight,
    down_bias,
):
    n_dp, n_seq = 8, 4
    dp_me, me = lax.axis_index("dp"), lax.axis_index("seq")
    device = dp_me * n_seq + me
    zero = jnp.int32(0)
    rows, width = hidden_in.shape
    group = rows * n_seq
    hidden_units = up_weight.shape[1]
    own_units = hidden_units // n_seq
    deep = width // (n_dp * n_seq)
    per_line = n_seq * deep
    unit_rows = hidden_units // (n_dp * n_seq)
    own = width // n_seq
    heads = own // HEAD_DIM
    wide = own_units + 3 * own

    def by_head(values):
        split = values.reshape(values.shape[0], 3, n_seq, own)
        return jnp.moveaxis(split, 2, 0).reshape(n_seq, values.shape[0], 3 * own)

    def from_heads(blocks):
        split = jnp.moveaxis(blocks.reshape(n_seq, -1, 3, own), 0, 2)
        return split.reshape(-1, 3 * width)

    def spread(values, length, place):
        empty = jnp.zeros((values.shape[0], length), values.dtype)
        return lax.dynamic_update_slice(empty, values, (zero, place))

    up_blocks = jnp.moveaxis(up_weight.reshape(deep, n_dp, n_seq, unit_rows), 2, 0)
    up_blocks = up_blocks.reshape(n_seq, deep, own_units)
    by_width = jnp.stack([attn_gain, attn_shift, mlp_gain, mlp_shift, dense_bias, down_bias])
    by_width = jnp.pad(spread(by_width, width, device * deep), ((0, 2), (0, 0)))
    bias_row = spread(qkv_bias[None], 3 * width, device * qkv_bias.shape[0])
    bias_row = jnp.pad(by_head(bias_row), ((0, 0), (6, 1), (0, 0)))
    left = jnp.concatenate([up_blocks, jnp.broadcast_to(by_width, (n_seq,) + by_width.shape)], axis=1)
    right = jnp.concatenate([by_head(qkv_weight), bias_row], axis=1)
    got = seq_exchange(jnp.concatenate([left, right], axis=2))
    up_piece = got[:, :deep, :own_units].reshape(per_line, own_units)
    qkv_piece = got[:, :deep, own_units:].reshape(per_line, 3 * own)
    extra = jnp.sum(got[:, deep:].astype(F32), axis=0)
    up_row = spread(up_bias[None].astype(F32), own_units, dp_me * unit_rows)
    extra = (
        extra[:, :width]
        + jnp.pad(extra[:, own_units:], ((0, 0), (0, width - 3 * own)))
        + jnp.pad(up_row, ((7, 0), (0, 0)))
    ).astype(BF)
    beside = jnp.swapaxes(dense_weight.reshape(deep, n_seq, own), 0, 1).reshape(per_line, own)
    attn_piece = jnp.concatenate([jnp.concatenate([qkv_piece, beside], axis=1), extra], axis=0)
    attn_pieces = dp_pieces(attn_piece)
    mlp_pieces = dp_pieces(jnp.concatenate([up_piece, down_weight], axis=0))

    both = seq_gather(jnp.concatenate([hidden_in, grad_out], axis=0))
    hidden_group = both[:, :rows].reshape(group, width)
    dy = both[:, rows:].reshape(group, width)

    row_lengths = lengths[0]
    segment, position = place(row_lengths, jnp.arange(group, dtype=jnp.int32))
    lane = jnp.arange(128, dtype=jnp.int32) % HEAD_DIM
    powers = jnp.power(F32(10000.0), -(2.0 * (lane % (ROT // 2)).astype(F32)) / ROT)
    angles = position.astype(F32)[:, None] * powers[None, :]
    cosine = jnp.where(lane < ROT, jnp.cos(angles), 1.0)
    sine = jnp.sin(angles)
    sine_a = jnp.where(lane < ROT // 2, -sine, 0.0)
    sine_b = jnp.where((lane >= ROT // 2) & (lane < ROT), sine, 0.0)

    def normed(values):
        centered = values - jnp.mean(values, axis=-1, keepdims=True)
        inverse = lax.rsqrt(jnp.mean(centered * centered, axis=-1, keepdims=True) + EPS)
        return centered * inverse, inverse

    unit = normed(hidden_group.astype(F32))[0]

    flat = (group, width)
    placed = kernel_call(
        functools.partial(place_kernel, deep),
        ((flat[1:] * 2, BF), ((n_dp * deep, width), BF), ((8, width), F32)) + (((2 * deep, group), BF),) * 4,
        attn_pieces + (dy,),
        scratch=(((n_dp * deep, width), F32), ((n_dp * deep, group), BF)),
        flops=2 * n_dp * deep * width * group,
    )
    weights, dense, vectors = placed[:3]
    d_blocks = seq_shuffle(placed[3:])
    attn_in, qk, v = kernel_call(
        project_kernel,
        ((flat, BF), ((group, 2 * own), BF), ((group, own), BF)),
        (unit, weights, vectors, cosine, sine_a, sine_b),
        flops=2 * group * width * width,
    )
    attended = kernel_call(
        functools.partial(attention_kernel, deep),
        (((2 * deep, group), BF),) * 4 + ((flat, BF),),
        (qk, v, *d_blocks, segment[:, None], segment[None, :], cosine, sine_a, sine_b),
        scratch=(((own, group), F32),) * 4 + ((flat, F32),),
        flops=14 * group * group * own,
    )
    d_joined = attended[4]
    row_blocks = seq_shuffle(attended[:4])
    results = kernel_call(
        functools.partial(attention_grads_kernel, deep),
        pick_shapes(per_line, width) + ((flat, F32), (flat, F32), ((8, width), F32)),
        (*row_blocks, dense, dy, attn_in, d_joined, weights, unit, vectors),
        scratch=(((n_dp * deep, group), BF), ((width, width), F32)),
        flops=5 * group * width * width,
        megabytes=32,
    )
    attn_sum = dp_sum(*results[:6])

    results = kernel_call(
        functools.partial(mlp_kernel, per_line),
        pick_shapes(per_line + unit_rows + 8, width) + (((2, rows, 2 * width), BF), ((2, rows, 2 * width), F32)),
        (*mlp_pieces, unit, dy, vectors) + tuple(results[6:]),
        scratch=(
            ((width, own_units), BF),
            ((own_units, width), BF),
            (flat, BF),
            ((group, own_units), BF),
            ((group, own_units), BF),
            ((width, own_units), BF),
            ((own_units, width), BF),
            ((n_seq, rows, 2 * width), F32),
            ((8, width), F32),
        ),
        flops=12 * group * width * own_units,
        megabytes=40,
    )
    mlp_sum = dp_sum(*results[:6])
    give, keep = results[6:]

    chip = lax.shift_right_logical(me, 1)
    both = keep + lax.ppermute(give, "seq", CORE_SWAP).astype(F32)
    far = lax.ppermute(pick(both, 1 - chip).astype(BF), "seq", CHIP_SWAP)
    pair = pick(both, chip) + far.astype(F32)
    x = hidden_in.astype(F32)
    block_out = x + vectors[4] + vectors[5] + pair[:, :width]
    upstream = pair[:, width:]
    own_unit, inverse = normed(x)
    inner = (
        upstream
        - jnp.mean(upstream, axis=-1, keepdims=True)
        - own_unit * jnp.mean(upstream * own_unit, axis=-1, keepdims=True)
    )
    grad_in = grad_out.astype(F32) + inverse * inner

    qkv_back = attn_sum[:, : 3 * own].reshape(n_seq, deep, 3 * own).astype(BF)
    qkv_own = from_heads(seq_exchange(qkv_back).astype(F32))
    dense_own = attn_sum[:, 3 * own :].reshape(n_seq, deep, own)
    dense_own = jnp.swapaxes(dense_own, 0, 1).reshape(deep, width)
    tail = mlp_sum[per_line + unit_rows :]
    back = jnp.concatenate(
        [mlp_sum[:per_line].reshape(n_seq, deep, own_units), jnp.broadcast_to(tail, (n_seq,) + tail.shape)], axis=1
    )
    back = seq_exchange(back.astype(BF)).astype(F32)
    up_own = jnp.moveaxis(back[:, :deep].reshape(n_seq, deep, n_dp, unit_rows), 0, 2)
    by_width = jnp.sum(back[:, deep : deep + 5], axis=0)
    by_width = lax.dynamic_slice(by_width, (zero, device * deep), (5, deep))
    qkv_bias_grad = from_heads(back[:, deep + 5 : deep + 6, : 3 * own])[0]
    qkv_bias_grad = lax.dynamic_slice(qkv_bias_grad, (device * qkv_bias.shape[0],), qkv_bias.shape)
    up_bias_grad = lax.dynamic_slice(tail[6], (dp_me * unit_rows,), (unit_rows,))
    return (
        block_out.astype(BF),
        grad_in.astype(BF),
        by_width[0],
        by_width[1],
        by_width[2],
        by_width[3],
        qkv_own,
        qkv_bias_grad,
        dense_own,
        by_width[4],
        up_own.reshape(deep, hidden_units),
        up_bias_grad,
        mlp_sum[per_line : per_line + unit_rows],
        by_width[4],
    )


def per_device(*args):
    if lax.axis_size("dp") == 8 and lax.axis_size("seq") == 4:
        return line_device(*args)
    return general_device(*args)


def solution(mesh):
    both = ("dp", "seq")
    matrix, vector = P(both, None), P(both)
    params = (vector, vector, vector, vector, matrix, vector, matrix, vector, matrix, vector, matrix, vector)
    return jax.shard_map(
        per_device,
        mesh=mesh,
        in_specs=(matrix, P("dp", None), matrix) + params,
        out_specs=(matrix, matrix) + params,
        check_vma=False,
    )
```

```python
import functools

import jax
import jax.numpy as jnp
from jax import lax
from jax.experimental import pallas as pl
from jax.experimental.pallas import tpu as pltpu
from jax.sharding import PartitionSpec as P

HEADS = 12
HEAD_DIM = 64
ROT = 16
EPS = 1e-05
NEGATIVE = -1e30
BF = jnp.bfloat16
F32 = jnp.float32


def dot(spec, a, b):
    return jnp.einsum(spec, a, b, preferred_element_type=F32)


def frequencies():
    steps = jnp.arange(ROT // 2, dtype=F32)
    return jnp.power(F32(10000.0), -(2.0 * steps) / ROT)


def rotate(values, cosine, sine, sign):
    half = ROT // 2
    first = values[..., :half]
    second = values[..., half:ROT]
    turned_one = first * cosine - sign * second * sine
    turned_two = second * cosine + sign * first * sine
    return jnp.concatenate([turned_one, turned_two, values[..., ROT:]], axis=-1)


def place(row_lengths, index):
    ends = jnp.cumsum(row_lengths)
    after = (index[:, None] >= ends[None, :]).astype(jnp.int32)
    segment = jnp.sum(after, axis=1)
    start = jnp.sum(after * row_lengths[None, :], axis=1)
    return (segment, index - start)


def pick(values, index):
    return lax.dynamic_index_in_dim(values, index, 0, keepdims=False)


CHIP_SWAP = [(0, 2), (2, 0), (1, 3), (3, 1)]
CORE_SWAP = [(0, 1), (1, 0), (2, 3), (3, 2)]


def in_order(second, mine, other, axis=0):
    return jnp.stack([jnp.where(second, other, mine), jnp.where(second, mine, other)], axis=axis)


def seq_exchange(blocks):
    n = lax.axis_size("seq")
    if n != 4:
        return lax.all_to_all(blocks, "seq", 0, 0)
    me = lax.axis_index("seq")
    chip, core = me // 2, me % 2
    halves = blocks.reshape((2, 2) + blocks.shape[1:])
    far = lax.ppermute(pick(halves, 1 - chip), "seq", CHIP_SWAP)
    by_chip = in_order(chip == 1, pick(halves, chip), far, axis=1)
    other = lax.ppermute(pick(by_chip, 1 - core), "seq", CORE_SWAP)
    return in_order(core == 1, pick(by_chip, core), other, axis=1).reshape(blocks.shape)


def seq_gather(values):
    n = lax.axis_size("seq")
    if n != 4:
        return lax.all_gather(values, "seq", axis=0)
    me = lax.axis_index("seq")
    chip, core = me // 2, me % 2
    far = lax.ppermute(values, "seq", CHIP_SWAP)
    mine = in_order(chip == 1, values, far)
    other = lax.ppermute(mine, "seq", CORE_SWAP)
    return in_order(core == 1, mine, other, axis=1).reshape((n,) + values.shape)


def seq_reduce(values):
    n = lax.axis_size("seq")
    if n != 4:
        return lax.psum_scatter(values.astype(BF), "seq", scatter_dimension=0).astype(F32)
    me = lax.axis_index("seq")
    chip, core = me // 2, me % 2
    parts = values.reshape((2, 2) + values.shape[1:])
    keep = lax.dynamic_index_in_dim(parts, core, 1, keepdims=False)
    give = lax.dynamic_index_in_dim(parts, 1 - core, 1, keepdims=False).astype(BF)
    both = keep.astype(F32) + lax.ppermute(give, "seq", CORE_SWAP).astype(F32)
    far = lax.ppermute(pick(both, 1 - chip).astype(BF), "seq", CHIP_SWAP)
    return pick(both, chip) + far.astype(F32)


SIDE_SWAP = [(i, i ^ 1) for i in range(8)]


def along(step):
    return [(i, (i + 2 * step) % 8) for i in range(8)]


def dp_gather(block):
    n = lax.axis_size("dp")
    if n != 8:
        return lax.all_gather(block, "dp", axis=0)
    me = lax.axis_index("dp")
    line, side = me // 2, me % 2
    near1 = lax.ppermute(block, "dp", along(1))
    near3 = lax.ppermute(block, "dp", along(3))
    near2 = lax.ppermute(block, "dp", along(2))
    far0 = lax.ppermute(block, "dp", SIDE_SWAP)
    far13 = lax.ppermute(jnp.stack([near1, near3]), "dp", SIDE_SWAP)
    far2 = lax.ppermute(near2, "dp", SIDE_SWAP)
    full = jnp.zeros((4, 2) + block.shape, block.dtype)
    zero = jnp.int32(0)
    for step, near, far in ((0, block, far0), (1, near1, far13[0]), (3, near3, far13[1]), (2, near2, far2)):
        pair = in_order(side == 1, near, far)
        full = lax.dynamic_update_slice(full, pair[None], ((line - step) % 4, zero, zero, zero))
    return full.reshape((n,) + block.shape)


def dp_reduce(block_of):
    n = lax.axis_size("dp")
    if n != 8:
        blocks = jnp.stack([block_of(jnp.int32(i)).astype(BF) for i in range(n)])
        return lax.psum_scatter(blocks, "dp", scatter_dimension=0).astype(F32)
    me = lax.axis_index("dp")
    line, side = me // 2, me % 2

    def over_side(*steps):
        targets = [2 * ((line + step) % 4) for step in steps]
        moved = lax.ppermute(jnp.stack([block_of(t + 1 - side) for t in targets]), "dp", SIDE_SWAP)
        return [block_of(t + side).astype(F32) + moved[j].astype(F32) for j, t in enumerate(targets)]

    (sum2,) = over_side(2)
    sum1, sum3 = over_side(1, 3)
    (sum0,) = over_side(0)
    got2 = lax.ppermute(sum2.astype(BF), "dp", along(2)).astype(F32)
    got1 = lax.ppermute(sum1.astype(BF), "dp", along(1)).astype(F32)
    got3 = lax.ppermute(sum3.astype(BF), "dp", along(3)).astype(F32)
    return sum0 + got1 + got2 + got3


def attention(queries, keys, values, d_out, segment, scale):
    tokens = queries.shape[1]
    index = jnp.arange(tokens, dtype=jnp.int32)
    allowed = (segment[:, None] == segment[None, :]) & (index[None, :] <= index[:, None])
    scores = dot("htd,hnd->htn", queries, keys) * scale
    masked = jnp.where(allowed[None], scores, NEGATIVE)
    top = jnp.max(masked, axis=-1, keepdims=True)
    weights = jnp.where(allowed[None], jnp.exp(masked - top), 0.0)
    probs = weights / jnp.sum(weights, axis=-1, keepdims=True)
    probs_r = probs.astype(BF)
    attended = dot("htn,hnd->htd", probs_r, values)
    d_probs = dot("htd,hnd->htn", d_out, values)
    delta = jnp.sum(probs * d_probs, axis=-1, keepdims=True)
    d_scores = (probs * (d_probs - delta)).astype(BF)
    d_queries = dot("htn,hnd->htd", d_scores, keys) * scale
    d_keys = dot("htn,htd->hnd", d_scores, queries) * scale
    d_values = dot("htn,htd->hnd", probs_r, d_out)
    return attended, d_queries, d_keys, d_values


def general_device(
    hidden_in,
    lengths,
    grad_out,
    attn_gain,
    attn_shift,
    mlp_gain,
    mlp_shift,
    qkv_weight,
    qkv_bias,
    dense_weight,
    dense_bias,
    up_weight,
    up_bias,
    down_weight,
    down_bias,
):
    n_dp, n_seq = lax.axis_size("dp"), lax.axis_size("seq")
    me = lax.axis_index("seq")
    rows, width = hidden_in.shape
    group = rows * n_seq
    scale = HEAD_DIM ** (-0.5)
    hidden_units = up_weight.shape[1]
    own_units = hidden_units // n_seq
    deep = width // (n_dp * n_seq)
    unit_rows = hidden_units // (n_dp * n_seq)
    heads = -(-HEADS // n_seq)
    own = heads * HEAD_DIM
    spare = heads * n_seq - HEADS

    def by_head(values):
        lead = values.shape[:-1]
        split = values.reshape(lead + (3, HEADS, HEAD_DIM))
        if spare:
            split = jnp.pad(split, [(0, 0)] * (len(lead) + 1) + [(0, spare), (0, 0)])
        split = split.reshape(lead + (3, n_seq, own))
        return jnp.moveaxis(split, -2, 0).reshape((n_seq,) + lead + (3 * own,))

    def from_heads(blocks):
        lead = blocks.shape[1:-1]
        split = jnp.moveaxis(blocks.reshape((n_seq,) + lead + (3, own)), 0, -2)
        split = split.reshape(lead + (3, HEADS + spare, HEAD_DIM))[..., :HEADS, :]
        return split.reshape(lead + (3 * width,))

    vectors = (attn_gain, attn_shift, mlp_gain, mlp_shift, qkv_bias, dense_bias, up_bias, down_bias)
    sizes = [v.shape[0] for v in vectors]
    length = sum(sizes)
    wide = own_units + 3 * own
    up_blocks = jnp.moveaxis(up_weight.reshape(deep, n_dp, n_seq, unit_rows), 2, 0)
    up_blocks = up_blocks.reshape(n_seq, deep, own_units)
    vector = jnp.pad(jnp.concatenate(vectors), (0, wide - length))
    blocks = jnp.concatenate(
        [
            jnp.concatenate([up_blocks, by_head(qkv_weight)], axis=2),
            jnp.broadcast_to(vector, (n_seq, 1, wide)),
        ],
        axis=1,
    )
    got = seq_exchange(blocks)
    per_line = n_seq * deep
    up_rows = per_line * own_units // width
    up_piece = got[:, :deep, :own_units].reshape(up_rows, width)
    qkv_piece = got[:, :deep, own_units:].reshape(per_line, 3 * own)
    group_vector = got[:, deep, :length]

    both = seq_gather(jnp.concatenate([hidden_in, grad_out], axis=0))
    hidden_group = both[:, :rows].reshape(group, width)
    grad_group = both[:, rows:].reshape(group, width)

    def beside(values):
        lead = values.shape[:-2]
        split = values.reshape(lead + (deep, n_seq, width // n_seq))
        return jnp.swapaxes(split, -3, -2).reshape(lead + (per_line, width // n_seq))

    def from_beside(values):
        lead = values.shape[:-2]
        split = values.reshape(lead + (n_seq, deep, width // n_seq))
        return jnp.swapaxes(split, -3, -2).reshape(lead + (deep, width))

    attn_wide = 3 * own + width // n_seq
    vec_rows = -(-n_seq * length // attn_wide)
    vec_rows += -vec_rows % 8
    vec_piece = jnp.pad(group_vector.reshape(-1), (0, vec_rows * attn_wide - n_seq * length))
    attn_piece = jnp.concatenate([qkv_piece, beside(dense_weight)], axis=1)
    attn_piece = jnp.concatenate([attn_piece, vec_piece.reshape(vec_rows, attn_wide)], axis=0)
    attn_all = dp_gather(attn_piece)
    mlp_all = dp_gather(jnp.concatenate([up_piece, down_weight], axis=0))
    qkv_full = attn_all[:, :per_line, : 3 * own].reshape(width, 3 * own)
    dense_rows = from_beside(attn_all[:, :per_line, 3 * own :]).reshape(n_dp * deep, width)
    up_full = mlp_all[:, :up_rows].reshape(width, own_units)
    down_full = mlp_all[:, up_rows:].reshape(own_units, width)
    every = attn_all[:, per_line:].reshape(n_dp, vec_rows * attn_wide)[:, : n_seq * length]
    every = every.reshape(n_dp * n_seq, length).astype(F32)
    whole = []
    start = 0
    for size in sizes:
        whole.append(every[:, start : start + size].reshape(-1))
        start += size
    f_attn_gain, f_attn_shift, f_mlp_gain, f_mlp_shift, f_qkv_bias, f_dense_bias, f_up_bias, f_down_bias = whole
    own_qkv_bias = pick(by_head(f_qkv_bias), me)
    own_up_bias = lax.dynamic_index_in_dim(
        f_up_bias.reshape(n_dp, n_seq, unit_rows), me, 1, keepdims=False
    ).reshape(-1)

    row_lengths = lengths[0]
    index = jnp.arange(group, dtype=jnp.int32)
    segment, position = place(row_lengths, index)
    angles = position.astype(F32)[:, None] * frequencies()[None, :]
    cosine = jnp.cos(angles)[:, None, :]
    sine = jnp.sin(angles)[:, None, :]

    tokens = hidden_group.astype(F32)
    center = jnp.mean(tokens, axis=-1, keepdims=True)
    centered = tokens - center
    spread = jnp.mean(centered * centered, axis=-1, keepdims=True)
    unit = centered * lax.rsqrt(spread + EPS)
    attn_in = (unit * f_attn_gain + f_attn_shift).astype(BF)
    mlp_in = (unit * f_mlp_gain + f_mlp_shift).astype(BF)

    joined = dot("td,de->te", attn_in, qkv_full) + own_qkv_bias
    joined = joined.reshape(group, 3, heads, HEAD_DIM)
    queries = jnp.moveaxis(rotate(joined[:, 0], cosine, sine, 1.0).astype(BF), 1, 0)
    keys = jnp.moveaxis(rotate(joined[:, 1], cosine, sine, 1.0).astype(BF), 1, 0)
    values = jnp.moveaxis(joined[:, 2].astype(BF), 1, 0)
    feature_rows = n_dp * deep
    direct = spare == 0 and own % per_line == 0
    d_rows = dot("fe,te->ft", dense_rows, grad_group).astype(BF)
    if direct:
        runs = own // per_line
        moved = seq_exchange(d_rows.reshape(n_seq, runs * deep, group))
        moved = moved.reshape(n_seq, runs, deep, group)
        d_attended = jnp.moveaxis(moved, 0, 1).reshape(heads, HEAD_DIM, group)
    else:
        moved = lax.all_gather(d_rows.reshape(n_dp, deep, group), "seq", axis=1)
        moved = moved.reshape(width, group)
        moved = jnp.pad(moved, ((0, spare * HEAD_DIM), (0, 0)))
        d_attended = pick(moved.reshape(n_seq, heads, HEAD_DIM, group), me)
    d_attended = jnp.swapaxes(d_attended, 1, 2)
    attended, d_queries, d_keys, d_values = attention(queries, keys, values, d_attended, segment, scale)
    attended = jnp.swapaxes(attended.astype(BF), 1, 2).reshape(own, group)
    if direct:
        given = jnp.moveaxis(attended.reshape(runs, n_seq, deep, group), 1, 0)
        rows_attended = seq_exchange(given.reshape(n_seq, runs * deep, group)).reshape(feature_rows, group)
    else:
        given = lax.all_gather(attended, "seq", axis=0, tiled=True)[:width]
        rows_attended = lax.dynamic_index_in_dim(
            given.reshape(n_dp, n_seq, deep, group), me, 1, keepdims=False
        ).reshape(feature_rows, group)
    attn_out = dot("ft,fe->te", rows_attended, dense_rows)
    dense_grad = dot("ft,te->fe", rows_attended, grad_group).astype(BF).reshape(n_dp, deep, width)
    d_queries = rotate(jnp.moveaxis(d_queries, 0, 1), cosine, sine, -1.0)
    d_keys = rotate(jnp.moveaxis(d_keys, 0, 1), cosine, sine, -1.0)
    d_joined = jnp.stack([d_queries, d_keys, jnp.moveaxis(d_values, 0, 1)], axis=1)
    d_joined = d_joined.astype(BF).reshape(group, 3 * own)
    qkv_grad = dot("td,te->de", attn_in, d_joined).astype(BF).reshape(n_dp, n_seq * deep, 3 * own)
    d_attn_in = dot("te,de->td", d_joined, qkv_full)
    attn_terms = jnp.concatenate([qkv_grad, beside(dense_grad)], axis=2)
    attn_sum = dp_reduce(lambda i: pick(attn_terms, i))

    upper = dot("td,df->tf", mlp_in, up_full) + own_up_bias
    cdf = 0.5 * (1.0 + lax.erf(upper * F32(0.7071067811865476)))
    pdf = jnp.exp(-0.5 * upper * upper) * F32(0.3989422804014327)
    act = (upper * cdf).astype(BF)
    d_act = dot("td,fd->tf", grad_group, down_full)
    d_up = (d_act * (cdf + upper * pdf)).astype(BF)
    down_grad = dot("tf,td->fd", act, grad_group).astype(BF).reshape(n_dp, unit_rows, width)
    up_grad = dot("td,tf->df", mlp_in, d_up).astype(BF).reshape(n_dp, up_rows, width)
    mlp_out = dot("tf,fd->td", act, down_full)
    d_mlp_in = dot("tf,df->td", d_up, up_full)

    mine = jnp.arange(n_seq) == me
    qkv_bias_grad = jnp.sum(d_joined.astype(F32), axis=0)
    qkv_bias_grad = from_heads(jnp.where(mine[:, None], qkv_bias_grad[None], 0.0))
    up_bias_grad = jnp.sum(d_up.astype(F32), axis=0).reshape(n_dp, 1, unit_rows)
    up_bias_grad = jnp.where(mine[None, :, None], up_bias_grad, 0.0)
    bias_sum = jnp.sum(grad_out.astype(F32), axis=0)
    terms = (
        jnp.sum(d_attn_in * unit, axis=0),
        jnp.sum(d_attn_in, axis=0),
        jnp.sum(d_mlp_in * unit, axis=0),
        jnp.sum(d_mlp_in, axis=0),
        qkv_bias_grad,
        bias_sum,
        up_bias_grad,
        bias_sum,
    )
    terms = [t.reshape(n_dp, n_seq, size) for t, size in zip(terms, sizes)]
    terms = jnp.concatenate(terms, axis=2).reshape(n_dp, n_seq * length)
    tail_rows = -(-n_seq * length // width)
    tail_rows += -tail_rows % 8
    terms = jnp.pad(terms, ((0, 0), (0, tail_rows * width - n_seq * length)))
    terms = terms.reshape(n_dp, tail_rows, width).astype(BF)
    mlp_sum = dp_reduce(lambda i: jnp.concatenate([pick(up_grad, i), pick(down_grad, i), pick(terms, i)], axis=0))

    upstream = d_attn_in * f_attn_gain + d_mlp_in * f_mlp_gain
    pair = jnp.concatenate([(attn_out + mlp_out).astype(BF), upstream.astype(BF)], axis=1)
    pair = seq_reduce(pair.reshape(n_seq, rows, 2 * width))
    block_out = hidden_in.astype(F32) + f_dense_bias + f_down_bias + pair[:, :width]
    upstream = pair[:, width:]
    x = hidden_in.astype(F32)
    centered = x - jnp.mean(x, axis=-1, keepdims=True)
    inverse = lax.rsqrt(jnp.mean(centered * centered, axis=-1, keepdims=True) + EPS)
    own_unit = centered * inverse
    inner = (
        upstream
        - jnp.mean(upstream, axis=-1, keepdims=True)
        - own_unit * jnp.mean(upstream * own_unit, axis=-1, keepdims=True)
    )
    grad_in = grad_out.astype(F32) + inverse * inner

    qkv_back = attn_sum[:, : 3 * own].reshape(n_seq, deep, 3 * own).astype(BF)
    qkv_own = from_heads(seq_exchange(qkv_back).astype(F32))
    dense_own = from_beside(attn_sum[:, 3 * own :])
    vec_sum = mlp_sum[up_rows + unit_rows :].reshape(-1)[: n_seq * length].reshape(n_seq, 1, length)
    vec_sum = jnp.pad(vec_sum, ((0, 0), (0, 0), (0, -length % own_units)))
    vec_sum = vec_sum.reshape(n_seq, -1, own_units)
    back = jnp.concatenate([mlp_sum[:up_rows].reshape(n_seq, deep, own_units), vec_sum], axis=1)
    back = seq_exchange(back.astype(BF)).astype(F32)
    up_own = jnp.moveaxis(back[:, :deep].reshape(n_seq, deep, n_dp, unit_rows), 0, 2)
    vec_own = jnp.sum(back[:, deep:].reshape(n_seq, -1), axis=0)
    owned = []
    start = 0
    for size in sizes:
        owned.append(vec_own[start : start + size])
        start += size
    return (
        block_out.astype(BF),
        grad_in.astype(BF),
        owned[0],
        owned[1],
        owned[2],
        owned[3],
        qkv_own,
        owned[4],
        dense_own,
        owned[5],
        up_own.reshape(deep, hidden_units),
        owned[6],
        mlp_sum[up_rows : up_rows + unit_rows],
        owned[7],
    )


SCALE = HEAD_DIM**-0.5


def kernel_call(body, outs, args, scratch=(), megabytes=24, flops=0, apart=0):
    moved = sum(a.size * a.dtype.itemsize for a in args)
    held = [pl.BlockSpec(memory_space=pl.ANY)] * apart
    held += [pl.BlockSpec(memory_space=pltpu.VMEM)] * (len(args) - apart)
    return pl.pallas_call(
        body,
        out_shape=tuple(jax.ShapeDtypeStruct(shape, kind) for shape, kind in outs),
        in_specs=held,
        scratch_shapes=[pltpu.VMEM(*item) if isinstance(item, tuple) else item for item in scratch],
        compiler_params=pltpu.CompilerParams(vmem_limit_bytes=megabytes << 20),
        cost_estimate=pl.CostEstimate(flops=flops, bytes_accessed=moved, transcendentals=0),
    )(*args)


def dot_nn(a, b):
    return lax.dot_general(a, b, (((1,), (0,)), ((), ())), preferred_element_type=F32)


def dot_nt(a, b):
    return lax.dot_general(a, b, (((1,), (1,)), ((), ())), preferred_element_type=F32)


def dot_tn(a, b):
    return lax.dot_general(a, b, (((0,), (0,)), ((), ())), preferred_element_type=F32)


def line_and_side():
    me = lax.axis_index("dp")
    return lax.shift_right_logical(me, 1), lax.bitwise_and(me, 1)


def dp_index(line, step, side):
    return 2 * lax.bitwise_and(line + step, 3) + side


def dp_pieces(block):
    near1 = lax.ppermute(block, "dp", along(1))
    far0 = lax.ppermute(block, "dp", SIDE_SWAP)
    near3 = lax.ppermute(block, "dp", along(3))
    near2 = lax.ppermute(block, "dp", along(2))
    far1 = lax.ppermute(near1, "dp", SIDE_SWAP)
    far3 = lax.ppermute(near3, "dp", SIDE_SWAP)
    far2 = lax.ppermute(once(near2, far3), "dp", SIDE_SWAP)
    return (block, far0, near1, far1, near3, far3, near2, far2)


def piece_owners():
    line, side = line_and_side()
    return [dp_index(line, step, s) for step in (0, 3, 1, 2) for s in (side, 1 - side)]


def dp_sum(send2, send13, send0, keep2, keep13, keep0):
    moved2 = lax.ppermute(send2, "dp", SIDE_SWAP)
    moved13 = lax.ppermute(send13, "dp", SIDE_SWAP)
    moved0 = lax.ppermute(send0, "dp", SIDE_SWAP)
    sum2 = (keep2.astype(F32) + moved2.astype(F32)).astype(BF)
    sum1 = (keep13[0].astype(F32) + moved13[0].astype(F32)).astype(BF)
    sum3 = (keep13[1].astype(F32) + moved13[1].astype(F32)).astype(BF)
    got2 = lax.ppermute(sum2, "dp", along(2))
    got1 = lax.ppermute(sum1, "dp", along(1))
    got3 = lax.ppermute(sum3, "dp", along(3))
    total = keep0.astype(F32) + moved0.astype(F32)
    return (moved2, moved13), total + got2.astype(F32) + got1.astype(F32) + got3.astype(F32)


def pick_blocks(block_of, send2, send13, send0, keep2, keep13, keep0):
    line, side = line_and_side()
    for far, (r2, r13, r0) in ((True, (send2, send13, send0)), (False, (keep2, keep13, keep0))):
        s = 1 - side if far else side
        r2[...] = block_of(dp_index(line, 2, s))
        r13[0] = block_of(dp_index(line, 1, s))
        r13[1] = block_of(dp_index(line, 3, s))
        r0[...] = block_of(dp_index(line, 0, s))


def pick_shapes(rows, width):
    one, two = ((rows, width), BF), ((2, rows, width), BF)
    return (one, two, one, one, two, one)


def once(values, *others):
    return lax.optimization_barrier((values, *others))[0]


def seq_shuffle(blocks):
    got = [blocks[0]]
    for other in (1, 2, 3):
        pairs = [(i, i ^ other) for i in range(4)]
        got.append(lax.ppermute(blocks[other], "seq", pairs))
    return got


def place_kernel(deep, *refs):
    pieces, (dy, weights, dense, vectors), d_blocks, (rows32, d_rows) = refs[:8], refs[8:12], refs[12:16], refs[16:]
    per_line = 4 * deep
    quarter = dy.shape[1] // 4
    own = weights.shape[1] - quarter
    total = jnp.zeros(vectors.shape, F32)
    for piece, owner in zip(pieces, piece_owners()):
        weights[pl.ds(pl.multiple_of(owner * per_line, per_line), per_line), :] = piece[:per_line, :]
        total = total + piece[per_line:, :].astype(F32)
        beside = piece[:per_line, own:].astype(F32)
        for q in range(4):
            rows32[pl.ds(pl.multiple_of(owner * deep, 8), deep), q * quarter : (q + 1) * quarter] = beside[
                q * deep : (q + 1) * deep
            ]
    vectors[...] = total
    dense[...] = rows32[...].astype(BF)
    d_rows[...] = dot_nt(dense[...], dy[...]).astype(BF)
    me = lax.axis_index("seq")
    count = d_blocks[0].shape[0]
    for j in range(4):
        d_blocks[j][...] = d_rows[pl.ds(pl.multiple_of(lax.bitwise_xor(me, j) * count, 16), count), :]


def turn(values, cosine, sine_a, sine_b, sign):
    half = ROT // 2
    ahead = pltpu.roll(values, 128 - half, 1)
    behind = pltpu.roll(values, half, 1)
    return values * cosine + sign * (ahead * sine_a + behind * sine_b)


def project_kernel(unit, weights, vectors, cosine, sine_a, sine_b, attn_in, qk, v):
    gain, shift, bias = vectors[0:1, :], vectors[1:2, :], vectors[6:7, :]
    turned = qk.shape[1]
    size = 128

    def step(i, carry):
        rows = pl.ds(pl.multiple_of(i * size, size), size)
        normed = (unit[rows, :] * gain + shift).astype(BF)
        attn_in[rows, :] = normed
        joined = dot_nn(normed, weights[...]) + bias
        tables = cosine[rows, :], sine_a[rows, :], sine_b[rows, :]
        for c in range(0, turned, 128):
            qk[rows, c : c + 128] = turn(joined[:, c : c + 128], *tables, 1.0).astype(BF)
        v[rows, :] = joined[:, turned : turned + v.shape[1]].astype(BF)
        return carry

    lax.fori_loop(0, unit.shape[0] // size, step, 0)


def attention_kernel(deep, *refs):
    qk, v, d0, d1, d2, d3, seg_column, seg_row, cosine, sine_a, sine_b = refs[:11]
    given, d_joined, (d_t, out_t, dk_t, dv_t, acc) = refs[11:15], refs[15], refs[16:]
    tokens, own = v.shape
    me = lax.axis_index("seq")
    runs = own // (4 * deep)
    for j, ref in enumerate((d0, d1, d2, d3)):
        source = lax.bitwise_xor(me, j)
        block = ref[...].astype(F32)
        for r in range(runs):
            place = pl.multiple_of(r * 4 * deep + source * deep, 8)
            d_t[pl.ds(place, deep), :] = block[r * deep : (r + 1) * deep]
    d_out = jnp.transpose(d_t[...]).astype(BF)
    q_t = jnp.transpose(qk[:, :own].astype(F32)).astype(BF)
    d_tb = d_t[...].astype(BF)
    dk_t[...] = jnp.zeros(dk_t.shape, F32)
    dv_t[...] = jnp.zeros(dv_t.shape, F32)
    size = 256
    for h in range(own // HEAD_DIM):
        lanes = slice(h * HEAD_DIM, (h + 1) * HEAD_DIM)
        q_h = qk[:, lanes]
        k_h = qk[:, own + h * HEAD_DIM : own + (h + 1) * HEAD_DIM]
        v_h = v[:, lanes]
        d_h = d_out[:, lanes]
        for first in range(0, tokens, size):
            rows = slice(first, first + size)
            n = first + size
            scores = dot_nt(q_h[rows], k_h[:n]) * SCALE
            query = lax.broadcasted_iota(jnp.int32, (size, n), 0) + first
            key = lax.broadcasted_iota(jnp.int32, (size, n), 1)
            allowed = (seg_column[rows, :] == seg_row[:, :n]) & (key <= query)
            scores = jnp.where(allowed, scores, NEGATIVE)
            weights = jnp.where(allowed, jnp.exp(scores - jnp.max(scores, axis=1, keepdims=True)), 0.0)
            probs = weights * (1.0 / jnp.sum(weights, axis=1, keepdims=True))
            probs_r = probs.astype(BF)
            out_t[lanes, rows] = jnp.transpose(dot_nn(probs_r, v_h[:n]))
            d_probs = dot_nt(d_h[rows], v_h[:n])
            delta = jnp.sum(probs * d_probs, axis=1, keepdims=True)
            d_scores = (probs * (d_probs - delta)).astype(BF)
            acc[rows, lanes] = dot_nn(d_scores, k_h[:n]) * SCALE
            dk_t[lanes, :n] += dot_nn(q_t[lanes, rows], d_scores)
            dv_t[lanes, :n] += dot_nn(d_tb[lanes, rows], probs_r)
    acc[:, own : 2 * own] = jnp.transpose(dk_t[...]) * SCALE
    for c in range(0, 2 * own, 128):
        turned = turn(acc[:, c : c + 128], cosine[...], sine_a[...], sine_b[...], -1.0)
        d_joined[:, c : c + 128] = turned.astype(BF)
    d_joined[:, 2 * own : 3 * own] = jnp.transpose(dv_t[...]).astype(BF)
    d_joined[:, 3 * own :] = jnp.zeros((tokens, d_joined.shape[1] - 3 * own), BF)
    for j in range(4):
        target = lax.bitwise_xor(me, j)
        parts = [out_t[pl.ds(pl.multiple_of(r * 4 * deep + target * deep, 8), deep), :] for r in range(runs)]
        given[j][...] = jnp.concatenate(parts, axis=0).astype(BF)


def attention_grads_kernel(deep, *refs):
    r0, r1, r2, r3, dense, dy, attn_in, d_joined, weights, unit, vectors = refs[:11]
    picks, (attn_out, scaled, sums), (rows_t, grads) = refs[11:17], refs[17:20], refs[20:]
    me = lax.axis_index("seq")
    count = r0.shape[0]
    width = dy.shape[1]
    quarter = width // 4
    own = width - quarter
    for j, ref in enumerate((r0, r1, r2, r3)):
        rows_t[pl.ds(pl.multiple_of(lax.bitwise_xor(me, j) * count, 16), count), :] = ref[...]
    size = 128
    for c in range(0, width, size):
        grads[c : c + size, :] = dot_tn(attn_in[:, c : c + size], d_joined[...])
    dense_grad = dot_nn(rows_t[...], dy[...])
    for p in range(8):
        for q in range(4):
            start = p * 4 * deep + q * deep
            grads[start : start + deep, own:] = dense_grad[p * deep : (p + 1) * deep, q * quarter : (q + 1) * quarter]
    per_line = 4 * deep

    def block_of(index):
        return grads[pl.ds(pl.multiple_of(index * per_line, per_line), per_line), :].astype(BF)

    pick_blocks(block_of, *picks)
    attended = jnp.transpose(rows_t[...].astype(F32)).astype(BF)
    gain = vectors[0:1, :]
    tokens = dy.shape[0]
    sums[...] = jnp.zeros(sums.shape, F32)
    for c in range(0, tokens, size):
        rows = slice(c, c + size)
        attn_out[rows, :] = dot_nn(attended[rows], dense[...])
        back = dot_nt(d_joined[rows, :], weights[...])
        scaled[rows, :] = back * gain
        sums[0:1, :] += jnp.sum(back * unit[rows, :], axis=0, keepdims=True)
        sums[1:2, :] += jnp.sum(back, axis=0, keepdims=True)
        sums[5:6, :] += jnp.sum(d_joined[rows, :].astype(F32), axis=0, keepdims=True)


def pack_kernel(deep, *refs):
    qkv, up, vectors_in, blocks, (all_blocks, row_block) = *refs[:2], refs[2:9], refs[9:13], refs[13:]
    width = qkv.shape[1] // 3
    own = width // 4
    units = up.shape[1] // 32
    half = up.shape[1] // 8
    me = lax.axis_index("seq")
    device = 4 * lax.axis_index("dp") + me
    row_block[...] = jnp.zeros(row_block.shape, F32)
    for r in range(6):
        row_block[r : r + 1, :deep] = vectors_in[r][...].astype(F32)
    vectors = pltpu.roll(row_block[:, :width], device * deep, 1)
    row_block[0:6, :] = jnp.zeros((6, row_block.shape[1]), F32)
    row_block[6:7, : 3 * deep] = vectors_in[6][...].astype(F32)
    bias_rows = pltpu.roll(row_block[...], device * (3 * deep), 1)
    up_values, qkv_values = up[...].astype(F32), qkv[...].astype(F32)
    for t in range(4):
        parts = [up_values[:, ((l * 2 + y) * 4 + t) * units :][:, :units] for y in range(2) for l in range(4)]
        all_blocks[t, :deep, : 2 * half] = jnp.concatenate(parts, axis=1)
        all_blocks[t, deep:, : 2 * half] = vectors
        for part in range(3):
            lanes = slice(part * width + t * own, part * width + (t + 1) * own)
            place = slice(2 * half + part * own, 2 * half + (part + 1) * own)
            all_blocks[t, :deep, place] = qkv_values[:, lanes]
            all_blocks[t, deep:, place] = bias_rows[:, lanes]
    for j in range(4):
        blocks[j][...] = all_blocks[lax.bitwise_xor(me, j)].astype(BF)


def unpack_kernel(deep, r0, r1, r2, r3, dense, up_bias, attn_piece, up_keep, up_give, rows32, row_block):
    me = lax.axis_index("seq")
    line, side = line_and_side()
    width = dense.shape[1]
    quarter = width // 4
    half = up_keep.shape[1]
    own = 3 * quarter
    extra = jnp.zeros((8, rows32.shape[1]), F32)
    for j, ref in enumerate((r0, r1, r2, r3)):
        block = ref[...].astype(F32)
        source = lax.bitwise_xor(me, j)
        rows32[pl.ds(pl.multiple_of(source * deep, 8), deep), :] = block[:deep]
        extra = extra + block[deep:]
    rows = 4 * deep
    first, second = rows32[:, :half], rows32[:, half : 2 * half]
    up_keep[...] = jnp.where(side == 0, first, second).astype(BF)
    up_give[...] = jnp.where(side == 0, second, first).astype(BF)
    attn_piece[:rows, :own] = rows32[:, 2 * half :].astype(BF)
    dense_values = dense[...].astype(F32)
    beside = [dense_values[:, q * quarter : (q + 1) * quarter] for q in range(4)]
    attn_piece[:rows, own:] = jnp.concatenate(beside, axis=0).astype(BF)
    units = half // 4
    row_block[...] = jnp.zeros(row_block.shape, F32)
    row_block[7:8, :units] = up_bias[...].astype(F32)
    up_row = pltpu.roll(row_block[...], side * half + line * units, 1)
    qkv_row = jnp.concatenate([extra[:, 2 * half :], jnp.zeros((8, quarter), F32)], axis=1)
    attn_piece[rows:, :] = (extra[:, : 2 * half] + up_row + qkv_row).astype(BF)


def mlp_kernel(*refs):
    pieces, (unit_own, unit_other, dy_own, dy_other, vectors, attn_out, scaled, sums_in) = refs[:4], refs[4:12]
    give, keep, mlp_in, act, d_up, sums, up, down, done = refs[12:]
    line, side = line_and_side()
    width, half = up.shape
    units = half // 4
    copies = []
    for step, piece in zip((0, 3, 1, 2), pieces):
        l = lax.bitwise_and(line + step, 3)
        top, low = pl.ds(0, units), pl.ds(units, units)
        for source, target in (
            (piece.at[top, :], down.at[pl.ds(pl.multiple_of(l * units, 32), units), :]),
            (piece.at[low, pl.ds(0, half)], up.at[pl.ds(pl.multiple_of(2 * l * units, 32), units), :]),
            (piece.at[low, pl.ds(half, half)], up.at[pl.ds(pl.multiple_of((2 * l + 1) * units, 32), units), :]),
        ):
            copies.append(pltpu.make_async_copy(source, target, done.at[len(copies)]))
    for copy in copies:
        copy.start()
    gain, shift = vectors[2:3, :], vectors[3:4, :]
    bias = jnp.where(side == 0, vectors[7:8, :half], vectors[7:8, half:])
    sums[...] = sums_in[...]
    group = unit_own.shape[0]
    size = group // 4
    core = lax.bitwise_and(lax.axis_index("seq"), 1)
    for copy in copies:
        copy.wait()

    def tokens(unit, dy, offset, own):
        def step(i, carry):
            rows = pl.ds(pl.multiple_of(i * size, size), size)
            all_rows = pl.ds(pl.multiple_of(offset + i * size, size), size)
            u = unit[rows, :]
            normed = (u * gain + shift).astype(BF)
            mlp_in[all_rows, :] = normed
            upper = dot_nn(normed, up[...]) + bias
            cdf = 0.5 * (1.0 + lax.erf(upper * 0.7071067811865476))
            pdf = jnp.exp(-0.5 * upper * upper) * 0.3989422804014327
            act_rows = (upper * cdf).astype(BF)
            act[all_rows, :] = act_rows
            g = dy[rows, :]
            d_rows = (dot_nt(g, down[...]) * (cdf + upper * pdf)).astype(BF)
            d_up[all_rows, :] = d_rows
            out = dot_nn(act_rows, down[...])
            back = dot_nt(d_rows, up[...])
            sums[2:3, :] += jnp.sum(back * u, axis=0, keepdims=True)
            sums[3:4, :] += jnp.sum(back, axis=0, keepdims=True)
            sums[6:7, :half] += jnp.sum(d_rows.astype(F32), axis=0, keepdims=True)
            back = back * gain
            if own:
                out = out + attn_out[rows, :]
                back = back + scaled[rows, :]
                sums[4:5, :] += 0.25 * jnp.sum(g.astype(F32), axis=0, keepdims=True)
            place = (0 if own else 2) + lax.shift_right_logical(i, 1)
            out, back = out.astype(BF), back.astype(BF)

            @pl.when(lax.bitwise_and(i, 1) == core)
            def _():
                keep[place, :, :width] = out
                keep[place, :, width:] = back

            @pl.when(lax.bitwise_and(i, 1) != core)
            def _():
                give[place, :, :width] = out
                give[place, :, width:] = back

            return carry

        lax.fori_loop(0, 4, step, 0)

    tokens(unit_own, dy_own, 0, True)
    tokens(unit_other, dy_other, group, False)


def mlp_grads_kernel(mlp_in, act, d_up, dy_own, dy_other, sums, send1, send2, send3, own_terms, up_grad, down_grad):
    line, _ = line_and_side()
    sends = (send1, send2, send3)
    group, width = dy_own.shape
    half = act.shape[1]
    units = half // 4
    for c in range(0, width, 128):
        up_grad[c : c + 128, :] = dot_tn(mlp_in[:, c : c + 128], d_up[...]).astype(BF)
    for c in range(0, half, 128):
        total = dot_tn(act[:group, c : c + 128], dy_own[...]) + dot_tn(act[group:, c : c + 128], dy_other[...])
        down_grad[c : c + 128, :] = total.astype(BF)
    tail = sums[...].astype(BF)
    for step, ref in zip((1, 2, 3, 0), (*sends, own_terms)):
        l = lax.bitwise_and(line + step, 3)
        ref[:units, :] = down_grad[pl.ds(pl.multiple_of(l * units, 32), units), :]
        ref[units : 2 * units, :half] = up_grad[pl.ds(pl.multiple_of(2 * l * units, 32), units), :]
        ref[units : 2 * units, half:] = up_grad[pl.ds(pl.multiple_of((2 * l + 1) * units, 32), units), :]
        ref[2 * units :, :] = tail


def mlp_sum_kernel(own, g1, g2, g3, down_own, up_keep, up_give, tail):
    units, width = down_own.shape
    half = width // 2
    _, side = line_and_side()
    refs = (own, g1, g2, g3)

    def total(rows, lanes):
        return sum(ref[rows, lanes].astype(F32) for ref in refs)

    down_own[...] = total(slice(0, units), slice(None))
    first = total(slice(units, 2 * units), slice(0, half))
    second = total(slice(units, 2 * units), slice(half, width))
    last = total(slice(2 * units, 2 * units + 8), slice(None))
    tail[...] = last
    up_keep[...] = jnp.where(side == 0, first, second).astype(BF)
    up_give[:units, :] = jnp.where(side == 0, second, first).astype(BF)
    up_give[units:, :] = jnp.concatenate([last[:, :half], last[:, half:]], axis=0).astype(BF)


def owners_kernel(deep, keep, far, tail, b0, b1, b2, b3, rows32):
    _, side = line_and_side()
    me = lax.axis_index("seq")
    rows, half = keep.shape
    here, there = keep[...].astype(F32), far[:rows, :].astype(F32)
    rows32[:, :half] = jnp.where(side == 0, here, there)
    rows32[:, half:] = jnp.where(side == 0, there, here)
    far_tail = far[rows:, :].astype(F32)
    last = tail[...] + jnp.concatenate([far_tail[:8], far_tail[8:]], axis=1)
    for j, ref in enumerate((b0, b1, b2, b3)):
        target = lax.bitwise_xor(me, j)
        block = rows32[pl.ds(pl.multiple_of(target * deep, 8), deep), :]
        ref[...] = jnp.concatenate([block, last], axis=0).astype(BF)


def owned_kernel(deep, b0, b1, b2, b3, tail, up_own, vec_own, sources, row_block):
    line, _ = line_and_side()
    me = lax.axis_index("seq")
    device = 4 * lax.axis_index("dp") + me
    width = tail.shape[1]
    half, own = width // 2, width // 4
    units = half // 4
    for j, ref in enumerate((b0, b1, b2, b3)):
        sources[lax.bitwise_xor(me, j)] = ref[...].astype(F32)
    for l in range(4):
        parts = [
            sources[t, :deep, y * half + l * units : y * half + (l + 1) * units] for y in range(2) for t in range(4)
        ]
        up_own[:, l * 2 * half : (l + 1) * 2 * half] = jnp.concatenate(parts, axis=1)
    total = sources[0, deep:] + sources[1, deep:] + sources[2, deep:] + sources[3, deep:]
    rolled = pltpu.roll(total, width - device * deep, 1)
    vec_own[...] = rolled[:, :128]
    row_block[...] = jnp.zeros(row_block.shape, F32)
    for t in range(4):
        row = sources[t, deep + 5 : deep + 6, :]
        for part in range(3):
            place = part * width + t * own
            row_block[5:6, place : place + own] = row[:, part * own : (part + 1) * own]
    rolled = pltpu.roll(row_block[...], 3 * width - device * (3 * deep), 1)
    vec_own[5:6, :] = rolled[5:6, :128]
    rolled = pltpu.roll(tail[...], width - line * units, 1)
    vec_own[6:7, :] = rolled[6:7, :128]


def with_waits(count, body):
    def wrapped(*refs):
        body(*refs[count:])

    return wrapped


def line_device(
    hidden_in,
    lengths,
    grad_out,
    attn_gain,
    attn_shift,
    mlp_gain,
    mlp_shift,
    qkv_weight,
    qkv_bias,
    dense_weight,
    dense_bias,
    up_weight,
    up_bias,
    down_weight,
    down_bias,
):
    n_dp, n_seq = 8, 4
    dp_me, me = lax.axis_index("dp"), lax.axis_index("seq")
    line, side = lax.shift_right_logical(dp_me, 1), lax.bitwise_and(dp_me, 1)
    chip, core = lax.shift_right_logical(me, 1), lax.bitwise_and(me, 1)
    device = dp_me * n_seq + me
    zero = jnp.int32(0)
    rows, width = hidden_in.shape
    group = rows * n_seq
    hidden_units = up_weight.shape[1]
    units = hidden_units // (n_dp * n_seq)
    half = hidden_units // 8
    deep = width // (n_dp * n_seq)
    per_line = n_seq * deep
    own = width // n_seq
    wide = 2 * half + 3 * own
    flat = (group, width)

    vectors_in = (attn_gain, attn_shift, mlp_gain, mlp_shift, dense_bias, down_bias, qkv_bias)
    blocks = kernel_call(
        functools.partial(pack_kernel, deep),
        (((deep + 8, wide), BF),) * 4,
        (qkv_weight, up_weight, *[v[None] for v in vectors_in]),
        scratch=(((4, deep + 8, wide), F32), ((8, 3 * width), F32)),
        megabytes=16,
    )
    got = seq_shuffle(blocks)
    attn_piece, up_keep, up_give = kernel_call(
        functools.partial(unpack_kernel, deep),
        (((per_line + 8, width), BF), ((per_line, half), BF), ((per_line, half), BF)),
        (*got, dense_weight, up_bias[None]),
        scratch=(((per_line, wide), F32), ((8, width), F32)),
        megabytes=16,
    )
    attn_pieces = dp_pieces(attn_piece)
    up_far = lax.ppermute(up_give, "dp", SIDE_SWAP)
    up_both = jnp.concatenate(
        [jnp.where(side == 0, up_keep, up_far), jnp.where(side == 0, up_far, up_keep)], axis=1
    )
    mlp_piece = jnp.concatenate([down_weight, up_both], axis=0)
    from2, from1, from3 = [lax.ppermute(mlp_piece, "dp", along(k)) for k in (2, 1, 3)]
    mlp_pieces = (mlp_piece, from1, from3, from2)

    mine = jnp.concatenate([hidden_in, grad_out], axis=0)
    across = lax.ppermute(mine, "dp", SIDE_SWAP)

    def whole_group(values):
        far = lax.ppermute(values, "seq", CHIP_SWAP)
        by_chip = in_order(chip == 1, values, far)
        over = lax.ppermute(by_chip, "seq", CORE_SWAP)
        full = in_order(core == 1, by_chip, over, axis=1).reshape(n_seq, 2, rows, width)
        return full[:, 0].reshape(flat), full[:, 1].reshape(flat)

    hidden_group, dy = whole_group(once(mine, attn_pieces[2]))
    hidden_other, dy_other = whole_group(once(across, attn_pieces[6]))

    row_lengths = lengths[0]
    segment, position = place(row_lengths, jnp.arange(group, dtype=jnp.int32))
    lane = jnp.arange(128, dtype=jnp.int32) % HEAD_DIM
    powers = jnp.power(F32(10000.0), -(2.0 * (lane % (ROT // 2)).astype(F32)) / ROT)
    angles = position.astype(F32)[:, None] * powers[None, :]
    cosine = jnp.where(lane < ROT, jnp.cos(angles), 1.0)
    sine = jnp.sin(angles)
    sine_a = jnp.where(lane < ROT // 2, -sine, 0.0)
    sine_b = jnp.where((lane >= ROT // 2) & (lane < ROT), sine, 0.0)

    def normed(values):
        centered = values - jnp.mean(values, axis=-1, keepdims=True)
        inverse = lax.rsqrt(jnp.mean(centered * centered, axis=-1, keepdims=True) + EPS)
        return centered * inverse, inverse

    unit = normed(hidden_group.astype(F32))[0]
    unit_other = normed(hidden_other.astype(F32))[0]

    placed = kernel_call(
        functools.partial(place_kernel, deep),
        ((flat[1:] * 2, BF), ((n_dp * deep, width), BF), ((8, width), F32)) + (((2 * deep, group), BF),) * 4,
        attn_pieces + (dy,),
        scratch=(((n_dp * deep, width), F32), ((n_dp * deep, group), BF)),
        flops=2 * n_dp * deep * width * group,
    )
    weights, dense, vectors = placed[:3]
    d_blocks = seq_shuffle(placed[3:])
    attn_in, qk, v = kernel_call(
        project_kernel,
        ((flat, BF), ((group, 2 * own), BF), ((group, own), BF)),
        (unit, weights, vectors, cosine, sine_a, sine_b),
        flops=2 * group * width * width,
    )
    attended = kernel_call(
        with_waits(1, functools.partial(attention_kernel, deep)),
        (((2 * deep, group), BF),) * 4 + ((flat, BF),),
        (from2, qk, v, *d_blocks, segment[:, None], segment[None, :], cosine, sine_a, sine_b),
        scratch=(((own, group), F32),) * 4 + ((flat, F32),),
        flops=14 * group * group * own,
        apart=1,
    )
    d_joined = attended[4]
    row_blocks = seq_shuffle(attended[:4])
    results = kernel_call(
        with_waits(2, functools.partial(attention_grads_kernel, deep)),
        pick_shapes(per_line, width) + ((flat, F32), (flat, F32), ((8, width), F32)),
        (from1, from3, *row_blocks, dense, dy, attn_in, d_joined, weights, unit, vectors),
        scratch=(((n_dp * deep, group), BF), ((width, width), F32)),
        flops=5 * group * width * width,
        megabytes=32,
        apart=2,
    )
    moved, attn_sum = dp_sum(*results[:6])

    units_shape = ((2 * group, half), BF)
    give, keep, *held = kernel_call(
        mlp_kernel,
        (((4, rows, 2 * width), BF),) * 2 + (((2 * group, width), BF), units_shape, units_shape, ((8, width), F32)),
        (*mlp_pieces, unit, unit_other, dy, dy_other, vectors) + tuple(results[6:]),
        scratch=(((width, half), BF), ((half, width), BF), pltpu.SemaphoreType.DMA((12,))),
        flops=8 * group * width * 2 * half,
        megabytes=32,
        apart=4,
    )
    results = kernel_call(
        with_waits(len(moved), mlp_grads_kernel),
        (((2 * units + 8, width), BF),) * 4,
        (*moved, *held[:3], dy, dy_other, held[3]),
        scratch=(((width, half), BF), ((half, width), BF)),
        flops=4 * group * width * 2 * half,
        megabytes=24,
        apart=len(moved),
    )
    terms = [results[3]] + [lax.ppermute(send, "dp", along(k)) for k, send in zip((1, 2, 3), results[:3])]

    both = keep.astype(F32) + lax.ppermute(give, "seq", CORE_SWAP).astype(F32)
    beyond = lax.ppermute(both[2:].astype(BF), "dp", SIDE_SWAP)
    *terms, beyond = lax.optimization_barrier((*terms, beyond))
    both = both[:2] + beyond.astype(F32)
    far = lax.ppermute(pick(both, 1 - chip).astype(BF), "seq", CHIP_SWAP)
    pair = pick(both, chip) + far.astype(F32)
    x = hidden_in.astype(F32)
    block_out = x + vectors[4] + vectors[5] + pair[:, :width]
    upstream = pair[:, width:]
    own_unit, inverse = normed(x)
    inner = (
        upstream
        - jnp.mean(upstream, axis=-1, keepdims=True)
        - own_unit * jnp.mean(upstream * own_unit, axis=-1, keepdims=True)
    )
    grad_in = grad_out.astype(F32) + inverse * inner

    def from_heads(blocks):
        split = jnp.moveaxis(blocks.reshape(n_seq, -1, 3, own), 0, 2)
        return split.reshape(-1, 3 * width)

    qkv_back = attn_sum[:, : 3 * own].reshape(n_seq, deep, 3 * own).astype(BF)
    qkv_own = from_heads(seq_exchange(qkv_back).astype(F32))
    dense_own = attn_sum[:, 3 * own :].reshape(n_seq, deep, own)
    dense_own = jnp.swapaxes(dense_own, 0, 1).reshape(deep, width)
    down_own, up_keep, up_give, tail = kernel_call(
        mlp_sum_kernel,
        (((units, width), F32), ((per_line, half), BF), ((per_line + 16, half), BF), ((8, width), F32)),
        tuple(terms),
        megabytes=8,
    )
    up_far = lax.ppermute(up_give, "dp", SIDE_SWAP)
    blocks = kernel_call(
        functools.partial(owners_kernel, deep),
        (((deep + 8, width), BF),) * 4,
        (up_keep, up_far, tail),
        scratch=(((per_line, width), F32),),
        megabytes=8,
    )
    up_own, vec_own = kernel_call(
        functools.partial(owned_kernel, deep),
        (((deep, hidden_units), F32), ((8, 128), F32)),
        (*seq_shuffle(blocks), tail),
        scratch=(((4, deep + 8, width), F32), ((8, 3 * width), F32)),
        megabytes=8,
    )
    by_width = vec_own[:5, :deep]
    qkv_bias_grad = vec_own[5, : 3 * deep]
    up_bias_grad = vec_own[6, :units]
    return (
        block_out.astype(BF),
        grad_in.astype(BF),
        by_width[0],
        by_width[1],
        by_width[2],
        by_width[3],
        qkv_own,
        qkv_bias_grad,
        dense_own,
        by_width[4],
        up_own,
        up_bias_grad,
        down_own,
        by_width[4],
    )


def per_device(*args):
    if lax.axis_size("dp") == 8 and lax.axis_size("seq") == 4:
        return line_device(*args)
    return general_device(*args)


def solution(mesh):
    both = ("dp", "seq")
    matrix, vector = P(both, None), P(both)
    params = (vector, vector, vector, vector, matrix, vector, matrix, vector, matrix, vector, matrix, vector)
    return jax.shard_map(
        per_device,
        mesh=mesh,
        in_specs=(matrix, P("dp", None), matrix) + params,
        out_specs=(matrix, matrix) + params,
        check_vma=False,
    )
```

```python
import functools

import jax
import jax.numpy as jnp
from jax import lax
from jax.experimental import pallas as pl
from jax.experimental.pallas import tpu as pltpu
from jax.sharding import PartitionSpec as P

HEADS = 12
HEAD_DIM = 64
ROT = 16
EPS = 1e-05
NEGATIVE = -1e30
BF = jnp.bfloat16
F32 = jnp.float32


def dot(spec, a, b):
    return jnp.einsum(spec, a, b, preferred_element_type=F32)


def frequencies():
    steps = jnp.arange(ROT // 2, dtype=F32)
    return jnp.power(F32(10000.0), -(2.0 * steps) / ROT)


def rotate(values, cosine, sine, sign):
    half = ROT // 2
    first = values[..., :half]
    second = values[..., half:ROT]
    turned_one = first * cosine - sign * second * sine
    turned_two = second * cosine + sign * first * sine
    return jnp.concatenate([turned_one, turned_two, values[..., ROT:]], axis=-1)


def place(row_lengths, index):
    ends = jnp.cumsum(row_lengths)
    after = (index[:, None] >= ends[None, :]).astype(jnp.int32)
    segment = jnp.sum(after, axis=1)
    start = jnp.sum(after * row_lengths[None, :], axis=1)
    return (segment, index - start)


def pick(values, index):
    return lax.dynamic_index_in_dim(values, index, 0, keepdims=False)


CHIP_SWAP = [(0, 2), (2, 0), (1, 3), (3, 1)]
CORE_SWAP = [(0, 1), (1, 0), (2, 3), (3, 2)]


def in_order(second, mine, other, axis=0):
    return jnp.stack([jnp.where(second, other, mine), jnp.where(second, mine, other)], axis=axis)


def seq_exchange(blocks):
    n = lax.axis_size("seq")
    if n != 4:
        return lax.all_to_all(blocks, "seq", 0, 0)
    me = lax.axis_index("seq")
    chip, core = me // 2, me % 2
    halves = blocks.reshape((2, 2) + blocks.shape[1:])
    far = lax.ppermute(pick(halves, 1 - chip), "seq", CHIP_SWAP)
    by_chip = in_order(chip == 1, pick(halves, chip), far, axis=1)
    other = lax.ppermute(pick(by_chip, 1 - core), "seq", CORE_SWAP)
    return in_order(core == 1, pick(by_chip, core), other, axis=1).reshape(blocks.shape)


def seq_gather(values):
    n = lax.axis_size("seq")
    if n != 4:
        return lax.all_gather(values, "seq", axis=0)
    me = lax.axis_index("seq")
    chip, core = me // 2, me % 2
    far = lax.ppermute(values, "seq", CHIP_SWAP)
    mine = in_order(chip == 1, values, far)
    other = lax.ppermute(mine, "seq", CORE_SWAP)
    return in_order(core == 1, mine, other, axis=1).reshape((n,) + values.shape)


def seq_reduce(values):
    n = lax.axis_size("seq")
    if n != 4:
        return lax.psum_scatter(values.astype(BF), "seq", scatter_dimension=0).astype(F32)
    me = lax.axis_index("seq")
    chip, core = me // 2, me % 2
    parts = values.reshape((2, 2) + values.shape[1:])
    keep = lax.dynamic_index_in_dim(parts, core, 1, keepdims=False)
    give = lax.dynamic_index_in_dim(parts, 1 - core, 1, keepdims=False).astype(BF)
    both = keep.astype(F32) + lax.ppermute(give, "seq", CORE_SWAP).astype(F32)
    far = lax.ppermute(pick(both, 1 - chip).astype(BF), "seq", CHIP_SWAP)
    return pick(both, chip) + far.astype(F32)


SIDE_SWAP = [(i, i ^ 1) for i in range(8)]


def along(step):
    return [(i, (i + 2 * step) % 8) for i in range(8)]


def dp_gather(block):
    n = lax.axis_size("dp")
    if n != 8:
        return lax.all_gather(block, "dp", axis=0)
    me = lax.axis_index("dp")
    line, side = me // 2, me % 2
    near1 = lax.ppermute(block, "dp", along(1))
    near3 = lax.ppermute(block, "dp", along(3))
    near2 = lax.ppermute(block, "dp", along(2))
    far0 = lax.ppermute(block, "dp", SIDE_SWAP)
    far13 = lax.ppermute(jnp.stack([near1, near3]), "dp", SIDE_SWAP)
    far2 = lax.ppermute(near2, "dp", SIDE_SWAP)
    full = jnp.zeros((4, 2) + block.shape, block.dtype)
    zero = jnp.int32(0)
    for step, near, far in ((0, block, far0), (1, near1, far13[0]), (3, near3, far13[1]), (2, near2, far2)):
        pair = in_order(side == 1, near, far)
        full = lax.dynamic_update_slice(full, pair[None], ((line - step) % 4, zero, zero, zero))
    return full.reshape((n,) + block.shape)


def dp_reduce(block_of):
    n = lax.axis_size("dp")
    if n != 8:
        blocks = jnp.stack([block_of(jnp.int32(i)).astype(BF) for i in range(n)])
        return lax.psum_scatter(blocks, "dp", scatter_dimension=0).astype(F32)
    me = lax.axis_index("dp")
    line, side = me // 2, me % 2

    def over_side(*steps):
        targets = [2 * ((line + step) % 4) for step in steps]
        moved = lax.ppermute(jnp.stack([block_of(t + 1 - side) for t in targets]), "dp", SIDE_SWAP)
        return [block_of(t + side).astype(F32) + moved[j].astype(F32) for j, t in enumerate(targets)]

    (sum2,) = over_side(2)
    sum1, sum3 = over_side(1, 3)
    (sum0,) = over_side(0)
    got2 = lax.ppermute(sum2.astype(BF), "dp", along(2)).astype(F32)
    got1 = lax.ppermute(sum1.astype(BF), "dp", along(1)).astype(F32)
    got3 = lax.ppermute(sum3.astype(BF), "dp", along(3)).astype(F32)
    return sum0 + got1 + got2 + got3


def attention(queries, keys, values, d_out, segment, scale):
    tokens = queries.shape[1]
    index = jnp.arange(tokens, dtype=jnp.int32)
    allowed = (segment[:, None] == segment[None, :]) & (index[None, :] <= index[:, None])
    scores = dot("htd,hnd->htn", queries, keys) * scale
    masked = jnp.where(allowed[None], scores, NEGATIVE)
    top = jnp.max(masked, axis=-1, keepdims=True)
    weights = jnp.where(allowed[None], jnp.exp(masked - top), 0.0)
    probs = weights / jnp.sum(weights, axis=-1, keepdims=True)
    probs_r = probs.astype(BF)
    attended = dot("htn,hnd->htd", probs_r, values)
    d_probs = dot("htd,hnd->htn", d_out, values)
    delta = jnp.sum(probs * d_probs, axis=-1, keepdims=True)
    d_scores = (probs * (d_probs - delta)).astype(BF)
    d_queries = dot("htn,hnd->htd", d_scores, keys) * scale
    d_keys = dot("htn,htd->hnd", d_scores, queries) * scale
    d_values = dot("htn,htd->hnd", probs_r, d_out)
    return attended, d_queries, d_keys, d_values


def general_device(
    hidden_in,
    lengths,
    grad_out,
    attn_gain,
    attn_shift,
    mlp_gain,
    mlp_shift,
    qkv_weight,
    qkv_bias,
    dense_weight,
    dense_bias,
    up_weight,
    up_bias,
    down_weight,
    down_bias,
):
    n_dp, n_seq = lax.axis_size("dp"), lax.axis_size("seq")
    me = lax.axis_index("seq")
    rows, width = hidden_in.shape
    group = rows * n_seq
    scale = HEAD_DIM ** (-0.5)
    hidden_units = up_weight.shape[1]
    own_units = hidden_units // n_seq
    deep = width // (n_dp * n_seq)
    unit_rows = hidden_units // (n_dp * n_seq)
    heads = -(-HEADS // n_seq)
    own = heads * HEAD_DIM
    spare = heads * n_seq - HEADS

    def by_head(values):
        lead = values.shape[:-1]
        split = values.reshape(lead + (3, HEADS, HEAD_DIM))
        if spare:
            split = jnp.pad(split, [(0, 0)] * (len(lead) + 1) + [(0, spare), (0, 0)])
        split = split.reshape(lead + (3, n_seq, own))
        return jnp.moveaxis(split, -2, 0).reshape((n_seq,) + lead + (3 * own,))

    def from_heads(blocks):
        lead = blocks.shape[1:-1]
        split = jnp.moveaxis(blocks.reshape((n_seq,) + lead + (3, own)), 0, -2)
        split = split.reshape(lead + (3, HEADS + spare, HEAD_DIM))[..., :HEADS, :]
        return split.reshape(lead + (3 * width,))

    vectors = (attn_gain, attn_shift, mlp_gain, mlp_shift, qkv_bias, dense_bias, up_bias, down_bias)
    sizes = [v.shape[0] for v in vectors]
    length = sum(sizes)
    wide = own_units + 3 * own
    up_blocks = jnp.moveaxis(up_weight.reshape(deep, n_dp, n_seq, unit_rows), 2, 0)
    up_blocks = up_blocks.reshape(n_seq, deep, own_units)
    vector = jnp.pad(jnp.concatenate(vectors), (0, wide - length))
    blocks = jnp.concatenate(
        [
            jnp.concatenate([up_blocks, by_head(qkv_weight)], axis=2),
            jnp.broadcast_to(vector, (n_seq, 1, wide)),
        ],
        axis=1,
    )
    got = seq_exchange(blocks)
    per_line = n_seq * deep
    up_rows = per_line * own_units // width
    up_piece = got[:, :deep, :own_units].reshape(up_rows, width)
    qkv_piece = got[:, :deep, own_units:].reshape(per_line, 3 * own)
    group_vector = got[:, deep, :length]

    both = seq_gather(jnp.concatenate([hidden_in, grad_out], axis=0))
    hidden_group = both[:, :rows].reshape(group, width)
    grad_group = both[:, rows:].reshape(group, width)

    def beside(values):
        lead = values.shape[:-2]
        split = values.reshape(lead + (deep, n_seq, width // n_seq))
        return jnp.swapaxes(split, -3, -2).reshape(lead + (per_line, width // n_seq))

    def from_beside(values):
        lead = values.shape[:-2]
        split = values.reshape(lead + (n_seq, deep, width // n_seq))
        return jnp.swapaxes(split, -3, -2).reshape(lead + (deep, width))

    attn_wide = 3 * own + width // n_seq
    vec_rows = -(-n_seq * length // attn_wide)
    vec_rows += -vec_rows % 8
    vec_piece = jnp.pad(group_vector.reshape(-1), (0, vec_rows * attn_wide - n_seq * length))
    attn_piece = jnp.concatenate([qkv_piece, beside(dense_weight)], axis=1)
    attn_piece = jnp.concatenate([attn_piece, vec_piece.reshape(vec_rows, attn_wide)], axis=0)
    attn_all = dp_gather(attn_piece)
    mlp_all = dp_gather(jnp.concatenate([up_piece, down_weight], axis=0))
    qkv_full = attn_all[:, :per_line, : 3 * own].reshape(width, 3 * own)
    dense_rows = from_beside(attn_all[:, :per_line, 3 * own :]).reshape(n_dp * deep, width)
    up_full = mlp_all[:, :up_rows].reshape(width, own_units)
    down_full = mlp_all[:, up_rows:].reshape(own_units, width)
    every = attn_all[:, per_line:].reshape(n_dp, vec_rows * attn_wide)[:, : n_seq * length]
    every = every.reshape(n_dp * n_seq, length).astype(F32)
    whole = []
    start = 0
    for size in sizes:
        whole.append(every[:, start : start + size].reshape(-1))
        start += size
    f_attn_gain, f_attn_shift, f_mlp_gain, f_mlp_shift, f_qkv_bias, f_dense_bias, f_up_bias, f_down_bias = whole
    own_qkv_bias = pick(by_head(f_qkv_bias), me)
    own_up_bias = lax.dynamic_index_in_dim(
        f_up_bias.reshape(n_dp, n_seq, unit_rows), me, 1, keepdims=False
    ).reshape(-1)

    row_lengths = lengths[0]
    index = jnp.arange(group, dtype=jnp.int32)
    segment, position = place(row_lengths, index)
    angles = position.astype(F32)[:, None] * frequencies()[None, :]
    cosine = jnp.cos(angles)[:, None, :]
    sine = jnp.sin(angles)[:, None, :]

    tokens = hidden_group.astype(F32)
    center = jnp.mean(tokens, axis=-1, keepdims=True)
    centered = tokens - center
    spread = jnp.mean(centered * centered, axis=-1, keepdims=True)
    unit = centered * lax.rsqrt(spread + EPS)
    attn_in = (unit * f_attn_gain + f_attn_shift).astype(BF)
    mlp_in = (unit * f_mlp_gain + f_mlp_shift).astype(BF)

    joined = dot("td,de->te", attn_in, qkv_full) + own_qkv_bias
    joined = joined.reshape(group, 3, heads, HEAD_DIM)
    queries = jnp.moveaxis(rotate(joined[:, 0], cosine, sine, 1.0).astype(BF), 1, 0)
    keys = jnp.moveaxis(rotate(joined[:, 1], cosine, sine, 1.0).astype(BF), 1, 0)
    values = jnp.moveaxis(joined[:, 2].astype(BF), 1, 0)
    feature_rows = n_dp * deep
    direct = spare == 0 and own % per_line == 0
    d_rows = dot("fe,te->ft", dense_rows, grad_group).astype(BF)
    if direct:
        runs = own // per_line
        moved = seq_exchange(d_rows.reshape(n_seq, runs * deep, group))
        moved = moved.reshape(n_seq, runs, deep, group)
        d_attended = jnp.moveaxis(moved, 0, 1).reshape(heads, HEAD_DIM, group)
    else:
        moved = lax.all_gather(d_rows.reshape(n_dp, deep, group), "seq", axis=1)
        moved = moved.reshape(width, group)
        moved = jnp.pad(moved, ((0, spare * HEAD_DIM), (0, 0)))
        d_attended = pick(moved.reshape(n_seq, heads, HEAD_DIM, group), me)
    d_attended = jnp.swapaxes(d_attended, 1, 2)
    attended, d_queries, d_keys, d_values = attention(queries, keys, values, d_attended, segment, scale)
    attended = jnp.swapaxes(attended.astype(BF), 1, 2).reshape(own, group)
    if direct:
        given = jnp.moveaxis(attended.reshape(runs, n_seq, deep, group), 1, 0)
        rows_attended = seq_exchange(given.reshape(n_seq, runs * deep, group)).reshape(feature_rows, group)
    else:
        given = lax.all_gather(attended, "seq", axis=0, tiled=True)[:width]
        rows_attended = lax.dynamic_index_in_dim(
            given.reshape(n_dp, n_seq, deep, group), me, 1, keepdims=False
        ).reshape(feature_rows, group)
    attn_out = dot("ft,fe->te", rows_attended, dense_rows)
    dense_grad = dot("ft,te->fe", rows_attended, grad_group).astype(BF).reshape(n_dp, deep, width)
    d_queries = rotate(jnp.moveaxis(d_queries, 0, 1), cosine, sine, -1.0)
    d_keys = rotate(jnp.moveaxis(d_keys, 0, 1), cosine, sine, -1.0)
    d_joined = jnp.stack([d_queries, d_keys, jnp.moveaxis(d_values, 0, 1)], axis=1)
    d_joined = d_joined.astype(BF).reshape(group, 3 * own)
    qkv_grad = dot("td,te->de", attn_in, d_joined).astype(BF).reshape(n_dp, n_seq * deep, 3 * own)
    d_attn_in = dot("te,de->td", d_joined, qkv_full)
    attn_terms = jnp.concatenate([qkv_grad, beside(dense_grad)], axis=2)
    attn_sum = dp_reduce(lambda i: pick(attn_terms, i))

    upper = dot("td,df->tf", mlp_in, up_full) + own_up_bias
    cdf = 0.5 * (1.0 + lax.erf(upper * F32(0.7071067811865476)))
    pdf = jnp.exp(-0.5 * upper * upper) * F32(0.3989422804014327)
    act = (upper * cdf).astype(BF)
    d_act = dot("td,fd->tf", grad_group, down_full)
    d_up = (d_act * (cdf + upper * pdf)).astype(BF)
    down_grad = dot("tf,td->fd", act, grad_group).astype(BF).reshape(n_dp, unit_rows, width)
    up_grad = dot("td,tf->df", mlp_in, d_up).astype(BF).reshape(n_dp, up_rows, width)
    mlp_out = dot("tf,fd->td", act, down_full)
    d_mlp_in = dot("tf,df->td", d_up, up_full)

    mine = jnp.arange(n_seq) == me
    qkv_bias_grad = jnp.sum(d_joined.astype(F32), axis=0)
    qkv_bias_grad = from_heads(jnp.where(mine[:, None], qkv_bias_grad[None], 0.0))
    up_bias_grad = jnp.sum(d_up.astype(F32), axis=0).reshape(n_dp, 1, unit_rows)
    up_bias_grad = jnp.where(mine[None, :, None], up_bias_grad, 0.0)
    bias_sum = jnp.sum(grad_out.astype(F32), axis=0)
    terms = (
        jnp.sum(d_attn_in * unit, axis=0),
        jnp.sum(d_attn_in, axis=0),
        jnp.sum(d_mlp_in * unit, axis=0),
        jnp.sum(d_mlp_in, axis=0),
        qkv_bias_grad,
        bias_sum,
        up_bias_grad,
        bias_sum,
    )
    terms = [t.reshape(n_dp, n_seq, size) for t, size in zip(terms, sizes)]
    terms = jnp.concatenate(terms, axis=2).reshape(n_dp, n_seq * length)
    tail_rows = -(-n_seq * length // width)
    tail_rows += -tail_rows % 8
    terms = jnp.pad(terms, ((0, 0), (0, tail_rows * width - n_seq * length)))
    terms = terms.reshape(n_dp, tail_rows, width).astype(BF)
    mlp_sum = dp_reduce(lambda i: jnp.concatenate([pick(up_grad, i), pick(down_grad, i), pick(terms, i)], axis=0))

    upstream = d_attn_in * f_attn_gain + d_mlp_in * f_mlp_gain
    pair = jnp.concatenate([(attn_out + mlp_out).astype(BF), upstream.astype(BF)], axis=1)
    pair = seq_reduce(pair.reshape(n_seq, rows, 2 * width))
    block_out = hidden_in.astype(F32) + f_dense_bias + f_down_bias + pair[:, :width]
    upstream = pair[:, width:]
    x = hidden_in.astype(F32)
    centered = x - jnp.mean(x, axis=-1, keepdims=True)
    inverse = lax.rsqrt(jnp.mean(centered * centered, axis=-1, keepdims=True) + EPS)
    own_unit = centered * inverse
    inner = (
        upstream
        - jnp.mean(upstream, axis=-1, keepdims=True)
        - own_unit * jnp.mean(upstream * own_unit, axis=-1, keepdims=True)
    )
    grad_in = grad_out.astype(F32) + inverse * inner

    qkv_back = attn_sum[:, : 3 * own].reshape(n_seq, deep, 3 * own).astype(BF)
    qkv_own = from_heads(seq_exchange(qkv_back).astype(F32))
    dense_own = from_beside(attn_sum[:, 3 * own :])
    vec_sum = mlp_sum[up_rows + unit_rows :].reshape(-1)[: n_seq * length].reshape(n_seq, 1, length)
    vec_sum = jnp.pad(vec_sum, ((0, 0), (0, 0), (0, -length % own_units)))
    vec_sum = vec_sum.reshape(n_seq, -1, own_units)
    back = jnp.concatenate([mlp_sum[:up_rows].reshape(n_seq, deep, own_units), vec_sum], axis=1)
    back = seq_exchange(back.astype(BF)).astype(F32)
    up_own = jnp.moveaxis(back[:, :deep].reshape(n_seq, deep, n_dp, unit_rows), 0, 2)
    vec_own = jnp.sum(back[:, deep:].reshape(n_seq, -1), axis=0)
    owned = []
    start = 0
    for size in sizes:
        owned.append(vec_own[start : start + size])
        start += size
    return (
        block_out.astype(BF),
        grad_in.astype(BF),
        owned[0],
        owned[1],
        owned[2],
        owned[3],
        qkv_own,
        owned[4],
        dense_own,
        owned[5],
        up_own.reshape(deep, hidden_units),
        owned[6],
        mlp_sum[up_rows : up_rows + unit_rows],
        owned[7],
    )


SCALE = HEAD_DIM**-0.5


def kernel_call(body, outs, args, scratch=(), megabytes=24, flops=0, apart=0):
    moved = sum(a.size * a.dtype.itemsize for a in args)
    held = [pl.BlockSpec(memory_space=pl.ANY)] * apart
    held += [pl.BlockSpec(memory_space=pltpu.VMEM)] * (len(args) - apart)
    return pl.pallas_call(
        body,
        out_shape=tuple(jax.ShapeDtypeStruct(shape, kind) for shape, kind in outs),
        in_specs=held,
        scratch_shapes=[pltpu.VMEM(*item) if isinstance(item, tuple) else item for item in scratch],
        compiler_params=pltpu.CompilerParams(vmem_limit_bytes=megabytes << 20),
        cost_estimate=pl.CostEstimate(flops=flops, bytes_accessed=moved, transcendentals=0),
    )(*args)


def dot_nn(a, b):
    return lax.dot_general(a, b, (((1,), (0,)), ((), ())), preferred_element_type=F32)


def dot_nt(a, b):
    return lax.dot_general(a, b, (((1,), (1,)), ((), ())), preferred_element_type=F32)


def dot_tn(a, b):
    return lax.dot_general(a, b, (((0,), (0,)), ((), ())), preferred_element_type=F32)


def line_and_side():
    me = lax.axis_index("dp")
    return lax.shift_right_logical(me, 1), lax.bitwise_and(me, 1)


PAIR_SWAP = [(i, i ^ 2) for i in range(8)]
HALF_SWAP = [(i, i ^ 4) for i in range(8)]
LINE_ORDER = (0, 2, 1, 3)


def dp_index(line, step, side):
    return 2 * lax.bitwise_xor(line, step) + side


def pick_blocks(block_of, send, keep):
    line, side = line_and_side()
    for j, step in enumerate(LINE_ORDER):
        send[j] = block_of(dp_index(line, step, 1 - side))
        keep[j] = block_of(dp_index(line, step, side))


def add_kernel(here, there, *out):
    place = 0
    for ref in out:
        for j in range(ref.shape[0]):
            ref[j] = (here[place + j].astype(F32) + there[place + j].astype(F32)).astype(ref.dtype)
        place += ref.shape[0]


def add_blocks(here, there, *counts, waits=()):
    shape = here.shape[1:]
    return kernel_call(
        with_waits(len(waits), add_kernel),
        tuple(((count,) + shape, BF) for count in counts),
        (*waits, here, there),
        megabytes=8,
        apart=len(waits),
    )


def once(values, *others):
    return lax.optimization_barrier((values, *others))[0]


def seq_shuffle(blocks):
    got = [blocks[0]]
    for other in (1, 2, 3):
        pairs = [(i, i ^ other) for i in range(4)]
        got.append(lax.ppermute(blocks[other], "seq", pairs))
    return got


def place_kernel(deep, *refs):
    pieces, (dy, weights, dense, vectors), d_blocks, (rows32, d_rows) = refs[:4], refs[4:8], refs[8:12], refs[12:]
    line, side = line_and_side()
    per_line = 4 * deep
    quarter = dy.shape[1] // 4
    own = weights.shape[1] - quarter
    total = jnp.zeros(vectors.shape, F32)
    for place in range(8):
        piece = pieces[place // 2].at[place % 2]
        owner = dp_index(line, LINE_ORDER[place % 4], side if place < 4 else 1 - side)
        weights[pl.ds(pl.multiple_of(owner * per_line, per_line), per_line), :] = piece[:per_line, :]
        total = total + piece[per_line:, :].astype(F32)
        beside = piece[:per_line, own:].astype(F32)
        for q in range(4):
            rows32[pl.ds(pl.multiple_of(owner * deep, 8), deep), q * quarter : (q + 1) * quarter] = beside[
                q * deep : (q + 1) * deep
            ]
    vectors[...] = total
    dense[...] = rows32[...].astype(BF)
    d_rows[...] = dot_nt(dense[...], dy[...]).astype(BF)
    me = lax.axis_index("seq")
    count = d_blocks[0].shape[0]
    for j in range(4):
        d_blocks[j][...] = d_rows[pl.ds(pl.multiple_of(lax.bitwise_xor(me, j) * count, 16), count), :]


def turn(values, cosine, sine_a, sine_b, sign):
    half = ROT // 2
    ahead = pltpu.roll(values, 128 - half, 1)
    behind = pltpu.roll(values, half, 1)
    return values * cosine + sign * (ahead * sine_a + behind * sine_b)


def project_kernel(unit, weights, vectors, cosine, sine_a, sine_b, attn_in, qk, v):
    gain, shift, bias = vectors[0:1, :], vectors[1:2, :], vectors[6:7, :]
    turned = qk.shape[1]
    size = 128

    def step(i, carry):
        rows = pl.ds(pl.multiple_of(i * size, size), size)
        normed = (unit[rows, :] * gain + shift).astype(BF)
        attn_in[rows, :] = normed
        joined = dot_nn(normed, weights[...]) + bias
        tables = cosine[rows, :], sine_a[rows, :], sine_b[rows, :]
        for c in range(0, turned, 128):
            qk[rows, c : c + 128] = turn(joined[:, c : c + 128], *tables, 1.0).astype(BF)
        v[rows, :] = joined[:, turned : turned + v.shape[1]].astype(BF)
        return carry

    lax.fori_loop(0, unit.shape[0] // size, step, 0)


def attention_kernel(deep, *refs):
    qk, v, d0, d1, d2, d3, seg_column, seg_row, cosine, sine_a, sine_b = refs[:11]
    given, d_joined, (d_t, out_t, dk_t, dv_t, acc) = refs[11:15], refs[15], refs[16:]
    tokens, own = v.shape
    me = lax.axis_index("seq")
    runs = own // (4 * deep)
    for j, ref in enumerate((d0, d1, d2, d3)):
        source = lax.bitwise_xor(me, j)
        block = ref[...].astype(F32)
        for r in range(runs):
            place = pl.multiple_of(r * 4 * deep + source * deep, 8)
            d_t[pl.ds(place, deep), :] = block[r * deep : (r + 1) * deep]
    d_out = jnp.transpose(d_t[...]).astype(BF)
    q_t = jnp.transpose(qk[:, :own].astype(F32)).astype(BF)
    d_tb = d_t[...].astype(BF)
    dk_t[...] = jnp.zeros(dk_t.shape, F32)
    dv_t[...] = jnp.zeros(dv_t.shape, F32)
    size = 256
    for h in range(own // HEAD_DIM):
        lanes = slice(h * HEAD_DIM, (h + 1) * HEAD_DIM)
        q_h = qk[:, lanes]
        k_h = qk[:, own + h * HEAD_DIM : own + (h + 1) * HEAD_DIM]
        v_h = v[:, lanes]
        d_h = d_out[:, lanes]
        for first in range(0, tokens, size):
            rows = slice(first, first + size)
            n = first + size
            scores = dot_nt(q_h[rows], k_h[:n]) * SCALE
            query = lax.broadcasted_iota(jnp.int32, (size, n), 0) + first
            key = lax.broadcasted_iota(jnp.int32, (size, n), 1)
            allowed = (seg_column[rows, :] == seg_row[:, :n]) & (key <= query)
            scores = jnp.where(allowed, scores, NEGATIVE)
            weights = jnp.where(allowed, jnp.exp(scores - jnp.max(scores, axis=1, keepdims=True)), 0.0)
            probs = weights * (1.0 / jnp.sum(weights, axis=1, keepdims=True))
            probs_r = probs.astype(BF)
            out_t[lanes, rows] = jnp.transpose(dot_nn(probs_r, v_h[:n]))
            d_probs = dot_nt(d_h[rows], v_h[:n])
            delta = jnp.sum(probs * d_probs, axis=1, keepdims=True)
            d_scores = (probs * (d_probs - delta)).astype(BF)
            acc[rows, lanes] = dot_nn(d_scores, k_h[:n]) * SCALE
            dk_t[lanes, :n] += dot_nn(q_t[lanes, rows], d_scores)
            dv_t[lanes, :n] += dot_nn(d_tb[lanes, rows], probs_r)
    acc[:, own : 2 * own] = jnp.transpose(dk_t[...]) * SCALE
    for c in range(0, 2 * own, 128):
        turned = turn(acc[:, c : c + 128], cosine[...], sine_a[...], sine_b[...], -1.0)
        d_joined[:, c : c + 128] = turned.astype(BF)
    d_joined[:, 2 * own : 3 * own] = jnp.transpose(dv_t[...]).astype(BF)
    d_joined[:, 3 * own :] = jnp.zeros((tokens, d_joined.shape[1] - 3 * own), BF)
    for j in range(4):
        target = lax.bitwise_xor(me, j)
        parts = [out_t[pl.ds(pl.multiple_of(r * 4 * deep + target * deep, 8), deep), :] for r in range(runs)]
        given[j][...] = jnp.concatenate(parts, axis=0).astype(BF)


def attention_grads_kernel(deep, *refs):
    r0, r1, r2, r3, dense, dy, attn_in, d_joined, weights, unit, vectors = refs[:11]
    picks, (attn_out, scaled, sums), (rows_t, grads) = refs[11:13], refs[13:16], refs[16:]
    me = lax.axis_index("seq")
    count = r0.shape[0]
    width = dy.shape[1]
    quarter = width // 4
    own = width - quarter
    for j, ref in enumerate((r0, r1, r2, r3)):
        rows_t[pl.ds(pl.multiple_of(lax.bitwise_xor(me, j) * count, 16), count), :] = ref[...]
    size = 128
    for c in range(0, width, size):
        grads[c : c + size, :] = dot_tn(attn_in[:, c : c + size], d_joined[...])
    dense_grad = dot_nn(rows_t[...], dy[...])
    for p in range(8):
        for q in range(4):
            start = p * 4 * deep + q * deep
            grads[start : start + deep, own:] = dense_grad[p * deep : (p + 1) * deep, q * quarter : (q + 1) * quarter]
    per_line = 4 * deep

    def block_of(index):
        return grads[pl.ds(pl.multiple_of(index * per_line, per_line), per_line), :].astype(BF)

    pick_blocks(block_of, *picks)
    attended = jnp.transpose(rows_t[...].astype(F32)).astype(BF)
    gain = vectors[0:1, :]
    tokens = dy.shape[0]
    sums[...] = jnp.zeros(sums.shape, F32)
    for c in range(0, tokens, size):
        rows = slice(c, c + size)
        attn_out[rows, :] = dot_nn(attended[rows], dense[...])
        back = dot_nt(d_joined[rows, :], weights[...])
        scaled[rows, :] = back * gain
        sums[0:1, :] += jnp.sum(back * unit[rows, :], axis=0, keepdims=True)
        sums[1:2, :] += jnp.sum(back, axis=0, keepdims=True)
        sums[5:6, :] += jnp.sum(d_joined[rows, :].astype(F32), axis=0, keepdims=True)


def pack_kernel(deep, *refs):
    qkv, up, by_width, qkv_bias, x, dy, blocks, mine, (all_blocks, row_block) = *refs[:6], refs[6:10], *refs[10:11], refs[11:]
    width = qkv.shape[1] // 3
    own = width // 4
    units = up.shape[1] // 32
    me = lax.axis_index("seq")
    device = 4 * lax.axis_index("dp") + me
    row_block[...] = jnp.zeros(row_block.shape, F32)
    row_block[:6, :deep] = by_width[...].astype(F32)
    vectors = pltpu.roll(row_block[:, :width], device * deep, 1)
    row_block[0:6, :] = jnp.zeros((6, row_block.shape[1]), F32)
    row_block[6:7, : 3 * deep] = qkv_bias[...].astype(F32)
    bias_rows = pltpu.roll(row_block[...], device * (3 * deep), 1)
    up_values, qkv_values = up[...].astype(F32), qkv[...].astype(F32)
    empty = jnp.zeros((deep + 8, own), F32)
    both = jnp.concatenate([qkv_values, bias_rows], axis=0)
    for t in range(4):
        parts = [up_values[:, ((l * 2 + y) * 4 + t) * units :][:, :units] for y in range(2) for l in range(4)]
        all_blocks[t, :deep, :] = jnp.concatenate(parts, axis=1)
        parts = [both[:, part * width + t * own : part * width + (t + 1) * own] for part in range(3)]
        parts = jnp.concatenate(parts + [empty], axis=1)
        all_blocks[t, deep : 2 * deep, :] = parts[:deep]
        all_blocks[t, 2 * deep :, :] = parts[deep:] + vectors
    rows = x.shape[0]
    for j in range(4):
        blocks[j][...] = all_blocks[lax.bitwise_xor(me, j)].astype(BF)
    mine[:rows, :] = x[...]
    mine[rows:, :] = dy[...]


def unpack_kernel(deep, r0, r1, r2, r3, dense, up_bias, attn_piece, up_keep, up_give, up32, qkv32, row_block):
    me = lax.axis_index("seq")
    line, side = line_and_side()
    width = dense.shape[1]
    quarter = width // 4
    half = up_keep.shape[1]
    own = 3 * quarter
    extra = jnp.zeros((8, width), F32)
    for j, ref in enumerate((r0, r1, r2, r3)):
        block = ref[...].astype(F32)
        place = pl.ds(pl.multiple_of(lax.bitwise_xor(me, j) * deep, 8), deep)
        up32[place, :] = block[:deep]
        qkv32[place, :] = block[deep : 2 * deep]
        extra = extra + block[2 * deep :]
    rows = 4 * deep
    first, second = up32[:, :half], up32[:, half:]
    up_keep[...] = jnp.where(side == 0, first, second).astype(BF)
    up_give[...] = jnp.where(side == 0, second, first).astype(BF)
    attn_piece[:rows, :own] = qkv32[:, :own].astype(BF)
    dense_values = dense[...].astype(F32)
    beside = [dense_values[:, q * quarter : (q + 1) * quarter] for q in range(4)]
    attn_piece[:rows, own:] = jnp.concatenate(beside, axis=0).astype(BF)
    units = half // 4
    row_block[...] = jnp.zeros(row_block.shape, F32)
    row_block[7:8, :units] = up_bias[...].astype(F32)
    attn_piece[rows:, :] = (extra + pltpu.roll(row_block[...], side * half + line * units, 1)).astype(BF)


def mlp_kernel(*refs):
    pieces, (unit_own, unit_other, dy_own, dy_other, vectors, attn_out, scaled, sums_in) = refs[:2], refs[2:10]
    give, keep, keep_terms, send_terms, up, down, mlp_in, act, d_up, sums, up_grad, down_grad, done = refs[10:]
    line, side = line_and_side()
    width, half = up.shape
    units = half // 4
    copies = []
    for place, step in enumerate(LINE_ORDER):
        piece = pieces[place // 2].at[place % 2]
        l = lax.bitwise_xor(line, step)
        top, low = pl.ds(0, units), pl.ds(units, units)
        for source, target in (
            (piece.at[top, :], down.at[pl.ds(pl.multiple_of(l * units, 32), units), :]),
            (piece.at[low, pl.ds(0, half)], up.at[pl.ds(pl.multiple_of(2 * l * units, 32), units), :]),
            (piece.at[low, pl.ds(half, half)], up.at[pl.ds(pl.multiple_of((2 * l + 1) * units, 32), units), :]),
        ):
            copies.append(pltpu.make_async_copy(source, target, done.at[len(copies)]))
    for copy in copies:
        copy.start()
    gain, shift = vectors[2:3, :], vectors[3:4, :]
    bias = jnp.where(side == 0, vectors[7:8, :half], vectors[7:8, half:])
    sums[...] = sums_in[...]
    group = unit_own.shape[0]
    size = group // 4
    core = lax.bitwise_and(lax.axis_index("seq"), 1)
    for copy in copies:
        copy.wait()

    def tokens(unit, dy, offset, own):
        def step(i, carry):
            rows = pl.ds(pl.multiple_of(i * size, size), size)
            all_rows = pl.ds(pl.multiple_of(offset + i * size, size), size)
            u = unit[rows, :]
            normed = (u * gain + shift).astype(BF)
            mlp_in[all_rows, :] = normed
            upper = dot_nn(normed, up[...]) + bias
            cdf = 0.5 * (1.0 + lax.erf(upper * 0.7071067811865476))
            pdf = jnp.exp(-0.5 * upper * upper) * 0.3989422804014327
            act_rows = (upper * cdf).astype(BF)
            act[all_rows, :] = act_rows
            g = dy[rows, :]
            d_rows = (dot_nt(g, down[...]) * (cdf + upper * pdf)).astype(BF)
            d_up[all_rows, :] = d_rows
            out = dot_nn(act_rows, down[...])
            back = dot_nt(d_rows, up[...])
            sums[2:3, :] += jnp.sum(back * u, axis=0, keepdims=True)
            sums[3:4, :] += jnp.sum(back, axis=0, keepdims=True)
            sums[6:7, :half] += jnp.sum(d_rows.astype(F32), axis=0, keepdims=True)
            back = back * gain
            if own:
                out = out + attn_out[rows, :]
                back = back + scaled[rows, :]
                sums[4:5, :] += 0.25 * jnp.sum(g.astype(F32), axis=0, keepdims=True)
            place = (0 if own else 2) + lax.shift_right_logical(i, 1)
            out, back = out.astype(BF), back.astype(BF)

            @pl.when(lax.bitwise_and(i, 1) == core)
            def _():
                keep[place, :, :width] = out
                keep[place, :, width:] = back

            @pl.when(lax.bitwise_and(i, 1) != core)
            def _():
                give[place, :, :width] = out
                give[place, :, width:] = back

            return carry

        lax.fori_loop(0, 4, step, 0)

    tokens(unit_own, dy_own, 0, True)
    tokens(unit_other, dy_other, group, False)
    for c in range(0, width, 128):
        up_grad[c : c + 128, :] = dot_tn(mlp_in[:, c : c + 128], d_up[...]).astype(BF)
    for c in range(0, half, 128):
        total = dot_tn(act[:group, c : c + 128], dy_own[...]) + dot_tn(act[group:, c : c + 128], dy_other[...])
        down_grad[c : c + 128, :] = total.astype(BF)
    tail = sums[...].astype(BF)
    for place, step in enumerate(LINE_ORDER):
        ref = (keep_terms, send_terms)[place // 2].at[place % 2]
        l = lax.bitwise_xor(line, step)
        ref[:units, :] = down_grad[pl.ds(pl.multiple_of(l * units, 32), units), :]
        ref[units : 2 * units, :half] = up_grad[pl.ds(pl.multiple_of(2 * l * units, 32), units), :]
        ref[units : 2 * units, half:] = up_grad[pl.ds(pl.multiple_of((2 * l + 1) * units, 32), units), :]
        ref[2 * units :, :] = tail


def mlp_sum_kernel(own, far, down_own, up_keep, up_give, tail):
    units, width = down_own.shape
    half = width // 2
    _, side = line_and_side()
    refs = (own.at[0], far.at[0])

    def total(rows, lanes):
        return sum(ref[rows, lanes].astype(F32) for ref in refs)

    down_own[...] = total(slice(0, units), slice(None))
    first = total(slice(units, 2 * units), slice(0, half))
    second = total(slice(units, 2 * units), slice(half, width))
    last = total(slice(2 * units, 2 * units + 8), slice(None))
    tail[...] = last
    up_keep[...] = jnp.where(side == 0, first, second).astype(BF)
    up_give[:units, :] = jnp.where(side == 0, second, first).astype(BF)
    up_give[units:, :] = jnp.concatenate([last[:, :half], last[:, half:]], axis=0).astype(BF)


def owners_kernel(deep, keep, far, tail, b0, b1, b2, b3, rows32):
    _, side = line_and_side()
    me = lax.axis_index("seq")
    rows, half = keep.shape
    here, there = keep[...].astype(F32), far[:rows, :].astype(F32)
    rows32[:, :half] = jnp.where(side == 0, here, there)
    rows32[:, half:] = jnp.where(side == 0, there, here)
    far_tail = far[rows:, :].astype(F32)
    last = tail[...] + jnp.concatenate([far_tail[:8], far_tail[8:]], axis=1)
    for j, ref in enumerate((b0, b1, b2, b3)):
        target = lax.bitwise_xor(me, j)
        block = rows32[pl.ds(pl.multiple_of(target * deep, 8), deep), :]
        ref[...] = jnp.concatenate([block, last], axis=0).astype(BF)


def owned_kernel(deep, b0, b1, b2, b3, tail, up_own, vec_own, sources, row_block):
    line, _ = line_and_side()
    me = lax.axis_index("seq")
    device = 4 * lax.axis_index("dp") + me
    width = tail.shape[1]
    half, own = width // 2, width // 4
    units = half // 4
    for j, ref in enumerate((b0, b1, b2, b3)):
        sources[lax.bitwise_xor(me, j)] = ref[...].astype(F32)
    for l in range(4):
        parts = [
            sources[t, :deep, y * half + l * units : y * half + (l + 1) * units] for y in range(2) for t in range(4)
        ]
        up_own[:, l * 2 * half : (l + 1) * 2 * half] = jnp.concatenate(parts, axis=1)
    total = sources[0, deep:] + sources[1, deep:] + sources[2, deep:] + sources[3, deep:]
    rolled = pltpu.roll(total, width - device * deep, 1)
    vec_own[...] = rolled[:, :128]
    row_block[...] = jnp.zeros(row_block.shape, F32)
    for t in range(4):
        row = sources[t, deep + 5 : deep + 6, :]
        for part in range(3):
            place = part * width + t * own
            row_block[5:6, place : place + own] = row[:, part * own : (part + 1) * own]
    rolled = pltpu.roll(row_block[...], 3 * width - device * (3 * deep), 1)
    vec_own[5:6, :] = rolled[5:6, :128]
    rolled = pltpu.roll(tail[...], width - line * units, 1)
    vec_own[6:7, :] = rolled[6:7, :128]


def attention_sum_kernel(deep, own, far, b0, b1, b2, b3, dense_own, total):
    me = lax.axis_index("seq")
    total[...] = own[0].astype(F32) + far[0].astype(F32)
    quarter = total.shape[1] // 4
    for q in range(4):
        dense_own[:, q * quarter : (q + 1) * quarter] = total[q * deep : (q + 1) * deep, 3 * quarter :]
    for j, ref in enumerate((b0, b1, b2, b3)):
        target = lax.bitwise_xor(me, j)
        ref[...] = total[pl.ds(pl.multiple_of(target * deep, 8), deep), : 3 * quarter].astype(BF)


def attention_owned_kernel(b0, b1, b2, b3, qkv_own, sources):
    me = lax.axis_index("seq")
    width = qkv_own.shape[1] // 3
    own = width // 4
    for j, ref in enumerate((b0, b1, b2, b3)):
        sources[lax.bitwise_xor(me, j)] = ref[...].astype(F32)
    for part in range(3):
        lanes = slice(part * own, (part + 1) * own)
        whole = jnp.concatenate([sources[t, :, lanes] for t in range(4)], axis=1)
        qkv_own[:, part * width : (part + 1) * width] = whole


def with_waits(count, body):
    def wrapped(*refs):
        body(*refs[count:])

    return wrapped


def line_device(
    hidden_in,
    lengths,
    grad_out,
    attn_gain,
    attn_shift,
    mlp_gain,
    mlp_shift,
    qkv_weight,
    qkv_bias,
    dense_weight,
    dense_bias,
    up_weight,
    up_bias,
    down_weight,
    down_bias,
):
    n_dp, n_seq = 8, 4
    dp_me, me = lax.axis_index("dp"), lax.axis_index("seq")
    line, side = lax.shift_right_logical(dp_me, 1), lax.bitwise_and(dp_me, 1)
    chip, core = lax.shift_right_logical(me, 1), lax.bitwise_and(me, 1)
    device = dp_me * n_seq + me
    zero = jnp.int32(0)
    rows, width = hidden_in.shape
    group = rows * n_seq
    hidden_units = up_weight.shape[1]
    units = hidden_units // (n_dp * n_seq)
    half = hidden_units // 8
    deep = width // (n_dp * n_seq)
    per_line = n_seq * deep
    own = width // n_seq
    wide = 2 * half + 3 * own
    flat = (group, width)

    by_width = jnp.stack([attn_gain, attn_shift, mlp_gain, mlp_shift, dense_bias, down_bias])
    *blocks, mine = kernel_call(
        functools.partial(pack_kernel, deep),
        (((2 * deep + 8, width), BF),) * 4 + (((2 * rows, width), BF),),
        (qkv_weight, up_weight, by_width, qkv_bias[None], hidden_in, grad_out),
        scratch=(((4, 2 * deep + 8, width), F32), ((8, 3 * width), F32)),
        megabytes=16,
    )
    attn_piece, up_keep, up_give = kernel_call(
        functools.partial(unpack_kernel, deep),
        (((per_line + 8, width), BF), ((per_line, half), BF), ((per_line, half), BF)),
        (*seq_shuffle(blocks), dense_weight, up_bias[None]),
        scratch=(((per_line, width), F32), ((per_line, width), F32), ((8, width), F32)),
        megabytes=16,
    )

    across = lax.ppermute(mine, "dp", SIDE_SWAP)
    attn_half = lax.ppermute(attn_piece, "dp", HALF_SWAP)
    up_far = lax.ppermute(up_give, "dp", SIDE_SWAP)
    chip_far = lax.ppermute(once(mine, up_keep), "seq", CHIP_SWAP)

    attn_two = once(jnp.stack([attn_piece, attn_half]), up_far)
    attn_pair = lax.ppermute(attn_two, "dp", PAIR_SWAP)
    attn_side = lax.ppermute(attn_two, "dp", SIDE_SWAP)
    up_both = jnp.concatenate(
        [jnp.where(side == 0, up_keep, up_far), jnp.where(side == 0, up_far, up_keep)], axis=1
    )
    mlp_piece = once(jnp.concatenate([down_weight, up_both], axis=0), attn_half)
    mlp_half = lax.ppermute(mlp_piece, "dp", HALF_SWAP)
    by_chip = once(in_order(chip == 1, mine, chip_far), attn_half, up_far)
    core_far = lax.ppermute(by_chip, "seq", CORE_SWAP)

    attn_far = lax.ppermute(once(attn_pair, mlp_half), "dp", SIDE_SWAP)
    mlp_two = once(jnp.stack([mlp_piece, mlp_half]), attn_pair)
    mlp_pair = lax.ppermute(mlp_two, "dp", PAIR_SWAP)
    chip_beyond = lax.ppermute(once(across, mlp_half, attn_pair, attn_side), "seq", CHIP_SWAP)
    by_chip_beyond = once(in_order(chip == 1, across, chip_beyond), mlp_pair, attn_far)
    core_beyond = lax.ppermute(by_chip_beyond, "seq", CORE_SWAP)

    def whole_group(values, over):
        full = in_order(core == 1, values, over, axis=1).reshape(n_seq, 2, rows, width)
        return full[:, 0].reshape(flat), full[:, 1].reshape(flat)

    hidden_group, dy = whole_group(by_chip, core_far)
    hidden_other, dy_other = whole_group(by_chip_beyond, core_beyond)
    attn_pieces = (attn_two, attn_pair, attn_side, attn_far)

    row_lengths = lengths[0]
    segment, position = place(row_lengths, jnp.arange(group, dtype=jnp.int32))
    lane = jnp.arange(128, dtype=jnp.int32) % HEAD_DIM
    powers = jnp.power(F32(10000.0), -(2.0 * (lane % (ROT // 2)).astype(F32)) / ROT)
    angles = position.astype(F32)[:, None] * powers[None, :]
    cosine = jnp.where(lane < ROT, jnp.cos(angles), 1.0)
    sine = jnp.sin(angles)
    sine_a = jnp.where(lane < ROT // 2, -sine, 0.0)
    sine_b = jnp.where((lane >= ROT // 2) & (lane < ROT), sine, 0.0)

    def normed(values):
        centered = values - jnp.mean(values, axis=-1, keepdims=True)
        inverse = lax.rsqrt(jnp.mean(centered * centered, axis=-1, keepdims=True) + EPS)
        return centered * inverse, inverse

    unit = normed(hidden_group.astype(F32))[0]
    unit_other = normed(hidden_other.astype(F32))[0]

    placed = kernel_call(
        functools.partial(place_kernel, deep),
        ((flat[1:] * 2, BF), ((n_dp * deep, width), BF), ((8, width), F32)) + (((2 * deep, group), BF),) * 4,
        attn_pieces + (dy,),
        scratch=(((n_dp * deep, width), F32), ((n_dp * deep, group), BF)),
        flops=2 * n_dp * deep * width * group,
    )
    weights, dense, vectors = placed[:3]
    d_blocks = seq_shuffle(placed[3:])
    attn_in, qk, v = kernel_call(
        project_kernel,
        ((flat, BF), ((group, 2 * own), BF), ((group, own), BF)),
        (unit, weights, vectors, cosine, sine_a, sine_b),
        flops=2 * group * width * width,
    )
    attended = kernel_call(
        with_waits(1, functools.partial(attention_kernel, deep)),
        (((2 * deep, group), BF),) * 4 + ((flat, BF),),
        (mlp_pair, qk, v, *d_blocks, segment[:, None], segment[None, :], cosine, sine_a, sine_b),
        scratch=(((own, group), F32),) * 4 + ((flat, F32),),
        flops=14 * group * group * own,
        apart=1,
    )
    d_joined = attended[4]
    row_blocks = seq_shuffle(attended[:4])
    results = kernel_call(
        with_waits(1, functools.partial(attention_grads_kernel, deep)),
        (((4, per_line, width), BF),) * 2 + ((flat, F32), (flat, F32), ((8, width), F32)),
        (core_beyond, *row_blocks, dense, dy, attn_in, d_joined, weights, unit, vectors),
        scratch=(((n_dp * deep, group), BF), ((width, width), F32)),
        flops=5 * group * width * width,
        megabytes=32,
        apart=1,
    )
    attn_send, attn_keep = results[:2]

    give, keep, *results = kernel_call(
        mlp_kernel,
        (((4, rows, 2 * width), BF),) * 2 + (((2, 2 * units + 8, width), BF),) * 2,
        (mlp_two, mlp_pair, unit, unit_other, dy, dy_other, vectors) + tuple(results[2:]),
        scratch=(
            ((width, half), BF),
            ((half, width), BF),
            ((2 * group, width), BF),
            ((2 * group, half), BF),
            ((2 * group, half), BF),
            ((8, width), F32),
            ((width, half), BF),
            ((half, width), BF),
            pltpu.SemaphoreType.DMA((12,)),
        ),
        flops=12 * group * width * 2 * half,
        megabytes=32,
        apart=2,
    )
    keep_terms, send_terms = results
    mlp_got = lax.ppermute(send_terms, "dp", PAIR_SWAP)
    attn_moved = lax.ppermute(once(attn_send, keep_terms), "dp", SIDE_SWAP)
    both = keep.astype(F32) + lax.ppermute(give, "seq", CORE_SWAP).astype(F32)
    beyond = lax.ppermute(both[2:].astype(BF), "dp", SIDE_SWAP)
    mlp_mine, mlp_send = add_blocks(keep_terms, mlp_got, 1, 1)
    mlp_last = lax.ppermute(mlp_send, "dp", HALF_SWAP)
    attn_mine, attn_send = add_blocks(attn_keep, attn_moved, 2, 2, waits=(mlp_got,))
    attn_got = lax.ppermute(attn_send, "dp", PAIR_SWAP)
    attn_mine, attn_send = add_blocks(attn_mine, attn_got, 1, 1, waits=(mlp_send,))
    attn_last = lax.ppermute(attn_send, "dp", HALF_SWAP)

    both = both[:2] + beyond.astype(F32)
    chip_last = lax.ppermute(pick(both, 1 - chip).astype(BF), "seq", CHIP_SWAP)
    pair = pick(both, chip) + chip_last.astype(F32)
    x = hidden_in.astype(F32)
    block_out = x + vectors[4] + vectors[5] + pair[:, :width]
    upstream = pair[:, width:]
    own_unit, inverse = normed(x)
    inner = (
        upstream
        - jnp.mean(upstream, axis=-1, keepdims=True)
        - own_unit * jnp.mean(upstream * own_unit, axis=-1, keepdims=True)
    )
    grad_in = grad_out.astype(F32) + inverse * inner

    down_own, up_keep, up_give, tail = kernel_call(
        with_waits(1, mlp_sum_kernel),
        (((units, width), F32), ((per_line, half), BF), ((per_line + 16, half), BF), ((8, width), F32)),
        (beyond, mlp_mine, mlp_last),
        megabytes=8,
        apart=1,
    )
    up_far = lax.ppermute(up_give, "dp", SIDE_SWAP)
    blocks = kernel_call(
        functools.partial(owners_kernel, deep),
        (((deep + 8, width), BF),) * 4,
        (up_keep, up_far, tail),
        scratch=(((per_line, width), F32),),
        megabytes=8,
    )
    up_own, vec_own = kernel_call(
        with_waits(2, functools.partial(owned_kernel, deep)),
        (((deep, hidden_units), F32), ((8, 128), F32)),
        (chip_last, attn_last, *seq_shuffle(blocks), tail),
        scratch=(((4, deep + 8, width), F32), ((8, 3 * width), F32)),
        megabytes=8,
        apart=2,
    )
    *blocks, dense_own = kernel_call(
        with_waits(1, functools.partial(attention_sum_kernel, deep)),
        (((deep, 3 * own), BF),) * 4 + (((deep, width), F32),),
        (up_far, attn_mine, attn_last),
        scratch=(((per_line, width), F32),),
        megabytes=8,
        apart=1,
    )
    (qkv_own,) = kernel_call(
        attention_owned_kernel,
        (((deep, 3 * width), F32),),
        tuple(seq_shuffle(blocks)),
        scratch=(((4, deep, 3 * own), F32),),
        megabytes=8,
    )
    by_width = vec_own[:5, :deep]
    qkv_bias_grad = vec_own[5, : 3 * deep]
    up_bias_grad = vec_own[6, :units]
    return (
        block_out.astype(BF),
        grad_in.astype(BF),
        by_width[0],
        by_width[1],
        by_width[2],
        by_width[3],
        qkv_own,
        qkv_bias_grad,
        dense_own,
        by_width[4],
        up_own,
        up_bias_grad,
        down_own,
        by_width[4],
    )


def per_device(*args):
    if lax.axis_size("dp") == 8 and lax.axis_size("seq") == 4:
        return line_device(*args)
    return general_device(*args)


def solution(mesh):
    both = ("dp", "seq")
    matrix, vector = P(both, None), P(both)
    params = (vector, vector, vector, vector, matrix, vector, matrix, vector, matrix, vector, matrix, vector)
    return jax.shard_map(
        per_device,
        mesh=mesh,
        in_specs=(matrix, P("dp", None), matrix) + params,
        out_specs=(matrix, matrix) + params,
        check_vma=False,
    )
```

```python
import functools

import jax
import jax.numpy as jnp
from jax import lax
from jax.experimental import pallas as pl
from jax.experimental.pallas import tpu as pltpu
from jax.sharding import PartitionSpec as P

HEADS = 12
HEAD_DIM = 64
ROT = 16
EPS = 1e-05
NEGATIVE = -1e30
BF = jnp.bfloat16
F32 = jnp.float32


def dot(spec, a, b):
    return jnp.einsum(spec, a, b, preferred_element_type=F32)


def frequencies():
    steps = jnp.arange(ROT // 2, dtype=F32)
    return jnp.power(F32(10000.0), -(2.0 * steps) / ROT)


def rotate(values, cosine, sine, sign):
    half = ROT // 2
    first = values[..., :half]
    second = values[..., half:ROT]
    turned_one = first * cosine - sign * second * sine
    turned_two = second * cosine + sign * first * sine
    return jnp.concatenate([turned_one, turned_two, values[..., ROT:]], axis=-1)


def place(row_lengths, index):
    ends = jnp.cumsum(row_lengths)
    after = (index[:, None] >= ends[None, :]).astype(jnp.int32)
    segment = jnp.sum(after, axis=1)
    start = jnp.sum(after * row_lengths[None, :], axis=1)
    return (segment, index - start)


def pick(values, index):
    return lax.dynamic_index_in_dim(values, index, 0, keepdims=False)


CHIP_SWAP = [(0, 2), (2, 0), (1, 3), (3, 1)]
CORE_SWAP = [(0, 1), (1, 0), (2, 3), (3, 2)]


def in_order(second, mine, other, axis=0):
    return jnp.stack([jnp.where(second, other, mine), jnp.where(second, mine, other)], axis=axis)


def seq_exchange(blocks):
    n = lax.axis_size("seq")
    if n != 4:
        return lax.all_to_all(blocks, "seq", 0, 0)
    me = lax.axis_index("seq")
    chip, core = me // 2, me % 2
    halves = blocks.reshape((2, 2) + blocks.shape[1:])
    far = lax.ppermute(pick(halves, 1 - chip), "seq", CHIP_SWAP)
    by_chip = in_order(chip == 1, pick(halves, chip), far, axis=1)
    other = lax.ppermute(pick(by_chip, 1 - core), "seq", CORE_SWAP)
    return in_order(core == 1, pick(by_chip, core), other, axis=1).reshape(blocks.shape)


def seq_gather(values):
    n = lax.axis_size("seq")
    if n != 4:
        return lax.all_gather(values, "seq", axis=0)
    me = lax.axis_index("seq")
    chip, core = me // 2, me % 2
    far = lax.ppermute(values, "seq", CHIP_SWAP)
    mine = in_order(chip == 1, values, far)
    other = lax.ppermute(mine, "seq", CORE_SWAP)
    return in_order(core == 1, mine, other, axis=1).reshape((n,) + values.shape)


def seq_reduce(values):
    n = lax.axis_size("seq")
    if n != 4:
        return lax.psum_scatter(values.astype(BF), "seq", scatter_dimension=0).astype(F32)
    me = lax.axis_index("seq")
    chip, core = me // 2, me % 2
    parts = values.reshape((2, 2) + values.shape[1:])
    keep = lax.dynamic_index_in_dim(parts, core, 1, keepdims=False)
    give = lax.dynamic_index_in_dim(parts, 1 - core, 1, keepdims=False).astype(BF)
    both = keep.astype(F32) + lax.ppermute(give, "seq", CORE_SWAP).astype(F32)
    far = lax.ppermute(pick(both, 1 - chip).astype(BF), "seq", CHIP_SWAP)
    return pick(both, chip) + far.astype(F32)


SIDE_SWAP = [(i, i ^ 1) for i in range(8)]


def along(step):
    return [(i, (i + 2 * step) % 8) for i in range(8)]


def dp_gather(block):
    n = lax.axis_size("dp")
    if n != 8:
        return lax.all_gather(block, "dp", axis=0)
    me = lax.axis_index("dp")
    line, side = me // 2, me % 2
    near1 = lax.ppermute(block, "dp", along(1))
    near3 = lax.ppermute(block, "dp", along(3))
    near2 = lax.ppermute(block, "dp", along(2))
    far0 = lax.ppermute(block, "dp", SIDE_SWAP)
    far13 = lax.ppermute(jnp.stack([near1, near3]), "dp", SIDE_SWAP)
    far2 = lax.ppermute(near2, "dp", SIDE_SWAP)
    full = jnp.zeros((4, 2) + block.shape, block.dtype)
    zero = jnp.int32(0)
    for step, near, far in ((0, block, far0), (1, near1, far13[0]), (3, near3, far13[1]), (2, near2, far2)):
        pair = in_order(side == 1, near, far)
        full = lax.dynamic_update_slice(full, pair[None], ((line - step) % 4, zero, zero, zero))
    return full.reshape((n,) + block.shape)


def dp_reduce(block_of):
    n = lax.axis_size("dp")
    if n != 8:
        blocks = jnp.stack([block_of(jnp.int32(i)).astype(BF) for i in range(n)])
        return lax.psum_scatter(blocks, "dp", scatter_dimension=0).astype(F32)
    me = lax.axis_index("dp")
    line, side = me // 2, me % 2

    def over_side(*steps):
        targets = [2 * ((line + step) % 4) for step in steps]
        moved = lax.ppermute(jnp.stack([block_of(t + 1 - side) for t in targets]), "dp", SIDE_SWAP)
        return [block_of(t + side).astype(F32) + moved[j].astype(F32) for j, t in enumerate(targets)]

    (sum2,) = over_side(2)
    sum1, sum3 = over_side(1, 3)
    (sum0,) = over_side(0)
    got2 = lax.ppermute(sum2.astype(BF), "dp", along(2)).astype(F32)
    got1 = lax.ppermute(sum1.astype(BF), "dp", along(1)).astype(F32)
    got3 = lax.ppermute(sum3.astype(BF), "dp", along(3)).astype(F32)
    return sum0 + got1 + got2 + got3


def attention(queries, keys, values, d_out, segment, scale):
    tokens = queries.shape[1]
    index = jnp.arange(tokens, dtype=jnp.int32)
    allowed = (segment[:, None] == segment[None, :]) & (index[None, :] <= index[:, None])
    scores = dot("htd,hnd->htn", queries, keys) * scale
    masked = jnp.where(allowed[None], scores, NEGATIVE)
    top = jnp.max(masked, axis=-1, keepdims=True)
    weights = jnp.where(allowed[None], jnp.exp(masked - top), 0.0)
    probs = weights / jnp.sum(weights, axis=-1, keepdims=True)
    probs_r = probs.astype(BF)
    attended = dot("htn,hnd->htd", probs_r, values)
    d_probs = dot("htd,hnd->htn", d_out, values)
    delta = jnp.sum(probs * d_probs, axis=-1, keepdims=True)
    d_scores = (probs * (d_probs - delta)).astype(BF)
    d_queries = dot("htn,hnd->htd", d_scores, keys) * scale
    d_keys = dot("htn,htd->hnd", d_scores, queries) * scale
    d_values = dot("htn,htd->hnd", probs_r, d_out)
    return attended, d_queries, d_keys, d_values


def general_device(
    hidden_in,
    lengths,
    grad_out,
    attn_gain,
    attn_shift,
    mlp_gain,
    mlp_shift,
    qkv_weight,
    qkv_bias,
    dense_weight,
    dense_bias,
    up_weight,
    up_bias,
    down_weight,
    down_bias,
):
    n_dp, n_seq = lax.axis_size("dp"), lax.axis_size("seq")
    me = lax.axis_index("seq")
    rows, width = hidden_in.shape
    group = rows * n_seq
    scale = HEAD_DIM ** (-0.5)
    hidden_units = up_weight.shape[1]
    own_units = hidden_units // n_seq
    deep = width // (n_dp * n_seq)
    unit_rows = hidden_units // (n_dp * n_seq)
    heads = -(-HEADS // n_seq)
    own = heads * HEAD_DIM
    spare = heads * n_seq - HEADS

    def by_head(values):
        lead = values.shape[:-1]
        split = values.reshape(lead + (3, HEADS, HEAD_DIM))
        if spare:
            split = jnp.pad(split, [(0, 0)] * (len(lead) + 1) + [(0, spare), (0, 0)])
        split = split.reshape(lead + (3, n_seq, own))
        return jnp.moveaxis(split, -2, 0).reshape((n_seq,) + lead + (3 * own,))

    def from_heads(blocks):
        lead = blocks.shape[1:-1]
        split = jnp.moveaxis(blocks.reshape((n_seq,) + lead + (3, own)), 0, -2)
        split = split.reshape(lead + (3, HEADS + spare, HEAD_DIM))[..., :HEADS, :]
        return split.reshape(lead + (3 * width,))

    vectors = (attn_gain, attn_shift, mlp_gain, mlp_shift, qkv_bias, dense_bias, up_bias, down_bias)
    sizes = [v.shape[0] for v in vectors]
    length = sum(sizes)
    wide = own_units + 3 * own
    up_blocks = jnp.moveaxis(up_weight.reshape(deep, n_dp, n_seq, unit_rows), 2, 0)
    up_blocks = up_blocks.reshape(n_seq, deep, own_units)
    vector = jnp.pad(jnp.concatenate(vectors), (0, wide - length))
    blocks = jnp.concatenate(
        [
            jnp.concatenate([up_blocks, by_head(qkv_weight)], axis=2),
            jnp.broadcast_to(vector, (n_seq, 1, wide)),
        ],
        axis=1,
    )
    got = seq_exchange(blocks)
    per_line = n_seq * deep
    up_rows = per_line * own_units // width
    up_piece = got[:, :deep, :own_units].reshape(up_rows, width)
    qkv_piece = got[:, :deep, own_units:].reshape(per_line, 3 * own)
    group_vector = got[:, deep, :length]

    both = seq_gather(jnp.concatenate([hidden_in, grad_out], axis=0))
    hidden_group = both[:, :rows].reshape(group, width)
    grad_group = both[:, rows:].reshape(group, width)

    def beside(values):
        lead = values.shape[:-2]
        split = values.reshape(lead + (deep, n_seq, width // n_seq))
        return jnp.swapaxes(split, -3, -2).reshape(lead + (per_line, width // n_seq))

    def from_beside(values):
        lead = values.shape[:-2]
        split = values.reshape(lead + (n_seq, deep, width // n_seq))
        return jnp.swapaxes(split, -3, -2).reshape(lead + (deep, width))

    attn_wide = 3 * own + width // n_seq
    vec_rows = -(-n_seq * length // attn_wide)
    vec_rows += -vec_rows % 8
    vec_piece = jnp.pad(group_vector.reshape(-1), (0, vec_rows * attn_wide - n_seq * length))
    attn_piece = jnp.concatenate([qkv_piece, beside(dense_weight)], axis=1)
    attn_piece = jnp.concatenate([attn_piece, vec_piece.reshape(vec_rows, attn_wide)], axis=0)
    attn_all = dp_gather(attn_piece)
    mlp_all = dp_gather(jnp.concatenate([up_piece, down_weight], axis=0))
    qkv_full = attn_all[:, :per_line, : 3 * own].reshape(width, 3 * own)
    dense_rows = from_beside(attn_all[:, :per_line, 3 * own :]).reshape(n_dp * deep, width)
    up_full = mlp_all[:, :up_rows].reshape(width, own_units)
    down_full = mlp_all[:, up_rows:].reshape(own_units, width)
    every = attn_all[:, per_line:].reshape(n_dp, vec_rows * attn_wide)[:, : n_seq * length]
    every = every.reshape(n_dp * n_seq, length).astype(F32)
    whole = []
    start = 0
    for size in sizes:
        whole.append(every[:, start : start + size].reshape(-1))
        start += size
    f_attn_gain, f_attn_shift, f_mlp_gain, f_mlp_shift, f_qkv_bias, f_dense_bias, f_up_bias, f_down_bias = whole
    own_qkv_bias = pick(by_head(f_qkv_bias), me)
    own_up_bias = lax.dynamic_index_in_dim(
        f_up_bias.reshape(n_dp, n_seq, unit_rows), me, 1, keepdims=False
    ).reshape(-1)

    row_lengths = lengths[0]
    index = jnp.arange(group, dtype=jnp.int32)
    segment, position = place(row_lengths, index)
    angles = position.astype(F32)[:, None] * frequencies()[None, :]
    cosine = jnp.cos(angles)[:, None, :]
    sine = jnp.sin(angles)[:, None, :]

    tokens = hidden_group.astype(F32)
    center = jnp.mean(tokens, axis=-1, keepdims=True)
    centered = tokens - center
    spread = jnp.mean(centered * centered, axis=-1, keepdims=True)
    unit = centered * lax.rsqrt(spread + EPS)
    attn_in = (unit * f_attn_gain + f_attn_shift).astype(BF)
    mlp_in = (unit * f_mlp_gain + f_mlp_shift).astype(BF)

    joined = dot("td,de->te", attn_in, qkv_full) + own_qkv_bias
    joined = joined.reshape(group, 3, heads, HEAD_DIM)
    queries = jnp.moveaxis(rotate(joined[:, 0], cosine, sine, 1.0).astype(BF), 1, 0)
    keys = jnp.moveaxis(rotate(joined[:, 1], cosine, sine, 1.0).astype(BF), 1, 0)
    values = jnp.moveaxis(joined[:, 2].astype(BF), 1, 0)
    feature_rows = n_dp * deep
    direct = spare == 0 and own % per_line == 0
    d_rows = dot("fe,te->ft", dense_rows, grad_group).astype(BF)
    if direct:
        runs = own // per_line
        moved = seq_exchange(d_rows.reshape(n_seq, runs * deep, group))
        moved = moved.reshape(n_seq, runs, deep, group)
        d_attended = jnp.moveaxis(moved, 0, 1).reshape(heads, HEAD_DIM, group)
    else:
        moved = lax.all_gather(d_rows.reshape(n_dp, deep, group), "seq", axis=1)
        moved = moved.reshape(width, group)
        moved = jnp.pad(moved, ((0, spare * HEAD_DIM), (0, 0)))
        d_attended = pick(moved.reshape(n_seq, heads, HEAD_DIM, group), me)
    d_attended = jnp.swapaxes(d_attended, 1, 2)
    attended, d_queries, d_keys, d_values = attention(queries, keys, values, d_attended, segment, scale)
    attended = jnp.swapaxes(attended.astype(BF), 1, 2).reshape(own, group)
    if direct:
        given = jnp.moveaxis(attended.reshape(runs, n_seq, deep, group), 1, 0)
        rows_attended = seq_exchange(given.reshape(n_seq, runs * deep, group)).reshape(feature_rows, group)
    else:
        given = lax.all_gather(attended, "seq", axis=0, tiled=True)[:width]
        rows_attended = lax.dynamic_index_in_dim(
            given.reshape(n_dp, n_seq, deep, group), me, 1, keepdims=False
        ).reshape(feature_rows, group)
    attn_out = dot("ft,fe->te", rows_attended, dense_rows)
    dense_grad = dot("ft,te->fe", rows_attended, grad_group).astype(BF).reshape(n_dp, deep, width)
    d_queries = rotate(jnp.moveaxis(d_queries, 0, 1), cosine, sine, -1.0)
    d_keys = rotate(jnp.moveaxis(d_keys, 0, 1), cosine, sine, -1.0)
    d_joined = jnp.stack([d_queries, d_keys, jnp.moveaxis(d_values, 0, 1)], axis=1)
    d_joined = d_joined.astype(BF).reshape(group, 3 * own)
    qkv_grad = dot("td,te->de", attn_in, d_joined).astype(BF).reshape(n_dp, n_seq * deep, 3 * own)
    d_attn_in = dot("te,de->td", d_joined, qkv_full)
    attn_terms = jnp.concatenate([qkv_grad, beside(dense_grad)], axis=2)
    attn_sum = dp_reduce(lambda i: pick(attn_terms, i))

    upper = dot("td,df->tf", mlp_in, up_full) + own_up_bias
    cdf = 0.5 * (1.0 + lax.erf(upper * F32(0.7071067811865476)))
    pdf = jnp.exp(-0.5 * upper * upper) * F32(0.3989422804014327)
    act = (upper * cdf).astype(BF)
    d_act = dot("td,fd->tf", grad_group, down_full)
    d_up = (d_act * (cdf + upper * pdf)).astype(BF)
    down_grad = dot("tf,td->fd", act, grad_group).astype(BF).reshape(n_dp, unit_rows, width)
    up_grad = dot("td,tf->df", mlp_in, d_up).astype(BF).reshape(n_dp, up_rows, width)
    mlp_out = dot("tf,fd->td", act, down_full)
    d_mlp_in = dot("tf,df->td", d_up, up_full)

    mine = jnp.arange(n_seq) == me
    qkv_bias_grad = jnp.sum(d_joined.astype(F32), axis=0)
    qkv_bias_grad = from_heads(jnp.where(mine[:, None], qkv_bias_grad[None], 0.0))
    up_bias_grad = jnp.sum(d_up.astype(F32), axis=0).reshape(n_dp, 1, unit_rows)
    up_bias_grad = jnp.where(mine[None, :, None], up_bias_grad, 0.0)
    bias_sum = jnp.sum(grad_out.astype(F32), axis=0)
    terms = (
        jnp.sum(d_attn_in * unit, axis=0),
        jnp.sum(d_attn_in, axis=0),
        jnp.sum(d_mlp_in * unit, axis=0),
        jnp.sum(d_mlp_in, axis=0),
        qkv_bias_grad,
        bias_sum,
        up_bias_grad,
        bias_sum,
    )
    terms = [t.reshape(n_dp, n_seq, size) for t, size in zip(terms, sizes)]
    terms = jnp.concatenate(terms, axis=2).reshape(n_dp, n_seq * length)
    tail_rows = -(-n_seq * length // width)
    tail_rows += -tail_rows % 8
    terms = jnp.pad(terms, ((0, 0), (0, tail_rows * width - n_seq * length)))
    terms = terms.reshape(n_dp, tail_rows, width).astype(BF)
    mlp_sum = dp_reduce(lambda i: jnp.concatenate([pick(up_grad, i), pick(down_grad, i), pick(terms, i)], axis=0))

    upstream = d_attn_in * f_attn_gain + d_mlp_in * f_mlp_gain
    pair = jnp.concatenate([(attn_out + mlp_out).astype(BF), upstream.astype(BF)], axis=1)
    pair = seq_reduce(pair.reshape(n_seq, rows, 2 * width))
    block_out = hidden_in.astype(F32) + f_dense_bias + f_down_bias + pair[:, :width]
    upstream = pair[:, width:]
    x = hidden_in.astype(F32)
    centered = x - jnp.mean(x, axis=-1, keepdims=True)
    inverse = lax.rsqrt(jnp.mean(centered * centered, axis=-1, keepdims=True) + EPS)
    own_unit = centered * inverse
    inner = (
        upstream
        - jnp.mean(upstream, axis=-1, keepdims=True)
        - own_unit * jnp.mean(upstream * own_unit, axis=-1, keepdims=True)
    )
    grad_in = grad_out.astype(F32) + inverse * inner

    qkv_back = attn_sum[:, : 3 * own].reshape(n_seq, deep, 3 * own).astype(BF)
    qkv_own = from_heads(seq_exchange(qkv_back).astype(F32))
    dense_own = from_beside(attn_sum[:, 3 * own :])
    vec_sum = mlp_sum[up_rows + unit_rows :].reshape(-1)[: n_seq * length].reshape(n_seq, 1, length)
    vec_sum = jnp.pad(vec_sum, ((0, 0), (0, 0), (0, -length % own_units)))
    vec_sum = vec_sum.reshape(n_seq, -1, own_units)
    back = jnp.concatenate([mlp_sum[:up_rows].reshape(n_seq, deep, own_units), vec_sum], axis=1)
    back = seq_exchange(back.astype(BF)).astype(F32)
    up_own = jnp.moveaxis(back[:, :deep].reshape(n_seq, deep, n_dp, unit_rows), 0, 2)
    vec_own = jnp.sum(back[:, deep:].reshape(n_seq, -1), axis=0)
    owned = []
    start = 0
    for size in sizes:
        owned.append(vec_own[start : start + size])
        start += size
    return (
        block_out.astype(BF),
        grad_in.astype(BF),
        owned[0],
        owned[1],
        owned[2],
        owned[3],
        qkv_own,
        owned[4],
        dense_own,
        owned[5],
        up_own.reshape(deep, hidden_units),
        owned[6],
        mlp_sum[up_rows : up_rows + unit_rows],
        owned[7],
    )


SCALE = HEAD_DIM**-0.5


def kernel_call(body, outs, args, scratch=(), megabytes=24, flops=0, apart=0):
    moved = sum(a.size * a.dtype.itemsize for a in args)
    held = [pl.BlockSpec(memory_space=pl.ANY)] * apart
    held += [pl.BlockSpec(memory_space=pltpu.VMEM)] * (len(args) - apart)
    return pl.pallas_call(
        body,
        out_shape=tuple(jax.ShapeDtypeStruct(shape, kind) for shape, kind in outs),
        in_specs=held,
        scratch_shapes=[pltpu.VMEM(*item) if isinstance(item, tuple) else item for item in scratch],
        compiler_params=pltpu.CompilerParams(vmem_limit_bytes=megabytes << 20),
        cost_estimate=pl.CostEstimate(flops=flops, bytes_accessed=moved, transcendentals=0),
    )(*args)


def dot_nn(a, b):
    return lax.dot_general(a, b, (((1,), (0,)), ((), ())), preferred_element_type=F32)


def dot_nt(a, b):
    return lax.dot_general(a, b, (((1,), (1,)), ((), ())), preferred_element_type=F32)


def dot_tn(a, b):
    return lax.dot_general(a, b, (((0,), (0,)), ((), ())), preferred_element_type=F32)


def line_and_side():
    me = lax.axis_index("dp")
    return lax.shift_right_logical(me, 1), lax.bitwise_and(me, 1)


PAIR_SWAP = [(i, i ^ 2) for i in range(8)]
HALF_SWAP = [(i, i ^ 4) for i in range(8)]
LINE_ORDER = (0, 2, 1, 3)


def dp_index(line, step, side):
    return 2 * lax.bitwise_xor(line, step) + side


def pick_blocks(block_of, send, keep):
    line, side = line_and_side()
    for j, step in enumerate(LINE_ORDER):
        send[j] = block_of(dp_index(line, step, 1 - side))
        keep[j] = block_of(dp_index(line, step, side))


def add_kernel(here, there, *out):
    place = 0
    for ref in out:
        for j in range(ref.shape[0]):
            ref[j] = (here[place + j].astype(F32) + there[place + j].astype(F32)).astype(ref.dtype)
        place += ref.shape[0]


def add_blocks(here, there, *counts, waits=()):
    shape = here.shape[1:]
    return kernel_call(
        with_waits(len(waits), add_kernel),
        tuple(((count,) + shape, BF) for count in counts),
        (*waits, here, there),
        megabytes=8,
        apart=len(waits),
    )


def once(values, *others):
    return lax.optimization_barrier((values, *others))[0]


def seq_shuffle(blocks):
    got = [blocks[0]]
    for other in (1, 2, 3):
        pairs = [(i, i ^ other) for i in range(4)]
        got.append(lax.ppermute(blocks[other], "seq", pairs))
    return got


def place_kernel(deep, *refs):
    pieces, (dy, weights, dense, vectors), d_blocks, (rows32, d_rows) = refs[:4], refs[4:8], refs[8:12], refs[12:]
    line, side = line_and_side()
    per_line = 4 * deep
    quarter = dy.shape[1] // 4
    own = weights.shape[1] - quarter
    total = jnp.zeros(vectors.shape, F32)
    for place in range(8):
        piece = pieces[place // 2].at[place % 2]
        owner = dp_index(line, LINE_ORDER[place % 4], side if place < 4 else 1 - side)
        weights[pl.ds(pl.multiple_of(owner * per_line, per_line), per_line), :] = piece[:per_line, :]
        total = total + piece[per_line:, :].astype(F32)
        beside = piece[:per_line, own:].astype(F32)
        for q in range(4):
            rows32[pl.ds(pl.multiple_of(owner * deep, 8), deep), q * quarter : (q + 1) * quarter] = beside[
                q * deep : (q + 1) * deep
            ]
    vectors[...] = total
    dense[...] = rows32[...].astype(BF)
    d_rows[...] = dot_nt(dense[...], dy[...]).astype(BF)
    me = lax.axis_index("seq")
    count = d_blocks[0].shape[0]
    for j in range(4):
        d_blocks[j][...] = d_rows[pl.ds(pl.multiple_of(lax.bitwise_xor(me, j) * count, 16), count), :]


def turn(values, cosine, sine_a, sine_b, sign):
    half = ROT // 2
    ahead = pltpu.roll(values, 128 - half, 1)
    behind = pltpu.roll(values, half, 1)
    return values * cosine + sign * (ahead * sine_a + behind * sine_b)


def project_kernel(unit, weights, vectors, cosine, sine_a, sine_b, attn_in, qk, v):
    gain, shift, bias = vectors[0:1, :], vectors[1:2, :], vectors[6:7, :]
    turned = qk.shape[1]
    size = 128

    def step(i, carry):
        rows = pl.ds(pl.multiple_of(i * size, size), size)
        normed = (unit[rows, :] * gain + shift).astype(BF)
        attn_in[rows, :] = normed
        joined = dot_nn(normed, weights[...]) + bias
        tables = cosine[rows, :], sine_a[rows, :], sine_b[rows, :]
        for c in range(0, turned, 128):
            qk[rows, c : c + 128] = turn(joined[:, c : c + 128], *tables, 1.0).astype(BF)
        v[rows, :] = joined[:, turned : turned + v.shape[1]].astype(BF)
        return carry

    lax.fori_loop(0, unit.shape[0] // size, step, 0)


def attention_kernel(deep, *refs):
    qk, v, d0, d1, d2, d3, seg_column, seg_row, cosine, sine_a, sine_b = refs[:11]
    given, d_joined, (d_t, out_t, dk_t, dv_t, acc) = refs[11:15], refs[15], refs[16:]
    tokens, own = v.shape
    me = lax.axis_index("seq")
    runs = own // (4 * deep)
    for j, ref in enumerate((d0, d1, d2, d3)):
        source = lax.bitwise_xor(me, j)
        block = ref[...].astype(F32)
        for r in range(runs):
            place = pl.multiple_of(r * 4 * deep + source * deep, 8)
            d_t[pl.ds(place, deep), :] = block[r * deep : (r + 1) * deep]
    d_out = jnp.transpose(d_t[...]).astype(BF)
    q_t = jnp.transpose(qk[:, :own].astype(F32)).astype(BF)
    d_tb = d_t[...].astype(BF)
    dk_t[...] = jnp.zeros(dk_t.shape, F32)
    dv_t[...] = jnp.zeros(dv_t.shape, F32)
    size = 256
    for h in range(own // HEAD_DIM):
        lanes = slice(h * HEAD_DIM, (h + 1) * HEAD_DIM)
        q_h = qk[:, lanes]
        k_h = qk[:, own + h * HEAD_DIM : own + (h + 1) * HEAD_DIM]
        v_h = v[:, lanes]
        d_h = d_out[:, lanes]
        for first in range(0, tokens, size):
            rows = slice(first, first + size)
            n = first + size
            scores = dot_nt(q_h[rows], k_h[:n]) * SCALE
            query = lax.broadcasted_iota(jnp.int32, (size, n), 0) + first
            key = lax.broadcasted_iota(jnp.int32, (size, n), 1)
            allowed = (seg_column[rows, :] == seg_row[:, :n]) & (key <= query)
            scores = jnp.where(allowed, scores, NEGATIVE)
            weights = jnp.where(allowed, jnp.exp(scores - jnp.max(scores, axis=1, keepdims=True)), 0.0)
            probs = weights * (1.0 / jnp.sum(weights, axis=1, keepdims=True))
            probs_r = probs.astype(BF)
            out_t[lanes, rows] = jnp.transpose(dot_nn(probs_r, v_h[:n]))
            d_probs = dot_nt(d_h[rows], v_h[:n])
            delta = jnp.sum(probs * d_probs, axis=1, keepdims=True)
            d_scores = (probs * (d_probs - delta)).astype(BF)
            acc[rows, lanes] = dot_nn(d_scores, k_h[:n]) * SCALE
            dk_t[lanes, :n] += dot_nn(q_t[lanes, rows], d_scores)
            dv_t[lanes, :n] += dot_nn(d_tb[lanes, rows], probs_r)
    acc[:, own : 2 * own] = jnp.transpose(dk_t[...]) * SCALE
    for c in range(0, 2 * own, 128):
        turned = turn(acc[:, c : c + 128], cosine[...], sine_a[...], sine_b[...], -1.0)
        d_joined[:, c : c + 128] = turned.astype(BF)
    d_joined[:, 2 * own : 3 * own] = jnp.transpose(dv_t[...]).astype(BF)
    d_joined[:, 3 * own :] = jnp.zeros((tokens, d_joined.shape[1] - 3 * own), BF)
    for j in range(4):
        target = lax.bitwise_xor(me, j)
        parts = [out_t[pl.ds(pl.multiple_of(r * 4 * deep + target * deep, 8), deep), :] for r in range(runs)]
        given[j][...] = jnp.concatenate(parts, axis=0).astype(BF)


def attention_grads_kernel(deep, *refs):
    r0, r1, r2, r3, dense, dy, attn_in, d_joined, weights, unit, vectors, own_pair = refs[:12]
    picks, (give, keep), (rows_t, grads, sums) = refs[12:14], refs[14:16], refs[16:]
    me = lax.axis_index("seq")
    core = lax.bitwise_and(me, 1)
    count = r0.shape[0]
    width = dy.shape[1]
    quarter = width // 4
    own = width - quarter
    for j, ref in enumerate((r0, r1, r2, r3)):
        rows_t[pl.ds(pl.multiple_of(lax.bitwise_xor(me, j) * count, 16), count), :] = ref[...]
    attended = jnp.transpose(rows_t[...].astype(F32)).astype(BF)
    gain = vectors[0:1, :]
    size = dy.shape[0] // 4
    sums[...] = jnp.zeros(sums.shape, F32)
    for i in range(4):
        rows = slice(i * size, (i + 1) * size)
        out = dot_nn(attended[rows], dense[...]) + own_pair[i, :, :width].astype(F32)
        back = dot_nt(d_joined[rows, :], weights[...])
        sums[0:1, :] += jnp.sum(back * unit[rows, :], axis=0, keepdims=True)
        sums[1:2, :] += jnp.sum(back, axis=0, keepdims=True)
        sums[5:6, :] += jnp.sum(d_joined[rows, :].astype(F32), axis=0, keepdims=True)
        out = out.astype(BF)
        back = (back * gain + own_pair[i, :, width:].astype(F32)).astype(BF)

        @pl.when(core == i % 2)
        def _():
            keep[i // 2, :, :width] = out
            keep[i // 2, :, width:] = back

        @pl.when(core != i % 2)
        def _():
            give[i // 2, :, :width] = out
            give[i // 2, :, width:] = back

    for c in range(0, width, 128):
        grads[c : c + 128, :] = dot_tn(attn_in[:, c : c + 128], d_joined[...])
    dense_grad = dot_nn(rows_t[...], dy[...])
    for p in range(8):
        for q in range(4):
            start = p * 4 * deep + q * deep
            grads[start : start + deep, own:] = dense_grad[p * deep : (p + 1) * deep, q * quarter : (q + 1) * quarter]
    per_line = 4 * deep
    tail = sums[...]

    def block_of(index):
        block = grads[pl.ds(pl.multiple_of(index * per_line, per_line), per_line), :]
        return jnp.concatenate([block, tail], axis=0).astype(BF)

    pick_blocks(block_of, *picks)


def pack_kernel(deep, *refs):
    qkv, up, by_width, qkv_bias, x, dy, blocks, mine, (all_blocks, row_block) = *refs[:6], refs[6:10], *refs[10:11], refs[11:]
    width = qkv.shape[1] // 3
    own = width // 4
    units = up.shape[1] // 32
    me = lax.axis_index("seq")
    device = 4 * lax.axis_index("dp") + me
    row_block[...] = jnp.zeros(row_block.shape, F32)
    row_block[:6, :deep] = by_width[...].astype(F32)
    vectors = pltpu.roll(row_block[:, :width], device * deep, 1)
    row_block[0:6, :] = jnp.zeros((6, row_block.shape[1]), F32)
    row_block[6:7, : 3 * deep] = qkv_bias[...].astype(F32)
    bias_rows = pltpu.roll(row_block[...], device * (3 * deep), 1)
    up_values, qkv_values = up[...].astype(F32), qkv[...].astype(F32)
    empty = jnp.zeros((deep + 8, own), F32)
    both = jnp.concatenate([qkv_values, bias_rows], axis=0)
    for t in range(4):
        parts = [up_values[:, ((l * 2 + y) * 4 + t) * units :][:, :units] for y in range(2) for l in range(4)]
        all_blocks[t, :deep, :] = jnp.concatenate(parts, axis=1)
        parts = [both[:, part * width + t * own : part * width + (t + 1) * own] for part in range(3)]
        parts = jnp.concatenate(parts + [empty], axis=1)
        all_blocks[t, deep : 2 * deep, :] = parts[:deep]
        all_blocks[t, 2 * deep :, :] = parts[deep:] + vectors
    rows = x.shape[0]
    for j in range(4):
        blocks[j][...] = all_blocks[lax.bitwise_xor(me, j)].astype(BF)
    mine[:rows, :] = x[...]
    mine[rows:, :] = dy[...]


def unpack_kernel(deep, r0, r1, r2, r3, dense, up_bias, attn_piece, up_keep, up_give, up32, qkv32, row_block):
    me = lax.axis_index("seq")
    line, side = line_and_side()
    width = dense.shape[1]
    quarter = width // 4
    half = up_keep.shape[1]
    own = 3 * quarter
    extra = jnp.zeros((8, width), F32)
    for j, ref in enumerate((r0, r1, r2, r3)):
        block = ref[...].astype(F32)
        place = pl.ds(pl.multiple_of(lax.bitwise_xor(me, j) * deep, 8), deep)
        up32[place, :] = block[:deep]
        qkv32[place, :] = block[deep : 2 * deep]
        extra = extra + block[2 * deep :]
    rows = 4 * deep
    first, second = up32[:, :half], up32[:, half:]
    up_keep[...] = jnp.where(side == 0, first, second).astype(BF)
    up_give[...] = jnp.where(side == 0, second, first).astype(BF)
    attn_piece[:rows, :own] = qkv32[:, :own].astype(BF)
    dense_values = dense[...].astype(F32)
    beside = [dense_values[:, q * quarter : (q + 1) * quarter] for q in range(4)]
    attn_piece[:rows, own:] = jnp.concatenate(beside, axis=0).astype(BF)
    units = half // 4
    row_block[...] = jnp.zeros(row_block.shape, F32)
    row_block[7:8, :units] = up_bias[...].astype(F32)
    attn_piece[rows:, :] = (extra + pltpu.roll(row_block[...], side * half + line * units, 1)).astype(BF)


def mlp_tokens(unit, dy, vectors, up, down, mlp_in, act, d_up, sums, side, store):
    half = up.shape[1]
    gain, shift = vectors[2:3, :], vectors[3:4, :]
    bias = jnp.where(side == 0, vectors[7:8, :half], vectors[7:8, half:])
    sums[...] = jnp.zeros(sums.shape, F32)
    size = unit.shape[0] // 4

    def step(i, carry):
        rows = pl.ds(pl.multiple_of(i * size, size), size)
        u = unit[rows, :]
        normed = (u * gain + shift).astype(BF)
        mlp_in[rows, :] = normed
        upper = dot_nn(normed, up[...]) + bias
        cdf = 0.5 * (1.0 + lax.erf(upper * 0.7071067811865476))
        pdf = jnp.exp(-0.5 * upper * upper) * 0.3989422804014327
        act_rows = (upper * cdf).astype(BF)
        act[rows, :] = act_rows
        d_rows = (dot_nt(dy[rows, :], down[...]) * (cdf + upper * pdf)).astype(BF)
        d_up[rows, :] = d_rows
        out = dot_nn(act_rows, down[...]).astype(BF)
        back = dot_nt(d_rows, up[...])
        sums[2:3, :] += jnp.sum(back * u, axis=0, keepdims=True)
        sums[3:4, :] += jnp.sum(back, axis=0, keepdims=True)
        sums[6:7, :half] += jnp.sum(d_rows.astype(F32), axis=0, keepdims=True)
        store(i, out, (back * gain).astype(BF))
        return carry

    lax.fori_loop(0, 4, step, 0)


def mlp_kernel(*refs):
    pieces, (unit, dy, vectors) = refs[:4], refs[4:7]
    give, keep, mlp_in, act, d_up, sums, up, down, done = refs[7:]
    line, side = line_and_side()
    width, half = up.shape
    units = half // 4
    copies = []
    for place, step in enumerate(LINE_ORDER):
        low, high = [pieces[k + place // 2].at[place % 2] for k in (0, 2)]
        l = lax.bitwise_xor(line, step)
        for source, target in (
            (low, down.at[pl.ds(pl.multiple_of(l * units, 32), units), :]),
            (high.at[:, pl.ds(0, half)], up.at[pl.ds(pl.multiple_of(2 * l * units, 32), units), :]),
            (high.at[:, pl.ds(half, half)], up.at[pl.ds(pl.multiple_of((2 * l + 1) * units, 32), units), :]),
        ):
            copies.append(pltpu.make_async_copy(source, target, done.at[len(copies)]))
    for copy in copies:
        copy.start()
    core = lax.bitwise_and(lax.axis_index("seq"), 1)
    for copy in copies:
        copy.wait()

    def store(i, out, back):
        place = lax.shift_right_logical(i, 1)

        @pl.when(lax.bitwise_and(i, 1) == core)
        def _():
            keep[place, :, :width] = out
            keep[place, :, width:] = back

        @pl.when(lax.bitwise_and(i, 1) != core)
        def _():
            give[place, :, :width] = out
            give[place, :, width:] = back

    mlp_tokens(unit, dy, vectors, up, down, mlp_in, act, d_up, sums, side, store)


def mlp_own_kernel(unit, dy, vectors, up, down, own_pair, mlp_in, act, d_up, sums):
    _, side = line_and_side()
    width = up.shape[0]

    def store(i, out, back):
        own_pair[i, :, :width] = out
        own_pair[i, :, width:] = back

    mlp_tokens(unit, dy, vectors, up, down, mlp_in, act, d_up, sums, side, store)
    sums[4:5, :] = 0.25 * jnp.sum(dy[...].astype(F32), axis=0, keepdims=True)


def mlp_grads_kernel(*refs):
    own, other = refs[:5], refs[5:10]
    keep_up, send_up, keep_down, send_down, up_grad, down_grad = refs[10:]
    line, _ = line_and_side()
    half, width = down_grad.shape
    units = half // 4
    for c in range(0, width, 128):
        total = sum(dot_tn(mlp_in[:, c : c + 128], d_up[...]) for mlp_in, _, d_up, _, _ in (own, other))
        up_grad[c : c + 128, :] = total.astype(BF)
    for c in range(0, half, 128):
        total = sum(dot_tn(act[:, c : c + 128], dy[...]) for _, act, _, dy, _ in (own, other))
        down_grad[c : c + 128, :] = total.astype(BF)
    tail = (own[4][...] + other[4][...]).astype(BF)
    for place, step in enumerate(LINE_ORDER):
        ups, downs = ((keep_up, keep_down), (send_up, send_down))[place // 2]
        l = lax.bitwise_xor(line, step)
        downs[place % 2] = down_grad[pl.ds(pl.multiple_of(l * units, 32), units), :]
        ref = ups.at[place % 2]
        ref[:units, :half] = up_grad[pl.ds(pl.multiple_of(2 * l * units, 32), units), :]
        ref[:units, half:] = up_grad[pl.ds(pl.multiple_of((2 * l + 1) * units, 32), units), :]
        ref[units:, :] = tail


def up_sum_kernel(own, far, up_keep, up_give, tail):
    units, half = up_keep.shape
    width = 2 * half
    _, side = line_and_side()

    def total(rows, lanes):
        return own[0, rows, lanes].astype(F32) + far[0, rows, lanes].astype(F32)

    first, second = total(slice(0, units), slice(0, half)), total(slice(0, units), slice(half, width))
    last = total(slice(units, units + 8), slice(None))
    tail[...] = last
    up_keep[...] = jnp.where(side == 0, first, second).astype(BF)
    up_give[:units, :] = jnp.where(side == 0, second, first).astype(BF)
    up_give[units:, :] = jnp.concatenate([last[:, :half], last[:, half:]], axis=0).astype(BF)


def owners_kernel(deep, keep, far, tail, b0, b1, b2, b3, rows32):
    _, side = line_and_side()
    me = lax.axis_index("seq")
    rows, half = keep.shape
    here, there = keep[...].astype(F32), far[:rows, :].astype(F32)
    rows32[:, :half] = jnp.where(side == 0, here, there)
    rows32[:, half:] = jnp.where(side == 0, there, here)
    far_tail = far[rows:, :].astype(F32)
    last = tail[...] + jnp.concatenate([far_tail[:8], far_tail[8:]], axis=1)
    for j, ref in enumerate((b0, b1, b2, b3)):
        target = lax.bitwise_xor(me, j)
        block = rows32[pl.ds(pl.multiple_of(target * deep, 8), deep), :]
        ref[...] = jnp.concatenate([block, last], axis=0).astype(BF)


def owned_kernel(deep, b0, b1, b2, b3, tail, up_own, vec_own, sources):
    line, _ = line_and_side()
    me = lax.axis_index("seq")
    device = 4 * lax.axis_index("dp") + me
    width = tail.shape[1]
    half = width // 2
    units = half // 4
    for j, ref in enumerate((b0, b1, b2, b3)):
        sources[lax.bitwise_xor(me, j)] = ref[...].astype(F32)
    for l in range(4):
        parts = [
            sources[t, :deep, y * half + l * units : y * half + (l + 1) * units] for y in range(2) for t in range(4)
        ]
        up_own[:, l * 2 * half : (l + 1) * 2 * half] = jnp.concatenate(parts, axis=1)
    total = sources[0, deep:] + sources[1, deep:] + sources[2, deep:] + sources[3, deep:]
    rolled = pltpu.roll(total, width - device * deep, 1)
    vec_own[...] = rolled[:, :128]
    rolled = pltpu.roll(tail[...], width - line * units, 1)
    vec_own[6:7, :] = rolled[6:7, :128]


def attention_sum_kernel(deep, own, far, b0, b1, b2, b3, dense_own, total):
    me = lax.axis_index("seq")
    total[...] = own[0].astype(F32) + far[0].astype(F32)
    quarter = total.shape[1] // 4
    last = total[4 * deep :, :]
    for q in range(4):
        dense_own[:, q * quarter : (q + 1) * quarter] = total[q * deep : (q + 1) * deep, 3 * quarter :]
    for j, ref in enumerate((b0, b1, b2, b3)):
        target = lax.bitwise_xor(me, j)
        block = total[pl.ds(pl.multiple_of(target * deep, 8), deep), :]
        ref[...] = jnp.concatenate([block, last], axis=0).astype(BF)


def attention_owned_kernel(deep, b0, b1, b2, b3, qkv_own, vec_own, sources, row_block):
    me = lax.axis_index("seq")
    device = 4 * lax.axis_index("dp") + me
    width = b0.shape[1]
    own = width // 4
    for j, ref in enumerate((b0, b1, b2, b3)):
        sources[lax.bitwise_xor(me, j)] = ref[...].astype(F32)
    total = sources[0, deep:] + sources[1, deep:] + sources[2, deep:] + sources[3, deep:]
    vec_own[...] = pltpu.roll(total, width - device * deep, 1)[:, :128]
    row_block[...] = jnp.zeros(row_block.shape, F32)
    for part in range(3):
        lanes = slice(part * own, (part + 1) * own)
        whole = jnp.concatenate([sources[t, :, lanes] for t in range(4)], axis=1)
        qkv_own[:, part * width : (part + 1) * width] = whole[:deep]
        row_block[5:6, part * width : (part + 1) * width] = whole[deep + 5 : deep + 6]
    rolled = pltpu.roll(row_block[...], 3 * width - device * (3 * deep), 1)
    vec_own[5:6, :] = rolled[5:6, :128]


def with_waits(count, body):
    def wrapped(*refs):
        body(*refs[count:])

    return wrapped


def line_device(
    hidden_in,
    lengths,
    grad_out,
    attn_gain,
    attn_shift,
    mlp_gain,
    mlp_shift,
    qkv_weight,
    qkv_bias,
    dense_weight,
    dense_bias,
    up_weight,
    up_bias,
    down_weight,
    down_bias,
):
    n_dp, n_seq = 8, 4
    dp_me, me = lax.axis_index("dp"), lax.axis_index("seq")
    line, side = lax.shift_right_logical(dp_me, 1), lax.bitwise_and(dp_me, 1)
    chip, core = lax.shift_right_logical(me, 1), lax.bitwise_and(me, 1)
    device = dp_me * n_seq + me
    zero = jnp.int32(0)
    rows, width = hidden_in.shape
    group = rows * n_seq
    hidden_units = up_weight.shape[1]
    units = hidden_units // (n_dp * n_seq)
    half = hidden_units // 8
    deep = width // (n_dp * n_seq)
    per_line = n_seq * deep
    own = width // n_seq
    wide = 2 * half + 3 * own
    flat = (group, width)

    by_width = jnp.stack([attn_gain, attn_shift, mlp_gain, mlp_shift, dense_bias, down_bias])
    *blocks, mine = kernel_call(
        functools.partial(pack_kernel, deep),
        (((2 * deep + 8, width), BF),) * 4 + (((2 * rows, width), BF),),
        (qkv_weight, up_weight, by_width, qkv_bias[None], hidden_in, grad_out),
        scratch=(((4, 2 * deep + 8, width), F32), ((8, 3 * width), F32)),
        megabytes=16,
    )
    attn_piece, up_keep, up_give = kernel_call(
        functools.partial(unpack_kernel, deep),
        (((per_line + 8, width), BF), ((per_line, half), BF), ((per_line, half), BF)),
        (*seq_shuffle(blocks), dense_weight, up_bias[None]),
        scratch=(((per_line, width), F32), ((per_line, width), F32), ((8, width), F32)),
        megabytes=16,
    )

    across = lax.ppermute(mine, "dp", SIDE_SWAP)
    down_half = lax.ppermute(down_weight, "dp", HALF_SWAP)
    attn_piece, up_keep, up_give = once(attn_piece, down_half), up_keep, once(up_give, down_half)
    down_two = jnp.stack([down_weight, down_half])
    down_pair = lax.ppermute(down_two, "dp", PAIR_SWAP)
    attn_half = lax.ppermute(attn_piece, "dp", HALF_SWAP)
    up_far = lax.ppermute(up_give, "dp", SIDE_SWAP)
    chip_far = lax.ppermute(once(mine, up_keep), "seq", CHIP_SWAP)

    attn_two = once(jnp.stack([attn_piece, attn_half]), up_far)
    attn_pair = lax.ppermute(attn_two, "dp", PAIR_SWAP)
    attn_side = lax.ppermute(attn_two, "dp", SIDE_SWAP)
    up_both = jnp.concatenate(
        [jnp.where(side == 0, up_keep, up_far), jnp.where(side == 0, up_far, up_keep)], axis=1
    )
    mlp_piece = once(up_both, attn_half)
    mlp_half = lax.ppermute(mlp_piece, "dp", HALF_SWAP)
    by_chip = once(in_order(chip == 1, mine, chip_far), attn_half, up_far)
    core_far = lax.ppermute(by_chip, "seq", CORE_SWAP)

    attn_far = lax.ppermute(once(attn_pair, mlp_half), "dp", SIDE_SWAP)
    mlp_two = once(jnp.stack([mlp_piece, mlp_half]), attn_pair, down_pair)
    mlp_pair = lax.ppermute(mlp_two, "dp", PAIR_SWAP)
    chip_beyond = lax.ppermute(once(across, mlp_half, attn_pair, attn_side), "seq", CHIP_SWAP)

    def whole_group(values, over):
        full = in_order(core == 1, values, over, axis=1).reshape(n_seq, 2, rows, width)
        return full[:, 0].reshape(flat), full[:, 1].reshape(flat)

    hidden_group, dy = whole_group(by_chip, core_far)
    attn_pieces = (attn_two, attn_pair, attn_side, attn_far)

    row_lengths = lengths[0]
    segment, position = place(row_lengths, jnp.arange(group, dtype=jnp.int32))
    lane = jnp.arange(128, dtype=jnp.int32) % HEAD_DIM
    powers = jnp.power(F32(10000.0), -(2.0 * (lane % (ROT // 2)).astype(F32)) / ROT)
    angles = position.astype(F32)[:, None] * powers[None, :]
    cosine = jnp.where(lane < ROT, jnp.cos(angles), 1.0)
    sine = jnp.sin(angles)
    sine_a = jnp.where(lane < ROT // 2, -sine, 0.0)
    sine_b = jnp.where((lane >= ROT // 2) & (lane < ROT), sine, 0.0)

    def normed(values):
        centered = values - jnp.mean(values, axis=-1, keepdims=True)
        inverse = lax.rsqrt(jnp.mean(centered * centered, axis=-1, keepdims=True) + EPS)
        return centered * inverse, inverse

    unit = normed(hidden_group.astype(F32))[0]

    placed = kernel_call(
        with_waits(1, functools.partial(place_kernel, deep)),
        ((flat[1:] * 2, BF), ((n_dp * deep, width), BF), ((8, width), F32)) + (((2 * deep, group), BF),) * 4,
        (mlp_pair,) + attn_pieces + (dy,),
        scratch=(((n_dp * deep, width), F32), ((n_dp * deep, group), BF)),
        flops=2 * n_dp * deep * width * group,
        apart=1,
    )
    weights, dense, vectors = placed[:3]
    by_chip_beyond = once(in_order(chip == 1, across, chip_beyond), weights)
    core_beyond = lax.ppermute(by_chip_beyond, "seq", CORE_SWAP)
    hidden_other, dy_other = whole_group(by_chip_beyond, core_beyond)
    unit_other = normed(hidden_other.astype(F32))[0]
    d_blocks = seq_shuffle(placed[3:])
    attn_in, qk, v = kernel_call(
        project_kernel,
        ((flat, BF), ((group, 2 * own), BF), ((group, own), BF)),
        (unit, weights, vectors, cosine, sine_a, sine_b),
        flops=2 * group * width * width,
    )
    held_shapes = ((flat, BF), ((group, half), BF), ((group, half), BF))
    give, keep, *held_other, up_full, down_full = kernel_call(
        mlp_kernel,
        (((2, rows, 2 * width), BF),) * 2 + held_shapes + (((8, width), F32), ((width, half), BF), ((half, width), BF)),
        (down_two, down_pair, mlp_two, mlp_pair, unit_other, dy_other, vectors),
        scratch=(pltpu.SemaphoreType.DMA((12,)),),
        flops=4 * group * width * 2 * half,
        megabytes=16,
        apart=4,
    )
    attended = kernel_call(
        with_waits(1, functools.partial(attention_kernel, deep)),
        (((2 * deep, group), BF),) * 4 + ((flat, BF),),
        (held_other[2], qk, v, *d_blocks, segment[:, None], segment[None, :], cosine, sine_a, sine_b),
        scratch=(((own, group), F32),) * 4 + ((flat, F32),),
        flops=14 * group * group * own,
        megabytes=16,
        apart=1,
    )
    d_joined = attended[4]
    row_blocks = seq_shuffle(attended[:4])

    own_pair, *held_own = kernel_call(
        with_waits(1, mlp_own_kernel),
        (((4, rows, 2 * width), BF),) + held_shapes + (((8, width), F32),),
        (d_joined, unit, dy, vectors, up_full, down_full),
        flops=4 * group * width * 2 * half,
        megabytes=16,
        apart=1,
    )
    attn_send, attn_keep, own_give, own_keep = kernel_call(
        functools.partial(attention_grads_kernel, deep),
        (((4, per_line + 8, width), BF),) * 2 + (((2, rows, 2 * width), BF),) * 2,
        (*row_blocks, dense, dy, attn_in, d_joined, weights, unit, vectors, own_pair),
        scratch=(((n_dp * deep, group), BF), ((width, width), F32), ((8, width), F32)),
        flops=5 * group * width * width,
        megabytes=16,
    )
    up_shape, down_shape = ((2, units + 8, width), BF), ((2, units, width), BF)
    keep_up, send_up, keep_down, send_down = kernel_call(
        with_waits(1, mlp_grads_kernel),
        (up_shape, up_shape, down_shape, down_shape),
        (attn_send, *held_own[:3], dy, held_own[3], *held_other[:3], dy_other, held_other[3]),
        scratch=(((width, half), BF), ((half, width), BF)),
        flops=4 * group * width * 2 * half,
        megabytes=16,
        apart=1,
    )

    attn_moved = lax.ppermute(attn_send, "dp", SIDE_SWAP)
    up_got = lax.ppermute(send_up, "dp", PAIR_SWAP)
    down_got = lax.ppermute(send_down, "dp", PAIR_SWAP)
    both = keep.astype(F32) + lax.ppermute(once(give, keep_up), "seq", CORE_SWAP).astype(F32)
    both = both.astype(BF)
    first = (attn_moved, up_got, down_got, both)
    up_mine, up_send = add_blocks(keep_up, up_got, 1, 1)
    up_last = lax.ppermute(once(up_send, *first), "dp", HALF_SWAP)
    attn_mine, attn_send = add_blocks(attn_keep, attn_moved, 2, 2)
    attn_got = lax.ppermute(once(attn_send, *first), "dp", PAIR_SWAP)
    down_mine, down_send = add_blocks(keep_down, down_got, 1, 1)
    down_last = lax.ppermute(once(down_send, *first), "dp", HALF_SWAP)
    beyond = lax.ppermute(once(both, *first), "dp", SIDE_SWAP)
    attn_mine, attn_send = add_blocks(attn_mine, attn_got, 1, 1, waits=(up_last,))
    attn_last = lax.ppermute(attn_send, "dp", HALF_SWAP)

    both = own_keep.astype(F32) + lax.ppermute(own_give, "seq", CORE_SWAP).astype(F32) + beyond.astype(F32)
    chip_last = lax.ppermute(pick(both, 1 - chip).astype(BF), "seq", CHIP_SWAP)
    pair = pick(both, chip) + chip_last.astype(F32)
    x = hidden_in.astype(F32)
    block_out = x + vectors[4] + vectors[5] + pair[:, :width]
    upstream = pair[:, width:]
    own_unit, inverse = normed(x)
    inner = (
        upstream
        - jnp.mean(upstream, axis=-1, keepdims=True)
        - own_unit * jnp.mean(upstream * own_unit, axis=-1, keepdims=True)
    )
    grad_in = grad_out.astype(F32) + inverse * inner

    up_keep, up_give, tail = kernel_call(
        with_waits(1, up_sum_kernel),
        (((per_line, half), BF), ((per_line + 16, half), BF), ((8, width), F32)),
        (attn_got, up_mine, up_last),
        megabytes=8,
        apart=1,
    )
    down_own = down_mine[0].astype(F32) + down_last[0].astype(F32)
    up_far = lax.ppermute(up_give, "dp", SIDE_SWAP)
    blocks = kernel_call(
        with_waits(1, functools.partial(owners_kernel, deep)),
        (((deep + 8, width), BF),) * 4,
        (attn_last, up_keep, up_far, tail),
        scratch=(((per_line, width), F32),),
        megabytes=8,
        apart=1,
    )
    up_own, vec_own = kernel_call(
        with_waits(2, functools.partial(owned_kernel, deep)),
        (((deep, hidden_units), F32), ((8, 128), F32)),
        (chip_last, attn_last, *seq_shuffle(blocks), tail),
        scratch=(((4, deep + 8, width), F32),),
        megabytes=8,
        apart=2,
    )
    *blocks, dense_own = kernel_call(
        with_waits(1, functools.partial(attention_sum_kernel, deep)),
        (((deep + 8, width), BF),) * 4 + (((deep, width), F32),),
        (up_far, attn_mine, attn_last),
        scratch=(((per_line + 8, width), F32),),
        megabytes=8,
        apart=1,
    )
    qkv_own, vec_attn = kernel_call(
        with_waits(1, functools.partial(attention_owned_kernel, deep)),
        (((deep, 3 * width), F32), ((8, 128), F32)),
        (chip_last, *seq_shuffle(blocks)),
        scratch=(((4, deep + 8, width), F32), ((8, 3 * width), F32)),
        megabytes=8,
        apart=1,
    )
    by_width = vec_own[:5, :deep]
    qkv_bias_grad = vec_attn[5, : 3 * deep]
    up_bias_grad = vec_own[6, :units]
    return (
        block_out.astype(BF),
        grad_in.astype(BF),
        vec_attn[0, :deep],
        vec_attn[1, :deep],
        by_width[2],
        by_width[3],
        qkv_own,
        qkv_bias_grad,
        dense_own,
        by_width[4],
        up_own,
        up_bias_grad,
        down_own,
        by_width[4],
    )


def per_device(*args):
    if lax.axis_size("dp") == 8 and lax.axis_size("seq") == 4:
        return line_device(*args)
    return general_device(*args)


def solution(mesh):
    both = ("dp", "seq")
    matrix, vector = P(both, None), P(both)
    params = (vector, vector, vector, vector, matrix, vector, matrix, vector, matrix, vector, matrix, vector)
    return jax.shard_map(
        per_device,
        mesh=mesh,
        in_specs=(matrix, P("dp", None), matrix) + params,
        out_specs=(matrix, matrix) + params,
        check_vma=False,
    )
```

```python
import functools

import jax
import jax.numpy as jnp
from jax import lax
from jax.experimental import pallas as pl
from jax.experimental.pallas import tpu as pltpu
from jax.sharding import PartitionSpec as P

HEADS = 12
HEAD_DIM = 64
ROT = 16
EPS = 1e-05
NEGATIVE = -1e30
BF = jnp.bfloat16
F32 = jnp.float32


def dot(spec, a, b):
    return jnp.einsum(spec, a, b, preferred_element_type=F32)


def frequencies():
    steps = jnp.arange(ROT // 2, dtype=F32)
    return jnp.power(F32(10000.0), -(2.0 * steps) / ROT)


def rotate(values, cosine, sine, sign):
    half = ROT // 2
    first = values[..., :half]
    second = values[..., half:ROT]
    turned_one = first * cosine - sign * second * sine
    turned_two = second * cosine + sign * first * sine
    return jnp.concatenate([turned_one, turned_two, values[..., ROT:]], axis=-1)


def place(row_lengths, index):
    ends = jnp.cumsum(row_lengths)
    after = (index[:, None] >= ends[None, :]).astype(jnp.int32)
    segment = jnp.sum(after, axis=1)
    start = jnp.sum(after * row_lengths[None, :], axis=1)
    return (segment, index - start)


def pick(values, index):
    return lax.dynamic_index_in_dim(values, index, 0, keepdims=False)


CHIP_SWAP = [(0, 2), (2, 0), (1, 3), (3, 1)]
CORE_SWAP = [(0, 1), (1, 0), (2, 3), (3, 2)]


def in_order(second, mine, other, axis=0):
    return jnp.stack([jnp.where(second, other, mine), jnp.where(second, mine, other)], axis=axis)


def seq_exchange(blocks):
    n = lax.axis_size("seq")
    if n != 4:
        return lax.all_to_all(blocks, "seq", 0, 0)
    me = lax.axis_index("seq")
    chip, core = me // 2, me % 2
    halves = blocks.reshape((2, 2) + blocks.shape[1:])
    far = lax.ppermute(pick(halves, 1 - chip), "seq", CHIP_SWAP)
    by_chip = in_order(chip == 1, pick(halves, chip), far, axis=1)
    other = lax.ppermute(pick(by_chip, 1 - core), "seq", CORE_SWAP)
    return in_order(core == 1, pick(by_chip, core), other, axis=1).reshape(blocks.shape)


def seq_gather(values):
    n = lax.axis_size("seq")
    if n != 4:
        return lax.all_gather(values, "seq", axis=0)
    me = lax.axis_index("seq")
    chip, core = me // 2, me % 2
    far = lax.ppermute(values, "seq", CHIP_SWAP)
    mine = in_order(chip == 1, values, far)
    other = lax.ppermute(mine, "seq", CORE_SWAP)
    return in_order(core == 1, mine, other, axis=1).reshape((n,) + values.shape)


def seq_reduce(values):
    n = lax.axis_size("seq")
    if n != 4:
        return lax.psum_scatter(values.astype(BF), "seq", scatter_dimension=0).astype(F32)
    me = lax.axis_index("seq")
    chip, core = me // 2, me % 2
    parts = values.reshape((2, 2) + values.shape[1:])
    keep = lax.dynamic_index_in_dim(parts, core, 1, keepdims=False)
    give = lax.dynamic_index_in_dim(parts, 1 - core, 1, keepdims=False).astype(BF)
    both = keep.astype(F32) + lax.ppermute(give, "seq", CORE_SWAP).astype(F32)
    far = lax.ppermute(pick(both, 1 - chip).astype(BF), "seq", CHIP_SWAP)
    return pick(both, chip) + far.astype(F32)


SIDE_SWAP = [(i, i ^ 1) for i in range(8)]


def along(step):
    return [(i, (i + 2 * step) % 8) for i in range(8)]


def dp_gather(block):
    n = lax.axis_size("dp")
    if n != 8:
        return lax.all_gather(block, "dp", axis=0)
    me = lax.axis_index("dp")
    line, side = me // 2, me % 2
    near1 = lax.ppermute(block, "dp", along(1))
    near3 = lax.ppermute(block, "dp", along(3))
    near2 = lax.ppermute(block, "dp", along(2))
    far0 = lax.ppermute(block, "dp", SIDE_SWAP)
    far13 = lax.ppermute(jnp.stack([near1, near3]), "dp", SIDE_SWAP)
    far2 = lax.ppermute(near2, "dp", SIDE_SWAP)
    full = jnp.zeros((4, 2) + block.shape, block.dtype)
    zero = jnp.int32(0)
    for step, near, far in ((0, block, far0), (1, near1, far13[0]), (3, near3, far13[1]), (2, near2, far2)):
        pair = in_order(side == 1, near, far)
        full = lax.dynamic_update_slice(full, pair[None], ((line - step) % 4, zero, zero, zero))
    return full.reshape((n,) + block.shape)


def dp_reduce(block_of):
    n = lax.axis_size("dp")
    if n != 8:
        blocks = jnp.stack([block_of(jnp.int32(i)).astype(BF) for i in range(n)])
        return lax.psum_scatter(blocks, "dp", scatter_dimension=0).astype(F32)
    me = lax.axis_index("dp")
    line, side = me // 2, me % 2

    def over_side(*steps):
        targets = [2 * ((line + step) % 4) for step in steps]
        moved = lax.ppermute(jnp.stack([block_of(t + 1 - side) for t in targets]), "dp", SIDE_SWAP)
        return [block_of(t + side).astype(F32) + moved[j].astype(F32) for j, t in enumerate(targets)]

    (sum2,) = over_side(2)
    sum1, sum3 = over_side(1, 3)
    (sum0,) = over_side(0)
    got2 = lax.ppermute(sum2.astype(BF), "dp", along(2)).astype(F32)
    got1 = lax.ppermute(sum1.astype(BF), "dp", along(1)).astype(F32)
    got3 = lax.ppermute(sum3.astype(BF), "dp", along(3)).astype(F32)
    return sum0 + got1 + got2 + got3


def attention(queries, keys, values, d_out, segment, scale):
    tokens = queries.shape[1]
    index = jnp.arange(tokens, dtype=jnp.int32)
    allowed = (segment[:, None] == segment[None, :]) & (index[None, :] <= index[:, None])
    scores = dot("htd,hnd->htn", queries, keys) * scale
    masked = jnp.where(allowed[None], scores, NEGATIVE)
    top = jnp.max(masked, axis=-1, keepdims=True)
    weights = jnp.where(allowed[None], jnp.exp(masked - top), 0.0)
    probs = weights / jnp.sum(weights, axis=-1, keepdims=True)
    probs_r = probs.astype(BF)
    attended = dot("htn,hnd->htd", probs_r, values)
    d_probs = dot("htd,hnd->htn", d_out, values)
    delta = jnp.sum(probs * d_probs, axis=-1, keepdims=True)
    d_scores = (probs * (d_probs - delta)).astype(BF)
    d_queries = dot("htn,hnd->htd", d_scores, keys) * scale
    d_keys = dot("htn,htd->hnd", d_scores, queries) * scale
    d_values = dot("htn,htd->hnd", probs_r, d_out)
    return attended, d_queries, d_keys, d_values


def general_device(
    hidden_in,
    lengths,
    grad_out,
    attn_gain,
    attn_shift,
    mlp_gain,
    mlp_shift,
    qkv_weight,
    qkv_bias,
    dense_weight,
    dense_bias,
    up_weight,
    up_bias,
    down_weight,
    down_bias,
):
    n_dp, n_seq = lax.axis_size("dp"), lax.axis_size("seq")
    me = lax.axis_index("seq")
    rows, width = hidden_in.shape
    group = rows * n_seq
    scale = HEAD_DIM ** (-0.5)
    hidden_units = up_weight.shape[1]
    own_units = hidden_units // n_seq
    deep = width // (n_dp * n_seq)
    unit_rows = hidden_units // (n_dp * n_seq)
    heads = -(-HEADS // n_seq)
    own = heads * HEAD_DIM
    spare = heads * n_seq - HEADS

    def by_head(values):
        lead = values.shape[:-1]
        split = values.reshape(lead + (3, HEADS, HEAD_DIM))
        if spare:
            split = jnp.pad(split, [(0, 0)] * (len(lead) + 1) + [(0, spare), (0, 0)])
        split = split.reshape(lead + (3, n_seq, own))
        return jnp.moveaxis(split, -2, 0).reshape((n_seq,) + lead + (3 * own,))

    def from_heads(blocks):
        lead = blocks.shape[1:-1]
        split = jnp.moveaxis(blocks.reshape((n_seq,) + lead + (3, own)), 0, -2)
        split = split.reshape(lead + (3, HEADS + spare, HEAD_DIM))[..., :HEADS, :]
        return split.reshape(lead + (3 * width,))

    vectors = (attn_gain, attn_shift, mlp_gain, mlp_shift, qkv_bias, dense_bias, up_bias, down_bias)
    sizes = [v.shape[0] for v in vectors]
    length = sum(sizes)
    wide = own_units + 3 * own
    up_blocks = jnp.moveaxis(up_weight.reshape(deep, n_dp, n_seq, unit_rows), 2, 0)
    up_blocks = up_blocks.reshape(n_seq, deep, own_units)
    vector = jnp.pad(jnp.concatenate(vectors), (0, wide - length))
    blocks = jnp.concatenate(
        [
            jnp.concatenate([up_blocks, by_head(qkv_weight)], axis=2),
            jnp.broadcast_to(vector, (n_seq, 1, wide)),
        ],
        axis=1,
    )
    got = seq_exchange(blocks)
    per_line = n_seq * deep
    up_rows = per_line * own_units // width
    up_piece = got[:, :deep, :own_units].reshape(up_rows, width)
    qkv_piece = got[:, :deep, own_units:].reshape(per_line, 3 * own)
    group_vector = got[:, deep, :length]

    both = seq_gather(jnp.concatenate([hidden_in, grad_out], axis=0))
    hidden_group = both[:, :rows].reshape(group, width)
    grad_group = both[:, rows:].reshape(group, width)

    def beside(values):
        lead = values.shape[:-2]
        split = values.reshape(lead + (deep, n_seq, width // n_seq))
        return jnp.swapaxes(split, -3, -2).reshape(lead + (per_line, width // n_seq))

    def from_beside(values):
        lead = values.shape[:-2]
        split = values.reshape(lead + (n_seq, deep, width // n_seq))
        return jnp.swapaxes(split, -3, -2).reshape(lead + (deep, width))

    attn_wide = 3 * own + width // n_seq
    vec_rows = -(-n_seq * length // attn_wide)
    vec_rows += -vec_rows % 8
    vec_piece = jnp.pad(group_vector.reshape(-1), (0, vec_rows * attn_wide - n_seq * length))
    attn_piece = jnp.concatenate([qkv_piece, beside(dense_weight)], axis=1)
    attn_piece = jnp.concatenate([attn_piece, vec_piece.reshape(vec_rows, attn_wide)], axis=0)
    attn_all = dp_gather(attn_piece)
    mlp_all = dp_gather(jnp.concatenate([up_piece, down_weight], axis=0))
    qkv_full = attn_all[:, :per_line, : 3 * own].reshape(width, 3 * own)
    dense_rows = from_beside(attn_all[:, :per_line, 3 * own :]).reshape(n_dp * deep, width)
    up_full = mlp_all[:, :up_rows].reshape(width, own_units)
    down_full = mlp_all[:, up_rows:].reshape(own_units, width)
    every = attn_all[:, per_line:].reshape(n_dp, vec_rows * attn_wide)[:, : n_seq * length]
    every = every.reshape(n_dp * n_seq, length).astype(F32)
    whole = []
    start = 0
    for size in sizes:
        whole.append(every[:, start : start + size].reshape(-1))
        start += size
    f_attn_gain, f_attn_shift, f_mlp_gain, f_mlp_shift, f_qkv_bias, f_dense_bias, f_up_bias, f_down_bias = whole
    own_qkv_bias = pick(by_head(f_qkv_bias), me)
    own_up_bias = lax.dynamic_index_in_dim(
        f_up_bias.reshape(n_dp, n_seq, unit_rows), me, 1, keepdims=False
    ).reshape(-1)

    row_lengths = lengths[0]
    index = jnp.arange(group, dtype=jnp.int32)
    segment, position = place(row_lengths, index)
    angles = position.astype(F32)[:, None] * frequencies()[None, :]
    cosine = jnp.cos(angles)[:, None, :]
    sine = jnp.sin(angles)[:, None, :]

    tokens = hidden_group.astype(F32)
    center = jnp.mean(tokens, axis=-1, keepdims=True)
    centered = tokens - center
    spread = jnp.mean(centered * centered, axis=-1, keepdims=True)
    unit = centered * lax.rsqrt(spread + EPS)
    attn_in = (unit * f_attn_gain + f_attn_shift).astype(BF)
    mlp_in = (unit * f_mlp_gain + f_mlp_shift).astype(BF)

    joined = dot("td,de->te", attn_in, qkv_full) + own_qkv_bias
    joined = joined.reshape(group, 3, heads, HEAD_DIM)
    queries = jnp.moveaxis(rotate(joined[:, 0], cosine, sine, 1.0).astype(BF), 1, 0)
    keys = jnp.moveaxis(rotate(joined[:, 1], cosine, sine, 1.0).astype(BF), 1, 0)
    values = jnp.moveaxis(joined[:, 2].astype(BF), 1, 0)
    feature_rows = n_dp * deep
    direct = spare == 0 and own % per_line == 0
    d_rows = dot("fe,te->ft", dense_rows, grad_group).astype(BF)
    if direct:
        runs = own // per_line
        moved = seq_exchange(d_rows.reshape(n_seq, runs * deep, group))
        moved = moved.reshape(n_seq, runs, deep, group)
        d_attended = jnp.moveaxis(moved, 0, 1).reshape(heads, HEAD_DIM, group)
    else:
        moved = lax.all_gather(d_rows.reshape(n_dp, deep, group), "seq", axis=1)
        moved = moved.reshape(width, group)
        moved = jnp.pad(moved, ((0, spare * HEAD_DIM), (0, 0)))
        d_attended = pick(moved.reshape(n_seq, heads, HEAD_DIM, group), me)
    d_attended = jnp.swapaxes(d_attended, 1, 2)
    attended, d_queries, d_keys, d_values = attention(queries, keys, values, d_attended, segment, scale)
    attended = jnp.swapaxes(attended.astype(BF), 1, 2).reshape(own, group)
    if direct:
        given = jnp.moveaxis(attended.reshape(runs, n_seq, deep, group), 1, 0)
        rows_attended = seq_exchange(given.reshape(n_seq, runs * deep, group)).reshape(feature_rows, group)
    else:
        given = lax.all_gather(attended, "seq", axis=0, tiled=True)[:width]
        rows_attended = lax.dynamic_index_in_dim(
            given.reshape(n_dp, n_seq, deep, group), me, 1, keepdims=False
        ).reshape(feature_rows, group)
    attn_out = dot("ft,fe->te", rows_attended, dense_rows)
    dense_grad = dot("ft,te->fe", rows_attended, grad_group).astype(BF).reshape(n_dp, deep, width)
    d_queries = rotate(jnp.moveaxis(d_queries, 0, 1), cosine, sine, -1.0)
    d_keys = rotate(jnp.moveaxis(d_keys, 0, 1), cosine, sine, -1.0)
    d_joined = jnp.stack([d_queries, d_keys, jnp.moveaxis(d_values, 0, 1)], axis=1)
    d_joined = d_joined.astype(BF).reshape(group, 3 * own)
    qkv_grad = dot("td,te->de", attn_in, d_joined).astype(BF).reshape(n_dp, n_seq * deep, 3 * own)
    d_attn_in = dot("te,de->td", d_joined, qkv_full)
    attn_terms = jnp.concatenate([qkv_grad, beside(dense_grad)], axis=2)
    attn_sum = dp_reduce(lambda i: pick(attn_terms, i))

    upper = dot("td,df->tf", mlp_in, up_full) + own_up_bias
    cdf = 0.5 * (1.0 + lax.erf(upper * F32(0.7071067811865476)))
    pdf = jnp.exp(-0.5 * upper * upper) * F32(0.3989422804014327)
    act = (upper * cdf).astype(BF)
    d_act = dot("td,fd->tf", grad_group, down_full)
    d_up = (d_act * (cdf + upper * pdf)).astype(BF)
    down_grad = dot("tf,td->fd", act, grad_group).astype(BF).reshape(n_dp, unit_rows, width)
    up_grad = dot("td,tf->df", mlp_in, d_up).astype(BF).reshape(n_dp, up_rows, width)
    mlp_out = dot("tf,fd->td", act, down_full)
    d_mlp_in = dot("tf,df->td", d_up, up_full)

    mine = jnp.arange(n_seq) == me
    qkv_bias_grad = jnp.sum(d_joined.astype(F32), axis=0)
    qkv_bias_grad = from_heads(jnp.where(mine[:, None], qkv_bias_grad[None], 0.0))
    up_bias_grad = jnp.sum(d_up.astype(F32), axis=0).reshape(n_dp, 1, unit_rows)
    up_bias_grad = jnp.where(mine[None, :, None], up_bias_grad, 0.0)
    bias_sum = jnp.sum(grad_out.astype(F32), axis=0)
    terms = (
        jnp.sum(d_attn_in * unit, axis=0),
        jnp.sum(d_attn_in, axis=0),
        jnp.sum(d_mlp_in * unit, axis=0),
        jnp.sum(d_mlp_in, axis=0),
        qkv_bias_grad,
        bias_sum,
        up_bias_grad,
        bias_sum,
    )
    terms = [t.reshape(n_dp, n_seq, size) for t, size in zip(terms, sizes)]
    terms = jnp.concatenate(terms, axis=2).reshape(n_dp, n_seq * length)
    tail_rows = -(-n_seq * length // width)
    tail_rows += -tail_rows % 8
    terms = jnp.pad(terms, ((0, 0), (0, tail_rows * width - n_seq * length)))
    terms = terms.reshape(n_dp, tail_rows, width).astype(BF)
    mlp_sum = dp_reduce(lambda i: jnp.concatenate([pick(up_grad, i), pick(down_grad, i), pick(terms, i)], axis=0))

    upstream = d_attn_in * f_attn_gain + d_mlp_in * f_mlp_gain
    pair = jnp.concatenate([(attn_out + mlp_out).astype(BF), upstream.astype(BF)], axis=1)
    pair = seq_reduce(pair.reshape(n_seq, rows, 2 * width))
    block_out = hidden_in.astype(F32) + f_dense_bias + f_down_bias + pair[:, :width]
    upstream = pair[:, width:]
    x = hidden_in.astype(F32)
    centered = x - jnp.mean(x, axis=-1, keepdims=True)
    inverse = lax.rsqrt(jnp.mean(centered * centered, axis=-1, keepdims=True) + EPS)
    own_unit = centered * inverse
    inner = (
        upstream
        - jnp.mean(upstream, axis=-1, keepdims=True)
        - own_unit * jnp.mean(upstream * own_unit, axis=-1, keepdims=True)
    )
    grad_in = grad_out.astype(F32) + inverse * inner

    qkv_back = attn_sum[:, : 3 * own].reshape(n_seq, deep, 3 * own).astype(BF)
    qkv_own = from_heads(seq_exchange(qkv_back).astype(F32))
    dense_own = from_beside(attn_sum[:, 3 * own :])
    vec_sum = mlp_sum[up_rows + unit_rows :].reshape(-1)[: n_seq * length].reshape(n_seq, 1, length)
    vec_sum = jnp.pad(vec_sum, ((0, 0), (0, 0), (0, -length % own_units)))
    vec_sum = vec_sum.reshape(n_seq, -1, own_units)
    back = jnp.concatenate([mlp_sum[:up_rows].reshape(n_seq, deep, own_units), vec_sum], axis=1)
    back = seq_exchange(back.astype(BF)).astype(F32)
    up_own = jnp.moveaxis(back[:, :deep].reshape(n_seq, deep, n_dp, unit_rows), 0, 2)
    vec_own = jnp.sum(back[:, deep:].reshape(n_seq, -1), axis=0)
    owned = []
    start = 0
    for size in sizes:
        owned.append(vec_own[start : start + size])
        start += size
    return (
        block_out.astype(BF),
        grad_in.astype(BF),
        owned[0],
        owned[1],
        owned[2],
        owned[3],
        qkv_own,
        owned[4],
        dense_own,
        owned[5],
        up_own.reshape(deep, hidden_units),
        owned[6],
        mlp_sum[up_rows : up_rows + unit_rows],
        owned[7],
    )


SCALE = HEAD_DIM**-0.5


def kernel_call(body, outs, args, scratch=(), megabytes=24, flops=0, apart=0):
    moved = sum(a.size * a.dtype.itemsize for a in args)
    held = [pl.BlockSpec(memory_space=pl.ANY)] * apart
    held += [pl.BlockSpec(memory_space=pltpu.VMEM)] * (len(args) - apart)
    return pl.pallas_call(
        body,
        out_shape=tuple(jax.ShapeDtypeStruct(shape, kind) for shape, kind in outs),
        in_specs=held,
        scratch_shapes=[pltpu.VMEM(*item) if isinstance(item, tuple) else item for item in scratch],
        compiler_params=pltpu.CompilerParams(vmem_limit_bytes=megabytes << 20),
        cost_estimate=pl.CostEstimate(flops=flops, bytes_accessed=moved, transcendentals=0),
    )(*args)


def dot_nn(a, b):
    return lax.dot_general(a, b, (((1,), (0,)), ((), ())), preferred_element_type=F32)


def dot_nt(a, b):
    return lax.dot_general(a, b, (((1,), (1,)), ((), ())), preferred_element_type=F32)


def dot_tn(a, b):
    return lax.dot_general(a, b, (((0,), (0,)), ((), ())), preferred_element_type=F32)


def line_and_side():
    me = lax.axis_index("dp")
    return lax.shift_right_logical(me, 1), lax.bitwise_and(me, 1)


PAIR_SWAP = [(i, i ^ 2) for i in range(8)]
HALF_SWAP = [(i, i ^ 4) for i in range(8)]
LINE_ORDER = (0, 2, 1, 3)


def dp_index(line, step, side):
    return 2 * lax.bitwise_xor(line, step) + side


def pick_blocks(block_of, send, keep):
    line, side = line_and_side()
    for j, step in enumerate(LINE_ORDER):
        send[j] = block_of(dp_index(line, step, 1 - side))
        keep[j] = block_of(dp_index(line, step, side))


def add_kernel(here, there, *out):
    place = 0
    for ref in out:
        for j in range(ref.shape[0]):
            ref[j] = (here[place + j].astype(F32) + there[place + j].astype(F32)).astype(ref.dtype)
        place += ref.shape[0]


def add_blocks(here, there, *counts, waits=()):
    shape = here.shape[1:]
    return kernel_call(
        with_waits(len(waits), add_kernel),
        tuple(((count,) + shape, BF) for count in counts),
        (*waits, here, there),
        megabytes=8,
        apart=len(waits),
    )


def once(values, *others):
    return lax.optimization_barrier((values, *others))[0]


def seq_shuffle(blocks):
    got = [blocks[0]]
    for other in (1, 2, 3):
        pairs = [(i, i ^ other) for i in range(4)]
        got.append(lax.ppermute(blocks[other], "seq", pairs))
    return got


def place_kernel(deep, *refs):
    pieces, (dy, weights, dense, vectors), d_blocks, (rows32, d_rows) = refs[:4], refs[4:8], refs[8:12], refs[12:]
    line, side = line_and_side()
    per_line = 4 * deep
    quarter = dy.shape[1] // 4
    own = weights.shape[1] - quarter
    total = jnp.zeros(vectors.shape, F32)
    for place in range(8):
        piece = pieces[place // 2].at[place % 2]
        owner = dp_index(line, LINE_ORDER[place % 4], side if place < 4 else 1 - side)
        weights[pl.ds(pl.multiple_of(owner * per_line, per_line), per_line), :] = piece[:per_line, :]
        total = total + piece[per_line:, :].astype(F32)
        beside = piece[:per_line, own:].astype(F32)
        for q in range(4):
            rows32[pl.ds(pl.multiple_of(owner * deep, 8), deep), q * quarter : (q + 1) * quarter] = beside[
                q * deep : (q + 1) * deep
            ]
    vectors[...] = total
    dense[...] = rows32[...].astype(BF)
    d_rows[...] = dot_nt(dense[...], dy[...]).astype(BF)
    me = lax.axis_index("seq")
    count = d_blocks[0].shape[0]
    for j in range(4):
        d_blocks[j][...] = d_rows[pl.ds(pl.multiple_of(lax.bitwise_xor(me, j) * count, 16), count), :]


def turn(values, cosine, sine_a, sine_b, sign):
    half = ROT // 2
    ahead = pltpu.roll(values, 128 - half, 1)
    behind = pltpu.roll(values, half, 1)
    return values * cosine + sign * (ahead * sine_a + behind * sine_b)


def project_kernel(unit, weights, vectors, cosine, sine_a, sine_b, attn_in, qk, v):
    gain, shift, bias = vectors[0:1, :], vectors[1:2, :], vectors[6:7, :]
    turned = qk.shape[1]
    size = 128

    def step(i, carry):
        rows = pl.ds(pl.multiple_of(i * size, size), size)
        normed = (unit[rows, :] * gain + shift).astype(BF)
        attn_in[rows, :] = normed
        joined = dot_nn(normed, weights[...]) + bias
        tables = cosine[rows, :], sine_a[rows, :], sine_b[rows, :]
        for c in range(0, turned, 128):
            qk[rows, c : c + 128] = turn(joined[:, c : c + 128], *tables, 1.0).astype(BF)
        v[rows, :] = joined[:, turned : turned + v.shape[1]].astype(BF)
        return carry

    lax.fori_loop(0, unit.shape[0] // size, step, 0)


def attention_kernel(deep, *refs):
    qk, v, d0, d1, d2, d3, seg_column, seg_row, cosine, sine_a, sine_b = refs[:11]
    given, d_joined, (d_t, out_t, dk_t, dv_t, acc) = refs[11:15], refs[15], refs[16:]
    tokens, own = v.shape
    me = lax.axis_index("seq")
    runs = own // (4 * deep)
    for j, ref in enumerate((d0, d1, d2, d3)):
        source = lax.bitwise_xor(me, j)
        block = ref[...].astype(F32)
        for r in range(runs):
            place = pl.multiple_of(r * 4 * deep + source * deep, 8)
            d_t[pl.ds(place, deep), :] = block[r * deep : (r + 1) * deep]
    d_out = jnp.transpose(d_t[...]).astype(BF)
    q_t = jnp.transpose(qk[:, :own].astype(F32)).astype(BF)
    d_tb = d_t[...].astype(BF)
    dk_t[...] = jnp.zeros(dk_t.shape, F32)
    dv_t[...] = jnp.zeros(dv_t.shape, F32)
    size = 256
    for h in range(own // HEAD_DIM):
        lanes = slice(h * HEAD_DIM, (h + 1) * HEAD_DIM)
        q_h = qk[:, lanes]
        k_h = qk[:, own + h * HEAD_DIM : own + (h + 1) * HEAD_DIM]
        v_h = v[:, lanes]
        d_h = d_out[:, lanes]
        for first in range(0, tokens, size):
            rows = slice(first, first + size)
            n = first + size
            scores = dot_nt(q_h[rows], k_h[:n]) * SCALE
            query = lax.broadcasted_iota(jnp.int32, (size, n), 0) + first
            key = lax.broadcasted_iota(jnp.int32, (size, n), 1)
            allowed = (seg_column[rows, :] == seg_row[:, :n]) & (key <= query)
            scores = jnp.where(allowed, scores, NEGATIVE)
            weights = jnp.where(allowed, jnp.exp(scores - jnp.max(scores, axis=1, keepdims=True)), 0.0)
            probs = weights * (1.0 / jnp.sum(weights, axis=1, keepdims=True))
            probs_r = probs.astype(BF)
            out_t[lanes, rows] = jnp.transpose(dot_nn(probs_r, v_h[:n]))
            d_probs = dot_nt(d_h[rows], v_h[:n])
            delta = jnp.sum(probs * d_probs, axis=1, keepdims=True)
            d_scores = (probs * (d_probs - delta)).astype(BF)
            acc[rows, lanes] = dot_nn(d_scores, k_h[:n]) * SCALE
            dk_t[lanes, :n] += dot_nn(q_t[lanes, rows], d_scores)
            dv_t[lanes, :n] += dot_nn(d_tb[lanes, rows], probs_r)
    acc[:, own : 2 * own] = jnp.transpose(dk_t[...]) * SCALE
    for c in range(0, 2 * own, 128):
        turned = turn(acc[:, c : c + 128], cosine[...], sine_a[...], sine_b[...], -1.0)
        d_joined[:, c : c + 128] = turned.astype(BF)
    d_joined[:, 2 * own : 3 * own] = jnp.transpose(dv_t[...]).astype(BF)
    d_joined[:, 3 * own :] = jnp.zeros((tokens, d_joined.shape[1] - 3 * own), BF)
    for j in range(4):
        target = lax.bitwise_xor(me, j)
        parts = [out_t[pl.ds(pl.multiple_of(r * 4 * deep + target * deep, 8), deep), :] for r in range(runs)]
        given[j][...] = jnp.concatenate(parts, axis=0).astype(BF)


def attention_grads_kernel(deep, *refs):
    r0, r1, r2, r3, dense, dy, attn_in, d_joined, weights, unit, vectors, own_pair = refs[:12]
    picks, (give, keep), (rows_t, grads, sums) = refs[12:14], refs[14:16], refs[16:]
    me = lax.axis_index("seq")
    core = lax.bitwise_and(me, 1)
    count = r0.shape[0]
    width = dy.shape[1]
    quarter = width // 4
    own = width - quarter
    for j, ref in enumerate((r0, r1, r2, r3)):
        rows_t[pl.ds(pl.multiple_of(lax.bitwise_xor(me, j) * count, 16), count), :] = ref[...]
    attended = jnp.transpose(rows_t[...].astype(F32)).astype(BF)
    gain = vectors[0:1, :]
    size = dy.shape[0] // 4
    sums[...] = jnp.zeros(sums.shape, F32)
    for i in range(4):
        rows = slice(i * size, (i + 1) * size)
        out = dot_nn(attended[rows], dense[...]) + own_pair[i, :, :width].astype(F32)
        back = dot_nt(d_joined[rows, :], weights[...])
        sums[0:1, :] += jnp.sum(back * unit[rows, :], axis=0, keepdims=True)
        sums[1:2, :] += jnp.sum(back, axis=0, keepdims=True)
        sums[5:6, :] += jnp.sum(d_joined[rows, :].astype(F32), axis=0, keepdims=True)
        out = out.astype(BF)
        back = (back * gain + own_pair[i, :, width:].astype(F32)).astype(BF)

        @pl.when(core == i % 2)
        def _():
            keep[i // 2, :, :width] = out
            keep[i // 2, :, width:] = back

        @pl.when(core != i % 2)
        def _():
            give[i // 2, :, :width] = out
            give[i // 2, :, width:] = back

    for c in range(0, width, 128):
        grads[c : c + 128, :] = dot_tn(attn_in[:, c : c + 128], d_joined[...])
    dense_grad = dot_nn(rows_t[...], dy[...])
    for p in range(8):
        for q in range(4):
            start = p * 4 * deep + q * deep
            grads[start : start + deep, own:] = dense_grad[p * deep : (p + 1) * deep, q * quarter : (q + 1) * quarter]
    per_line = 4 * deep
    tail = sums[...]

    def block_of(index):
        block = grads[pl.ds(pl.multiple_of(index * per_line, per_line), per_line), :]
        return jnp.concatenate([block, tail], axis=0).astype(BF)

    pick_blocks(block_of, *picks)


def pack_kernel(deep, *refs):
    qkv, up, by_width, qkv_bias, x, dy, blocks, mine, (all_blocks, row_block) = *refs[:6], refs[6:10], *refs[10:11], refs[11:]
    width = qkv.shape[1] // 3
    own = width // 4
    units = up.shape[1] // 32
    me = lax.axis_index("seq")
    device = 4 * lax.axis_index("dp") + me
    row_block[...] = jnp.zeros(row_block.shape, F32)
    row_block[:6, :deep] = by_width[...].astype(F32)
    vectors = pltpu.roll(row_block[:, :width], device * deep, 1)
    row_block[0:6, :] = jnp.zeros((6, row_block.shape[1]), F32)
    row_block[6:7, : 3 * deep] = qkv_bias[...].astype(F32)
    bias_rows = pltpu.roll(row_block[...], device * (3 * deep), 1)
    up_values, qkv_values = up[...].astype(F32), qkv[...].astype(F32)
    empty = jnp.zeros((deep + 8, own), F32)
    both = jnp.concatenate([qkv_values, bias_rows], axis=0)
    for t in range(4):
        parts = [up_values[:, ((l * 2 + y) * 4 + t) * units :][:, :units] for y in range(2) for l in range(4)]
        all_blocks[t, :deep, :] = jnp.concatenate(parts, axis=1)
        parts = [both[:, part * width + t * own : part * width + (t + 1) * own] for part in range(3)]
        parts = jnp.concatenate(parts + [empty], axis=1)
        all_blocks[t, deep : 2 * deep, :] = parts[:deep]
        all_blocks[t, 2 * deep :, :] = parts[deep:] + vectors
    rows = x.shape[0]
    for j in range(4):
        blocks[j][...] = all_blocks[lax.bitwise_xor(me, j)].astype(BF)
    mine[:rows, :] = x[...]
    mine[rows:, :] = dy[...]


def unpack_kernel(deep, r0, r1, r2, r3, dense, up_bias, attn_piece, up_keep, up_give, up32, qkv32, row_block):
    me = lax.axis_index("seq")
    line, side = line_and_side()
    width = dense.shape[1]
    quarter = width // 4
    half = up_keep.shape[1]
    own = 3 * quarter
    extra = jnp.zeros((8, width), F32)
    for j, ref in enumerate((r0, r1, r2, r3)):
        block = ref[...].astype(F32)
        place = pl.ds(pl.multiple_of(lax.bitwise_xor(me, j) * deep, 8), deep)
        up32[place, :] = block[:deep]
        qkv32[place, :] = block[deep : 2 * deep]
        extra = extra + block[2 * deep :]
    rows = 4 * deep
    first, second = up32[:, :half], up32[:, half:]
    up_keep[...] = jnp.where(side == 0, first, second).astype(BF)
    up_give[...] = jnp.where(side == 0, second, first).astype(BF)
    attn_piece[:rows, :own] = qkv32[:, :own].astype(BF)
    dense_values = dense[...].astype(F32)
    beside = [dense_values[:, q * quarter : (q + 1) * quarter] for q in range(4)]
    attn_piece[:rows, own:] = jnp.concatenate(beside, axis=0).astype(BF)
    units = half // 4
    row_block[...] = jnp.zeros(row_block.shape, F32)
    row_block[7:8, :units] = up_bias[...].astype(F32)
    attn_piece[rows:, :] = (extra + pltpu.roll(row_block[...], side * half + line * units, 1)).astype(BF)


def mlp_tokens(unit, dy, vectors, up, down, mlp_in, act, d_up, sums, side, store):
    half = up.shape[1]
    gain, shift = vectors[2:3, :], vectors[3:4, :]
    bias = jnp.where(side == 0, vectors[7:8, :half], vectors[7:8, half:])
    sums[...] = jnp.zeros(sums.shape, F32)
    size = unit.shape[0] // 4

    def step(i, carry):
        rows = pl.ds(pl.multiple_of(i * size, size), size)
        u = unit[rows, :]
        normed = (u * gain + shift).astype(BF)
        mlp_in[rows, :] = normed
        upper = dot_nn(normed, up[...]) + bias
        cdf = 0.5 * (1.0 + lax.erf(upper * 0.7071067811865476))
        pdf = jnp.exp(-0.5 * upper * upper) * 0.3989422804014327
        act_rows = (upper * cdf).astype(BF)
        act[rows, :] = act_rows
        d_rows = (dot_nt(dy[rows, :], down[...]) * (cdf + upper * pdf)).astype(BF)
        d_up[rows, :] = d_rows
        out = dot_nn(act_rows, down[...]).astype(BF)
        back = dot_nt(d_rows, up[...])
        sums[2:3, :] += jnp.sum(back * u, axis=0, keepdims=True)
        sums[3:4, :] += jnp.sum(back, axis=0, keepdims=True)
        sums[6:7, :half] += jnp.sum(d_rows.astype(F32), axis=0, keepdims=True)
        store(i, out, (back * gain).astype(BF))
        return carry

    lax.fori_loop(0, 4, step, 0)


def mlp_kernel(*refs):
    pieces, (unit, dy, vectors) = refs[:4], refs[4:7]
    give, keep, mlp_in, act, d_up, sums, up, down, done = refs[7:]
    line, side = line_and_side()
    width, half = up.shape
    units = half // 4
    copies = []
    for place, step in enumerate(LINE_ORDER):
        low, high = [pieces[k + place // 2].at[place % 2] for k in (0, 2)]
        l = lax.bitwise_xor(line, step)
        for source, target in (
            (low, down.at[pl.ds(pl.multiple_of(l * units, 32), units), :]),
            (high.at[:, pl.ds(0, half)], up.at[pl.ds(pl.multiple_of(2 * l * units, 32), units), :]),
            (high.at[:, pl.ds(half, half)], up.at[pl.ds(pl.multiple_of((2 * l + 1) * units, 32), units), :]),
        ):
            copies.append(pltpu.make_async_copy(source, target, done.at[len(copies)]))
    for copy in copies:
        copy.start()
    core = lax.bitwise_and(lax.axis_index("seq"), 1)
    for copy in copies:
        copy.wait()

    def store(i, out, back):
        place = lax.shift_right_logical(i, 1)

        @pl.when(lax.bitwise_and(i, 1) == core)
        def _():
            keep[place, :, :width] = out
            keep[place, :, width:] = back

        @pl.when(lax.bitwise_and(i, 1) != core)
        def _():
            give[place, :, :width] = out
            give[place, :, width:] = back

    mlp_tokens(unit, dy, vectors, up, down, mlp_in, act, d_up, sums, side, store)


def mlp_own_kernel(unit, dy, vectors, up, down, own_pair, mlp_in, act, d_up, sums):
    _, side = line_and_side()
    width = up.shape[0]

    def store(i, out, back):
        own_pair[i, :, :width] = out
        own_pair[i, :, width:] = back

    mlp_tokens(unit, dy, vectors, up, down, mlp_in, act, d_up, sums, side, store)
    sums[4:5, :] = 0.25 * jnp.sum(dy[...].astype(F32), axis=0, keepdims=True)


def mlp_grads_kernel(*refs):
    own, other = refs[:5], refs[5:10]
    keep_up, send_up, keep_down, send_down, up_grad, down_grad = refs[10:]
    line, _ = line_and_side()
    half, width = down_grad.shape
    units = half // 4
    for c in range(0, width, 128):
        total = sum(dot_tn(mlp_in[:, c : c + 128], d_up[...]) for mlp_in, _, d_up, _, _ in (own, other))
        up_grad[c : c + 128, :] = total.astype(BF)
    for c in range(0, half, 128):
        total = sum(dot_tn(act[:, c : c + 128], dy[...]) for _, act, _, dy, _ in (own, other))
        down_grad[c : c + 128, :] = total.astype(BF)
    tail = (own[4][...] + other[4][...]).astype(BF)
    for place, step in enumerate(LINE_ORDER):
        ups, downs = ((keep_up, keep_down), (send_up, send_down))[place // 2]
        l = lax.bitwise_xor(line, step)
        downs[place % 2] = down_grad[pl.ds(pl.multiple_of(l * units, 32), units), :]
        ref = ups.at[place % 2]
        ref[:units, :half] = up_grad[pl.ds(pl.multiple_of(2 * l * units, 32), units), :]
        ref[:units, half:] = up_grad[pl.ds(pl.multiple_of((2 * l + 1) * units, 32), units), :]
        ref[units:, :] = tail


def up_sum_kernel(own, far, up_keep, up_give, tail):
    units, half = up_keep.shape
    width = 2 * half
    _, side = line_and_side()

    def total(rows, lanes):
        return own[0, rows, lanes].astype(F32) + far[0, rows, lanes].astype(F32)

    first, second = total(slice(0, units), slice(0, half)), total(slice(0, units), slice(half, width))
    last = total(slice(units, units + 8), slice(None))
    tail[...] = last
    up_keep[...] = jnp.where(side == 0, first, second).astype(BF)
    up_give[:units, :] = jnp.where(side == 0, second, first).astype(BF)
    up_give[units:, :] = jnp.concatenate([last[:, :half], last[:, half:]], axis=0).astype(BF)


def owners_kernel(deep, keep, far, tail, b0, b1, b2, b3, rows32):
    _, side = line_and_side()
    me = lax.axis_index("seq")
    rows, half = keep.shape
    here, there = keep[...].astype(F32), far[:rows, :].astype(F32)
    rows32[:, :half] = jnp.where(side == 0, here, there)
    rows32[:, half:] = jnp.where(side == 0, there, here)
    far_tail = far[rows:, :].astype(F32)
    last = tail[...] + jnp.concatenate([far_tail[:8], far_tail[8:]], axis=1)
    for j, ref in enumerate((b0, b1, b2, b3)):
        target = lax.bitwise_xor(me, j)
        block = rows32[pl.ds(pl.multiple_of(target * deep, 8), deep), :]
        ref[...] = jnp.concatenate([block, last], axis=0).astype(BF)


def owned_kernel(deep, b0, b1, b2, b3, tail, up_own, vec_own, sources):
    line, _ = line_and_side()
    me = lax.axis_index("seq")
    device = 4 * lax.axis_index("dp") + me
    width = tail.shape[1]
    half = width // 2
    units = half // 4
    for j, ref in enumerate((b0, b1, b2, b3)):
        sources[lax.bitwise_xor(me, j)] = ref[...].astype(F32)
    for l in range(4):
        parts = [
            sources[t, :deep, y * half + l * units : y * half + (l + 1) * units] for y in range(2) for t in range(4)
        ]
        up_own[:, l * 2 * half : (l + 1) * 2 * half] = jnp.concatenate(parts, axis=1)
    total = sources[0, deep:] + sources[1, deep:] + sources[2, deep:] + sources[3, deep:]
    rolled = pltpu.roll(total, width - device * deep, 1)
    vec_own[...] = rolled[:, :128]
    rolled = pltpu.roll(tail[...], width - line * units, 1)
    vec_own[6:7, :] = rolled[6:7, :128]


def attention_sum_kernel(deep, own, far, b0, b1, b2, b3, dense_own, total):
    me = lax.axis_index("seq")
    total[...] = own[0].astype(F32) + far[0].astype(F32)
    quarter = total.shape[1] // 4
    last = total[4 * deep :, :]
    for q in range(4):
        dense_own[:, q * quarter : (q + 1) * quarter] = total[q * deep : (q + 1) * deep, 3 * quarter :]
    for j, ref in enumerate((b0, b1, b2, b3)):
        target = lax.bitwise_xor(me, j)
        block = total[pl.ds(pl.multiple_of(target * deep, 8), deep), :]
        ref[...] = jnp.concatenate([block, last], axis=0).astype(BF)


def attention_owned_kernel(deep, b0, b1, b2, b3, qkv_own, vec_own, sources, row_block):
    me = lax.axis_index("seq")
    device = 4 * lax.axis_index("dp") + me
    width = b0.shape[1]
    own = width // 4
    for j, ref in enumerate((b0, b1, b2, b3)):
        sources[lax.bitwise_xor(me, j)] = ref[...].astype(F32)
    total = sources[0, deep:] + sources[1, deep:] + sources[2, deep:] + sources[3, deep:]
    vec_own[...] = pltpu.roll(total, width - device * deep, 1)[:, :128]
    row_block[...] = jnp.zeros(row_block.shape, F32)
    for part in range(3):
        lanes = slice(part * own, (part + 1) * own)
        whole = jnp.concatenate([sources[t, :, lanes] for t in range(4)], axis=1)
        qkv_own[:, part * width : (part + 1) * width] = whole[:deep]
        row_block[5:6, part * width : (part + 1) * width] = whole[deep + 5 : deep + 6]
    rolled = pltpu.roll(row_block[...], 3 * width - device * (3 * deep), 1)
    vec_own[5:6, :] = rolled[5:6, :128]


def with_waits(count, body):
    def wrapped(*refs):
        body(*refs[count:])

    return wrapped


def line_device(
    hidden_in,
    lengths,
    grad_out,
    attn_gain,
    attn_shift,
    mlp_gain,
    mlp_shift,
    qkv_weight,
    qkv_bias,
    dense_weight,
    dense_bias,
    up_weight,
    up_bias,
    down_weight,
    down_bias,
):
    n_dp, n_seq = 8, 4
    dp_me, me = lax.axis_index("dp"), lax.axis_index("seq")
    line, side = lax.shift_right_logical(dp_me, 1), lax.bitwise_and(dp_me, 1)
    chip, core = lax.shift_right_logical(me, 1), lax.bitwise_and(me, 1)
    device = dp_me * n_seq + me
    zero = jnp.int32(0)
    rows, width = hidden_in.shape
    group = rows * n_seq
    hidden_units = up_weight.shape[1]
    units = hidden_units // (n_dp * n_seq)
    half = hidden_units // 8
    deep = width // (n_dp * n_seq)
    per_line = n_seq * deep
    own = width // n_seq
    wide = 2 * half + 3 * own
    flat = (group, width)

    by_width = jnp.stack([attn_gain, attn_shift, mlp_gain, mlp_shift, dense_bias, down_bias])
    *blocks, mine = kernel_call(
        functools.partial(pack_kernel, deep),
        (((2 * deep + 8, width), BF),) * 4 + (((2 * rows, width), BF),),
        (qkv_weight, up_weight, by_width, qkv_bias[None], hidden_in, grad_out),
        scratch=(((4, 2 * deep + 8, width), F32), ((8, 3 * width), F32)),
        megabytes=16,
    )
    attn_piece, up_keep, up_give = kernel_call(
        functools.partial(unpack_kernel, deep),
        (((per_line + 8, width), BF), ((per_line, half), BF), ((per_line, half), BF)),
        (*seq_shuffle(blocks), dense_weight, up_bias[None]),
        scratch=(((per_line, width), F32), ((per_line, width), F32), ((8, width), F32)),
        megabytes=16,
    )

    across = lax.ppermute(mine, "dp", SIDE_SWAP)
    down_half = lax.ppermute(down_weight, "dp", HALF_SWAP)
    attn_piece, up_keep, up_give = once(attn_piece, down_half), up_keep, once(up_give, down_half)
    down_two = jnp.stack([down_weight, down_half])
    down_pair = lax.ppermute(down_two, "dp", PAIR_SWAP)
    attn_half = lax.ppermute(attn_piece, "dp", HALF_SWAP)
    up_far = lax.ppermute(up_give, "dp", SIDE_SWAP)
    chip_far = lax.ppermute(once(mine, up_keep), "seq", CHIP_SWAP)

    attn_two = once(jnp.stack([attn_piece, attn_half]), up_far)
    attn_pair = lax.ppermute(attn_two, "dp", PAIR_SWAP)
    attn_side = lax.ppermute(attn_two, "dp", SIDE_SWAP)
    up_both = jnp.concatenate(
        [jnp.where(side == 0, up_keep, up_far), jnp.where(side == 0, up_far, up_keep)], axis=1
    )
    mlp_piece = once(up_both, attn_half)
    mlp_half = lax.ppermute(mlp_piece, "dp", HALF_SWAP)
    by_chip = once(in_order(chip == 1, mine, chip_far), attn_half, up_far)
    core_far = lax.ppermute(by_chip, "seq", CORE_SWAP)

    attn_far = lax.ppermute(once(attn_pair, mlp_half), "dp", SIDE_SWAP)
    mlp_two = once(jnp.stack([mlp_piece, mlp_half]), attn_pair, down_pair)
    mlp_pair = lax.ppermute(mlp_two, "dp", PAIR_SWAP)
    chip_beyond = lax.ppermute(once(across, mlp_half, attn_pair, attn_side), "seq", CHIP_SWAP)

    def whole_group(values, over):
        full = in_order(core == 1, values, over, axis=1).reshape(n_seq, 2, rows, width)
        return full[:, 0].reshape(flat), full[:, 1].reshape(flat)

    hidden_group, dy = whole_group(by_chip, core_far)
    attn_pieces = (attn_two, attn_pair, attn_side, attn_far)

    row_lengths = lengths[0]
    segment, position = place(row_lengths, jnp.arange(group, dtype=jnp.int32))
    lane = jnp.arange(128, dtype=jnp.int32) % HEAD_DIM
    powers = jnp.power(F32(10000.0), -(2.0 * (lane % (ROT // 2)).astype(F32)) / ROT)
    angles = position.astype(F32)[:, None] * powers[None, :]
    cosine = jnp.where(lane < ROT, jnp.cos(angles), 1.0)
    sine = jnp.sin(angles)
    sine_a = jnp.where(lane < ROT // 2, -sine, 0.0)
    sine_b = jnp.where((lane >= ROT // 2) & (lane < ROT), sine, 0.0)

    def normed(values):
        centered = values - jnp.mean(values, axis=-1, keepdims=True)
        inverse = lax.rsqrt(jnp.mean(centered * centered, axis=-1, keepdims=True) + EPS)
        return centered * inverse, inverse

    unit = normed(hidden_group.astype(F32))[0]

    placed = kernel_call(
        functools.partial(place_kernel, deep),
        ((flat[1:] * 2, BF), ((n_dp * deep, width), BF), ((8, width), F32)) + (((2 * deep, group), BF),) * 4,
        attn_pieces + (dy,),
        scratch=(((n_dp * deep, width), F32), ((n_dp * deep, group), BF)),
        flops=2 * n_dp * deep * width * group,
    )
    weights, dense, vectors = placed[:3]
    by_chip_beyond = once(in_order(chip == 1, across, chip_beyond), weights)
    core_beyond = lax.ppermute(by_chip_beyond, "seq", CORE_SWAP)
    hidden_other, dy_other = whole_group(by_chip_beyond, core_beyond)
    unit_other = normed(hidden_other.astype(F32))[0]
    d_blocks = seq_shuffle(placed[3:])
    attn_in, qk, v = kernel_call(
        project_kernel,
        ((flat, BF), ((group, 2 * own), BF), ((group, own), BF)),
        (unit, weights, vectors, cosine, sine_a, sine_b),
        flops=2 * group * width * width,
    )
    attended = kernel_call(
        with_waits(1, functools.partial(attention_kernel, deep)),
        (((2 * deep, group), BF),) * 4 + ((flat, BF),),
        (mlp_pair, qk, v, *d_blocks, segment[:, None], segment[None, :], cosine, sine_a, sine_b),
        scratch=(((own, group), F32),) * 4 + ((flat, F32),),
        flops=14 * group * group * own,
        megabytes=16,
        apart=1,
    )
    d_joined = attended[4]
    held_shapes = ((flat, BF), ((group, half), BF), ((group, half), BF))
    give, keep, *held_other, up_full, down_full = kernel_call(
        with_waits(1, mlp_kernel),
        (((2, rows, 2 * width), BF),) * 2 + held_shapes + (((8, width), F32), ((width, half), BF), ((half, width), BF)),
        (d_joined, down_two, down_pair, mlp_two, mlp_pair, unit_other, dy_other, vectors),
        scratch=(pltpu.SemaphoreType.DMA((12,)),),
        flops=4 * group * width * 2 * half,
        megabytes=16,
        apart=5,
    )
    row_blocks = seq_shuffle(attended[:4])

    own_pair, *held_own = kernel_call(
        with_waits(1, mlp_own_kernel),
        (((4, rows, 2 * width), BF),) + held_shapes + (((8, width), F32),),
        (d_joined, unit, dy, vectors, up_full, down_full),
        flops=4 * group * width * 2 * half,
        megabytes=16,
        apart=1,
    )
    attn_send, attn_keep, own_give, own_keep = kernel_call(
        functools.partial(attention_grads_kernel, deep),
        (((4, per_line + 8, width), BF),) * 2 + (((2, rows, 2 * width), BF),) * 2,
        (*row_blocks, dense, dy, attn_in, d_joined, weights, unit, vectors, own_pair),
        scratch=(((n_dp * deep, group), BF), ((width, width), F32), ((8, width), F32)),
        flops=5 * group * width * width,
        megabytes=16,
    )
    up_shape, down_shape = ((2, units + 8, width), BF), ((2, units, width), BF)
    keep_up, send_up, keep_down, send_down = kernel_call(
        with_waits(1, mlp_grads_kernel),
        (up_shape, up_shape, down_shape, down_shape),
        (attn_send, *held_own[:3], dy, held_own[3], *held_other[:3], dy_other, held_other[3]),
        scratch=(((width, half), BF), ((half, width), BF)),
        flops=4 * group * width * 2 * half,
        megabytes=16,
        apart=1,
    )

    attn_moved = lax.ppermute(attn_send, "dp", SIDE_SWAP)
    up_got = lax.ppermute(send_up, "dp", PAIR_SWAP)
    down_got = lax.ppermute(send_down, "dp", PAIR_SWAP)
    both = keep.astype(F32) + lax.ppermute(once(give, keep_up), "seq", CORE_SWAP).astype(F32)
    both = both.astype(BF)
    first = (attn_moved, up_got, down_got, both)
    up_mine, up_send = add_blocks(keep_up, up_got, 1, 1)
    up_last = lax.ppermute(once(up_send, *first), "dp", HALF_SWAP)
    attn_mine, attn_send = add_blocks(attn_keep, attn_moved, 2, 2)
    attn_got = lax.ppermute(once(attn_send, *first), "dp", PAIR_SWAP)
    down_mine, down_send = add_blocks(keep_down, down_got, 1, 1)
    down_last = lax.ppermute(once(down_send, *first), "dp", HALF_SWAP)
    beyond = lax.ppermute(once(both, *first), "dp", SIDE_SWAP)
    attn_mine, attn_send = add_blocks(attn_mine, attn_got, 1, 1, waits=(up_last,))
    attn_last = lax.ppermute(attn_send, "dp", HALF_SWAP)

    both = own_keep.astype(F32) + lax.ppermute(own_give, "seq", CORE_SWAP).astype(F32) + beyond.astype(F32)
    chip_last = lax.ppermute(pick(both, 1 - chip).astype(BF), "seq", CHIP_SWAP)
    pair = pick(both, chip) + chip_last.astype(F32)
    x = hidden_in.astype(F32)
    block_out = x + vectors[4] + vectors[5] + pair[:, :width]
    upstream = pair[:, width:]
    own_unit, inverse = normed(x)
    inner = (
        upstream
        - jnp.mean(upstream, axis=-1, keepdims=True)
        - own_unit * jnp.mean(upstream * own_unit, axis=-1, keepdims=True)
    )
    grad_in = grad_out.astype(F32) + inverse * inner

    up_keep, up_give, tail = kernel_call(
        with_waits(1, up_sum_kernel),
        (((per_line, half), BF), ((per_line + 16, half), BF), ((8, width), F32)),
        (attn_got, up_mine, up_last),
        megabytes=8,
        apart=1,
    )
    down_own = down_mine[0].astype(F32) + down_last[0].astype(F32)
    up_far = lax.ppermute(up_give, "dp", SIDE_SWAP)
    blocks = kernel_call(
        with_waits(1, functools.partial(owners_kernel, deep)),
        (((deep + 8, width), BF),) * 4,
        (attn_last, up_keep, up_far, tail),
        scratch=(((per_line, width), F32),),
        megabytes=8,
        apart=1,
    )
    up_own, vec_own = kernel_call(
        with_waits(2, functools.partial(owned_kernel, deep)),
        (((deep, hidden_units), F32), ((8, 128), F32)),
        (chip_last, attn_last, *seq_shuffle(blocks), tail),
        scratch=(((4, deep + 8, width), F32),),
        megabytes=8,
        apart=2,
    )
    *blocks, dense_own = kernel_call(
        with_waits(1, functools.partial(attention_sum_kernel, deep)),
        (((deep + 8, width), BF),) * 4 + (((deep, width), F32),),
        (up_far, attn_mine, attn_last),
        scratch=(((per_line + 8, width), F32),),
        megabytes=8,
        apart=1,
    )
    qkv_own, vec_attn = kernel_call(
        with_waits(1, functools.partial(attention_owned_kernel, deep)),
        (((deep, 3 * width), F32), ((8, 128), F32)),
        (chip_last, *seq_shuffle(blocks)),
        scratch=(((4, deep + 8, width), F32), ((8, 3 * width), F32)),
        megabytes=8,
        apart=1,
    )
    by_width = vec_own[:5, :deep]
    qkv_bias_grad = vec_attn[5, : 3 * deep]
    up_bias_grad = vec_own[6, :units]
    return (
        block_out.astype(BF),
        grad_in.astype(BF),
        vec_attn[0, :deep],
        vec_attn[1, :deep],
        by_width[2],
        by_width[3],
        qkv_own,
        qkv_bias_grad,
        dense_own,
        by_width[4],
        up_own,
        up_bias_grad,
        down_own,
        by_width[4],
    )


def per_device(*args):
    if lax.axis_size("dp") == 8 and lax.axis_size("seq") == 4:
        return line_device(*args)
    return general_device(*args)


def solution(mesh):
    both = ("dp", "seq")
    matrix, vector = P(both, None), P(both)
    params = (vector, vector, vector, vector, matrix, vector, matrix, vector, matrix, vector, matrix, vector)
    return jax.shard_map(
        per_device,
        mesh=mesh,
        in_specs=(matrix, P("dp", None), matrix) + params,
        out_specs=(matrix, matrix) + params,
        check_vma=False,
    )
```

```python
import functools

import jax
import jax.numpy as jnp
from jax import lax
from jax.experimental import pallas as pl
from jax.experimental.pallas import tpu as pltpu
from jax.sharding import PartitionSpec as P

HEADS = 12
HEAD_DIM = 64
ROT = 16
EPS = 1e-05
NEGATIVE = -1e30
BF = jnp.bfloat16
F32 = jnp.float32


def dot(spec, a, b):
    return jnp.einsum(spec, a, b, preferred_element_type=F32)


def frequencies():
    steps = jnp.arange(ROT // 2, dtype=F32)
    return jnp.power(F32(10000.0), -(2.0 * steps) / ROT)


def rotate(values, cosine, sine, sign):
    half = ROT // 2
    first = values[..., :half]
    second = values[..., half:ROT]
    turned_one = first * cosine - sign * second * sine
    turned_two = second * cosine + sign * first * sine
    return jnp.concatenate([turned_one, turned_two, values[..., ROT:]], axis=-1)


def place(row_lengths, index):
    ends = jnp.cumsum(row_lengths)
    after = (index[:, None] >= ends[None, :]).astype(jnp.int32)
    segment = jnp.sum(after, axis=1)
    start = jnp.sum(after * row_lengths[None, :], axis=1)
    return (segment, index - start)


def pick(values, index):
    return lax.dynamic_index_in_dim(values, index, 0, keepdims=False)


CHIP_SWAP = [(0, 2), (2, 0), (1, 3), (3, 1)]
CORE_SWAP = [(0, 1), (1, 0), (2, 3), (3, 2)]


def in_order(second, mine, other, axis=0):
    return jnp.stack([jnp.where(second, other, mine), jnp.where(second, mine, other)], axis=axis)


def seq_exchange(blocks):
    n = lax.axis_size("seq")
    if n != 4:
        return lax.all_to_all(blocks, "seq", 0, 0)
    me = lax.axis_index("seq")
    chip, core = me // 2, me % 2
    halves = blocks.reshape((2, 2) + blocks.shape[1:])
    far = lax.ppermute(pick(halves, 1 - chip), "seq", CHIP_SWAP)
    by_chip = in_order(chip == 1, pick(halves, chip), far, axis=1)
    other = lax.ppermute(pick(by_chip, 1 - core), "seq", CORE_SWAP)
    return in_order(core == 1, pick(by_chip, core), other, axis=1).reshape(blocks.shape)


def seq_gather(values):
    n = lax.axis_size("seq")
    if n != 4:
        return lax.all_gather(values, "seq", axis=0)
    me = lax.axis_index("seq")
    chip, core = me // 2, me % 2
    far = lax.ppermute(values, "seq", CHIP_SWAP)
    mine = in_order(chip == 1, values, far)
    other = lax.ppermute(mine, "seq", CORE_SWAP)
    return in_order(core == 1, mine, other, axis=1).reshape((n,) + values.shape)


def seq_reduce(values):
    n = lax.axis_size("seq")
    if n != 4:
        return lax.psum_scatter(values.astype(BF), "seq", scatter_dimension=0).astype(F32)
    me = lax.axis_index("seq")
    chip, core = me // 2, me % 2
    parts = values.reshape((2, 2) + values.shape[1:])
    keep = lax.dynamic_index_in_dim(parts, core, 1, keepdims=False)
    give = lax.dynamic_index_in_dim(parts, 1 - core, 1, keepdims=False).astype(BF)
    both = keep.astype(F32) + lax.ppermute(give, "seq", CORE_SWAP).astype(F32)
    far = lax.ppermute(pick(both, 1 - chip).astype(BF), "seq", CHIP_SWAP)
    return pick(both, chip) + far.astype(F32)


SIDE_SWAP = [(i, i ^ 1) for i in range(8)]


def along(step):
    return [(i, (i + 2 * step) % 8) for i in range(8)]


def dp_gather(block):
    n = lax.axis_size("dp")
    if n != 8:
        return lax.all_gather(block, "dp", axis=0)
    me = lax.axis_index("dp")
    line, side = me // 2, me % 2
    near1 = lax.ppermute(block, "dp", along(1))
    near3 = lax.ppermute(block, "dp", along(3))
    near2 = lax.ppermute(block, "dp", along(2))
    far0 = lax.ppermute(block, "dp", SIDE_SWAP)
    far13 = lax.ppermute(jnp.stack([near1, near3]), "dp", SIDE_SWAP)
    far2 = lax.ppermute(near2, "dp", SIDE_SWAP)
    full = jnp.zeros((4, 2) + block.shape, block.dtype)
    zero = jnp.int32(0)
    for step, near, far in ((0, block, far0), (1, near1, far13[0]), (3, near3, far13[1]), (2, near2, far2)):
        pair = in_order(side == 1, near, far)
        full = lax.dynamic_update_slice(full, pair[None], ((line - step) % 4, zero, zero, zero))
    return full.reshape((n,) + block.shape)


def dp_reduce(block_of):
    n = lax.axis_size("dp")
    if n != 8:
        blocks = jnp.stack([block_of(jnp.int32(i)).astype(BF) for i in range(n)])
        return lax.psum_scatter(blocks, "dp", scatter_dimension=0).astype(F32)
    me = lax.axis_index("dp")
    line, side = me // 2, me % 2

    def over_side(*steps):
        targets = [2 * ((line + step) % 4) for step in steps]
        moved = lax.ppermute(jnp.stack([block_of(t + 1 - side) for t in targets]), "dp", SIDE_SWAP)
        return [block_of(t + side).astype(F32) + moved[j].astype(F32) for j, t in enumerate(targets)]

    (sum2,) = over_side(2)
    sum1, sum3 = over_side(1, 3)
    (sum0,) = over_side(0)
    got2 = lax.ppermute(sum2.astype(BF), "dp", along(2)).astype(F32)
    got1 = lax.ppermute(sum1.astype(BF), "dp", along(1)).astype(F32)
    got3 = lax.ppermute(sum3.astype(BF), "dp", along(3)).astype(F32)
    return sum0 + got1 + got2 + got3


def attention(queries, keys, values, d_out, segment, scale):
    tokens = queries.shape[1]
    index = jnp.arange(tokens, dtype=jnp.int32)
    allowed = (segment[:, None] == segment[None, :]) & (index[None, :] <= index[:, None])
    scores = dot("htd,hnd->htn", queries, keys) * scale
    masked = jnp.where(allowed[None], scores, NEGATIVE)
    top = jnp.max(masked, axis=-1, keepdims=True)
    weights = jnp.where(allowed[None], jnp.exp(masked - top), 0.0)
    probs = weights / jnp.sum(weights, axis=-1, keepdims=True)
    probs_r = probs.astype(BF)
    attended = dot("htn,hnd->htd", probs_r, values)
    d_probs = dot("htd,hnd->htn", d_out, values)
    delta = jnp.sum(probs * d_probs, axis=-1, keepdims=True)
    d_scores = (probs * (d_probs - delta)).astype(BF)
    d_queries = dot("htn,hnd->htd", d_scores, keys) * scale
    d_keys = dot("htn,htd->hnd", d_scores, queries) * scale
    d_values = dot("htn,htd->hnd", probs_r, d_out)
    return attended, d_queries, d_keys, d_values


def general_device(
    hidden_in,
    lengths,
    grad_out,
    attn_gain,
    attn_shift,
    mlp_gain,
    mlp_shift,
    qkv_weight,
    qkv_bias,
    dense_weight,
    dense_bias,
    up_weight,
    up_bias,
    down_weight,
    down_bias,
):
    n_dp, n_seq = lax.axis_size("dp"), lax.axis_size("seq")
    me = lax.axis_index("seq")
    rows, width = hidden_in.shape
    group = rows * n_seq
    scale = HEAD_DIM ** (-0.5)
    hidden_units = up_weight.shape[1]
    own_units = hidden_units // n_seq
    deep = width // (n_dp * n_seq)
    unit_rows = hidden_units // (n_dp * n_seq)
    heads = -(-HEADS // n_seq)
    own = heads * HEAD_DIM
    spare = heads * n_seq - HEADS

    def by_head(values):
        lead = values.shape[:-1]
        split = values.reshape(lead + (3, HEADS, HEAD_DIM))
        if spare:
            split = jnp.pad(split, [(0, 0)] * (len(lead) + 1) + [(0, spare), (0, 0)])
        split = split.reshape(lead + (3, n_seq, own))
        return jnp.moveaxis(split, -2, 0).reshape((n_seq,) + lead + (3 * own,))

    def from_heads(blocks):
        lead = blocks.shape[1:-1]
        split = jnp.moveaxis(blocks.reshape((n_seq,) + lead + (3, own)), 0, -2)
        split = split.reshape(lead + (3, HEADS + spare, HEAD_DIM))[..., :HEADS, :]
        return split.reshape(lead + (3 * width,))

    vectors = (attn_gain, attn_shift, mlp_gain, mlp_shift, qkv_bias, dense_bias, up_bias, down_bias)
    sizes = [v.shape[0] for v in vectors]
    length = sum(sizes)
    wide = own_units + 3 * own
    up_blocks = jnp.moveaxis(up_weight.reshape(deep, n_dp, n_seq, unit_rows), 2, 0)
    up_blocks = up_blocks.reshape(n_seq, deep, own_units)
    vector = jnp.pad(jnp.concatenate(vectors), (0, wide - length))
    blocks = jnp.concatenate(
        [
            jnp.concatenate([up_blocks, by_head(qkv_weight)], axis=2),
            jnp.broadcast_to(vector, (n_seq, 1, wide)),
        ],
        axis=1,
    )
    got = seq_exchange(blocks)
    per_line = n_seq * deep
    up_rows = per_line * own_units // width
    up_piece = got[:, :deep, :own_units].reshape(up_rows, width)
    qkv_piece = got[:, :deep, own_units:].reshape(per_line, 3 * own)
    group_vector = got[:, deep, :length]

    both = seq_gather(jnp.concatenate([hidden_in, grad_out], axis=0))
    hidden_group = both[:, :rows].reshape(group, width)
    grad_group = both[:, rows:].reshape(group, width)

    def beside(values):
        lead = values.shape[:-2]
        split = values.reshape(lead + (deep, n_seq, width // n_seq))
        return jnp.swapaxes(split, -3, -2).reshape(lead + (per_line, width // n_seq))

    def from_beside(values):
        lead = values.shape[:-2]
        split = values.reshape(lead + (n_seq, deep, width // n_seq))
        return jnp.swapaxes(split, -3, -2).reshape(lead + (deep, width))

    attn_wide = 3 * own + width // n_seq
    vec_rows = -(-n_seq * length // attn_wide)
    vec_rows += -vec_rows % 8
    vec_piece = jnp.pad(group_vector.reshape(-1), (0, vec_rows * attn_wide - n_seq * length))
    attn_piece = jnp.concatenate([qkv_piece, beside(dense_weight)], axis=1)
    attn_piece = jnp.concatenate([attn_piece, vec_piece.reshape(vec_rows, attn_wide)], axis=0)
    attn_all = dp_gather(attn_piece)
    mlp_all = dp_gather(jnp.concatenate([up_piece, down_weight], axis=0))
    qkv_full = attn_all[:, :per_line, : 3 * own].reshape(width, 3 * own)
    dense_rows = from_beside(attn_all[:, :per_line, 3 * own :]).reshape(n_dp * deep, width)
    up_full = mlp_all[:, :up_rows].reshape(width, own_units)
    down_full = mlp_all[:, up_rows:].reshape(own_units, width)
    every = attn_all[:, per_line:].reshape(n_dp, vec_rows * attn_wide)[:, : n_seq * length]
    every = every.reshape(n_dp * n_seq, length).astype(F32)
    whole = []
    start = 0
    for size in sizes:
        whole.append(every[:, start : start + size].reshape(-1))
        start += size
    f_attn_gain, f_attn_shift, f_mlp_gain, f_mlp_shift, f_qkv_bias, f_dense_bias, f_up_bias, f_down_bias = whole
    own_qkv_bias = pick(by_head(f_qkv_bias), me)
    own_up_bias = lax.dynamic_index_in_dim(
        f_up_bias.reshape(n_dp, n_seq, unit_rows), me, 1, keepdims=False
    ).reshape(-1)

    row_lengths = lengths[0]
    index = jnp.arange(group, dtype=jnp.int32)
    segment, position = place(row_lengths, index)
    angles = position.astype(F32)[:, None] * frequencies()[None, :]
    cosine = jnp.cos(angles)[:, None, :]
    sine = jnp.sin(angles)[:, None, :]

    tokens = hidden_group.astype(F32)
    center = jnp.mean(tokens, axis=-1, keepdims=True)
    centered = tokens - center
    spread = jnp.mean(centered * centered, axis=-1, keepdims=True)
    unit = centered * lax.rsqrt(spread + EPS)
    attn_in = (unit * f_attn_gain + f_attn_shift).astype(BF)
    mlp_in = (unit * f_mlp_gain + f_mlp_shift).astype(BF)

    joined = dot("td,de->te", attn_in, qkv_full) + own_qkv_bias
    joined = joined.reshape(group, 3, heads, HEAD_DIM)
    queries = jnp.moveaxis(rotate(joined[:, 0], cosine, sine, 1.0).astype(BF), 1, 0)
    keys = jnp.moveaxis(rotate(joined[:, 1], cosine, sine, 1.0).astype(BF), 1, 0)
    values = jnp.moveaxis(joined[:, 2].astype(BF), 1, 0)
    feature_rows = n_dp * deep
    direct = spare == 0 and own % per_line == 0
    d_rows = dot("fe,te->ft", dense_rows, grad_group).astype(BF)
    if direct:
        runs = own // per_line
        moved = seq_exchange(d_rows.reshape(n_seq, runs * deep, group))
        moved = moved.reshape(n_seq, runs, deep, group)
        d_attended = jnp.moveaxis(moved, 0, 1).reshape(heads, HEAD_DIM, group)
    else:
        moved = lax.all_gather(d_rows.reshape(n_dp, deep, group), "seq", axis=1)
        moved = moved.reshape(width, group)
        moved = jnp.pad(moved, ((0, spare * HEAD_DIM), (0, 0)))
        d_attended = pick(moved.reshape(n_seq, heads, HEAD_DIM, group), me)
    d_attended = jnp.swapaxes(d_attended, 1, 2)
    attended, d_queries, d_keys, d_values = attention(queries, keys, values, d_attended, segment, scale)
    attended = jnp.swapaxes(attended.astype(BF), 1, 2).reshape(own, group)
    if direct:
        given = jnp.moveaxis(attended.reshape(runs, n_seq, deep, group), 1, 0)
        rows_attended = seq_exchange(given.reshape(n_seq, runs * deep, group)).reshape(feature_rows, group)
    else:
        given = lax.all_gather(attended, "seq", axis=0, tiled=True)[:width]
        rows_attended = lax.dynamic_index_in_dim(
            given.reshape(n_dp, n_seq, deep, group), me, 1, keepdims=False
        ).reshape(feature_rows, group)
    attn_out = dot("ft,fe->te", rows_attended, dense_rows)
    dense_grad = dot("ft,te->fe", rows_attended, grad_group).astype(BF).reshape(n_dp, deep, width)
    d_queries = rotate(jnp.moveaxis(d_queries, 0, 1), cosine, sine, -1.0)
    d_keys = rotate(jnp.moveaxis(d_keys, 0, 1), cosine, sine, -1.0)
    d_joined = jnp.stack([d_queries, d_keys, jnp.moveaxis(d_values, 0, 1)], axis=1)
    d_joined = d_joined.astype(BF).reshape(group, 3 * own)
    qkv_grad = dot("td,te->de", attn_in, d_joined).astype(BF).reshape(n_dp, n_seq * deep, 3 * own)
    d_attn_in = dot("te,de->td", d_joined, qkv_full)
    attn_terms = jnp.concatenate([qkv_grad, beside(dense_grad)], axis=2)
    attn_sum = dp_reduce(lambda i: pick(attn_terms, i))

    upper = dot("td,df->tf", mlp_in, up_full) + own_up_bias
    cdf = 0.5 * (1.0 + lax.erf(upper * F32(0.7071067811865476)))
    pdf = jnp.exp(-0.5 * upper * upper) * F32(0.3989422804014327)
    act = (upper * cdf).astype(BF)
    d_act = dot("td,fd->tf", grad_group, down_full)
    d_up = (d_act * (cdf + upper * pdf)).astype(BF)
    down_grad = dot("tf,td->fd", act, grad_group).astype(BF).reshape(n_dp, unit_rows, width)
    up_grad = dot("td,tf->df", mlp_in, d_up).astype(BF).reshape(n_dp, up_rows, width)
    mlp_out = dot("tf,fd->td", act, down_full)
    d_mlp_in = dot("tf,df->td", d_up, up_full)

    mine = jnp.arange(n_seq) == me
    qkv_bias_grad = jnp.sum(d_joined.astype(F32), axis=0)
    qkv_bias_grad = from_heads(jnp.where(mine[:, None], qkv_bias_grad[None], 0.0))
    up_bias_grad = jnp.sum(d_up.astype(F32), axis=0).reshape(n_dp, 1, unit_rows)
    up_bias_grad = jnp.where(mine[None, :, None], up_bias_grad, 0.0)
    bias_sum = jnp.sum(grad_out.astype(F32), axis=0)
    terms = (
        jnp.sum(d_attn_in * unit, axis=0),
        jnp.sum(d_attn_in, axis=0),
        jnp.sum(d_mlp_in * unit, axis=0),
        jnp.sum(d_mlp_in, axis=0),
        qkv_bias_grad,
        bias_sum,
        up_bias_grad,
        bias_sum,
    )
    terms = [t.reshape(n_dp, n_seq, size) for t, size in zip(terms, sizes)]
    terms = jnp.concatenate(terms, axis=2).reshape(n_dp, n_seq * length)
    tail_rows = -(-n_seq * length // width)
    tail_rows += -tail_rows % 8
    terms = jnp.pad(terms, ((0, 0), (0, tail_rows * width - n_seq * length)))
    terms = terms.reshape(n_dp, tail_rows, width).astype(BF)
    mlp_sum = dp_reduce(lambda i: jnp.concatenate([pick(up_grad, i), pick(down_grad, i), pick(terms, i)], axis=0))

    upstream = d_attn_in * f_attn_gain + d_mlp_in * f_mlp_gain
    pair = jnp.concatenate([(attn_out + mlp_out).astype(BF), upstream.astype(BF)], axis=1)
    pair = seq_reduce(pair.reshape(n_seq, rows, 2 * width))
    block_out = hidden_in.astype(F32) + f_dense_bias + f_down_bias + pair[:, :width]
    upstream = pair[:, width:]
    x = hidden_in.astype(F32)
    centered = x - jnp.mean(x, axis=-1, keepdims=True)
    inverse = lax.rsqrt(jnp.mean(centered * centered, axis=-1, keepdims=True) + EPS)
    own_unit = centered * inverse
    inner = (
        upstream
        - jnp.mean(upstream, axis=-1, keepdims=True)
        - own_unit * jnp.mean(upstream * own_unit, axis=-1, keepdims=True)
    )
    grad_in = grad_out.astype(F32) + inverse * inner

    qkv_back = attn_sum[:, : 3 * own].reshape(n_seq, deep, 3 * own).astype(BF)
    qkv_own = from_heads(seq_exchange(qkv_back).astype(F32))
    dense_own = from_beside(attn_sum[:, 3 * own :])
    vec_sum = mlp_sum[up_rows + unit_rows :].reshape(-1)[: n_seq * length].reshape(n_seq, 1, length)
    vec_sum = jnp.pad(vec_sum, ((0, 0), (0, 0), (0, -length % own_units)))
    vec_sum = vec_sum.reshape(n_seq, -1, own_units)
    back = jnp.concatenate([mlp_sum[:up_rows].reshape(n_seq, deep, own_units), vec_sum], axis=1)
    back = seq_exchange(back.astype(BF)).astype(F32)
    up_own = jnp.moveaxis(back[:, :deep].reshape(n_seq, deep, n_dp, unit_rows), 0, 2)
    vec_own = jnp.sum(back[:, deep:].reshape(n_seq, -1), axis=0)
    owned = []
    start = 0
    for size in sizes:
        owned.append(vec_own[start : start + size])
        start += size
    return (
        block_out.astype(BF),
        grad_in.astype(BF),
        owned[0],
        owned[1],
        owned[2],
        owned[3],
        qkv_own,
        owned[4],
        dense_own,
        owned[5],
        up_own.reshape(deep, hidden_units),
        owned[6],
        mlp_sum[up_rows : up_rows + unit_rows],
        owned[7],
    )


SCALE = HEAD_DIM**-0.5


def kernel_call(body, outs, args, scratch=(), megabytes=24, flops=0, apart=0):
    moved = sum(a.size * a.dtype.itemsize for a in args)
    held = [pl.BlockSpec(memory_space=pl.ANY)] * apart
    held += [pl.BlockSpec(memory_space=pltpu.VMEM)] * (len(args) - apart)
    return pl.pallas_call(
        body,
        out_shape=tuple(jax.ShapeDtypeStruct(shape, kind) for shape, kind in outs),
        in_specs=held,
        scratch_shapes=[pltpu.VMEM(*item) if isinstance(item, tuple) else item for item in scratch],
        compiler_params=pltpu.CompilerParams(vmem_limit_bytes=megabytes << 20),
        cost_estimate=pl.CostEstimate(flops=flops, bytes_accessed=moved, transcendentals=0),
    )(*args)


def dot_nn(a, b):
    return lax.dot_general(a, b, (((1,), (0,)), ((), ())), preferred_element_type=F32)


def dot_nt(a, b):
    return lax.dot_general(a, b, (((1,), (1,)), ((), ())), preferred_element_type=F32)


def dot_tn(a, b):
    return lax.dot_general(a, b, (((0,), (0,)), ((), ())), preferred_element_type=F32)


def line_and_side():
    me = lax.axis_index("dp")
    return lax.shift_right_logical(me, 1), lax.bitwise_and(me, 1)


PAIR_SWAP = [(i, i ^ 2) for i in range(8)]
HALF_SWAP = [(i, i ^ 4) for i in range(8)]
LINE_ORDER = (0, 2, 1, 3)


def dp_index(line, step, side):
    return 2 * lax.bitwise_xor(line, step) + side


def pick_blocks(block_of, send, keep):
    line, side = line_and_side()
    for j, step in enumerate(LINE_ORDER):
        send[j] = block_of(dp_index(line, step, 1 - side))
        keep[j] = block_of(dp_index(line, step, side))


def add_kernel(here, there, *out):
    place = 0
    for ref in out:
        for j in range(ref.shape[0]):
            ref[j] = (here[place + j].astype(F32) + there[place + j].astype(F32)).astype(ref.dtype)
        place += ref.shape[0]


def add_blocks(here, there, *counts, waits=()):
    shape = here.shape[1:]
    return kernel_call(
        with_waits(len(waits), add_kernel),
        tuple(((count,) + shape, BF) for count in counts),
        (*waits, here, there),
        megabytes=8,
        apart=len(waits),
    )


def once(values, *others):
    return lax.optimization_barrier((values, *others))[0]


def seq_shuffle(blocks):
    got = [blocks[0]]
    for other in (1, 2, 3):
        pairs = [(i, i ^ other) for i in range(4)]
        got.append(lax.ppermute(blocks[other], "seq", pairs))
    return got


def place_kernel(deep, *refs):
    pieces, (dy, weights, dense, vectors), d_blocks, (rows32, d_rows) = refs[:4], refs[4:8], refs[8:12], refs[12:]
    line, side = line_and_side()
    per_line = 4 * deep
    quarter = dy.shape[1] // 4
    own = weights.shape[1] - quarter
    total = jnp.zeros(vectors.shape, F32)
    for place in range(8):
        piece = pieces[place // 2].at[place % 2]
        owner = dp_index(line, LINE_ORDER[place % 4], side if place < 4 else 1 - side)
        weights[pl.ds(pl.multiple_of(owner * per_line, per_line), per_line), :] = piece[:per_line, :]
        total = total + piece[per_line:, :].astype(F32)
        beside = piece[:per_line, own:].astype(F32)
        for q in range(4):
            rows32[pl.ds(pl.multiple_of(owner * deep, 8), deep), q * quarter : (q + 1) * quarter] = beside[
                q * deep : (q + 1) * deep
            ]
    vectors[...] = total
    dense[...] = rows32[...].astype(BF)
    d_rows[...] = dot_nt(dense[...], dy[...]).astype(BF)
    me = lax.axis_index("seq")
    count = d_blocks[0].shape[0]
    for j in range(4):
        d_blocks[j][...] = d_rows[pl.ds(pl.multiple_of(lax.bitwise_xor(me, j) * count, 16), count), :]


def turn(values, cosine, sine_a, sine_b, sign):
    half = ROT // 2
    ahead = pltpu.roll(values, 128 - half, 1)
    behind = pltpu.roll(values, half, 1)
    return values * cosine + sign * (ahead * sine_a + behind * sine_b)


def project_kernel(unit, weights, vectors, cosine, sine_a, sine_b, attn_in, qk, v):
    gain, shift, bias = vectors[0:1, :], vectors[1:2, :], vectors[6:7, :]
    turned = qk.shape[1]
    size = 128

    def step(i, carry):
        rows = pl.ds(pl.multiple_of(i * size, size), size)
        normed = (unit[rows, :] * gain + shift).astype(BF)
        attn_in[rows, :] = normed
        joined = dot_nn(normed, weights[...]) + bias
        tables = cosine[rows, :], sine_a[rows, :], sine_b[rows, :]
        for c in range(0, turned, 128):
            qk[rows, c : c + 128] = turn(joined[:, c : c + 128], *tables, 1.0).astype(BF)
        v[rows, :] = joined[:, turned : turned + v.shape[1]].astype(BF)
        return carry

    lax.fori_loop(0, unit.shape[0] // size, step, 0)


def attention_kernel(deep, *refs):
    qk, v, d0, d1, d2, d3, seg_column, seg_row, cosine, sine_a, sine_b = refs[:11]
    given, d_joined, (d_t, out_t, dk_t, dv_t, acc) = refs[11:15], refs[15], refs[16:]
    tokens, own = v.shape
    me = lax.axis_index("seq")
    runs = own // (4 * deep)
    for j, ref in enumerate((d0, d1, d2, d3)):
        source = lax.bitwise_xor(me, j)
        block = ref[...].astype(F32)
        for r in range(runs):
            place = pl.multiple_of(r * 4 * deep + source * deep, 8)
            d_t[pl.ds(place, deep), :] = block[r * deep : (r + 1) * deep]
    d_out = jnp.transpose(d_t[...]).astype(BF)
    q_t = jnp.transpose(qk[:, :own].astype(F32)).astype(BF)
    d_tb = d_t[...].astype(BF)
    dk_t[...] = jnp.zeros(dk_t.shape, F32)
    dv_t[...] = jnp.zeros(dv_t.shape, F32)
    size = 256
    for h in range(own // HEAD_DIM):
        lanes = slice(h * HEAD_DIM, (h + 1) * HEAD_DIM)
        q_h = qk[:, lanes]
        k_h = qk[:, own + h * HEAD_DIM : own + (h + 1) * HEAD_DIM]
        v_h = v[:, lanes]
        d_h = d_out[:, lanes]
        for first in range(0, tokens, size):
            rows = slice(first, first + size)
            n = first + size
            scores = dot_nt(q_h[rows] * SCALE, k_h[:n])
            query = lax.broadcasted_iota(jnp.int32, (size, n), 0) + first
            key = lax.broadcasted_iota(jnp.int32, (size, n), 1)
            allowed = (seg_column[rows, :] == seg_row[:, :n]) & (key <= query)
            scores = jnp.where(allowed, scores, NEGATIVE)
            weights = jnp.exp(scores - jnp.max(scores, axis=1, keepdims=True))
            probs = weights * (1.0 / jnp.sum(weights, axis=1, keepdims=True))
            probs_r = probs.astype(BF)
            out_t[lanes, rows] = jnp.transpose(dot_nn(probs_r, v_h[:n]))
            d_probs = dot_nt(d_h[rows], v_h[:n])
            delta = jnp.sum(probs * d_probs, axis=1, keepdims=True)
            d_scores = (probs * (d_probs - delta)).astype(BF)
            acc[rows, lanes] = dot_nn(d_scores, k_h[:n]) * SCALE
            dk_t[lanes, :n] += dot_nn(q_t[lanes, rows], d_scores)
            dv_t[lanes, :n] += dot_nn(d_tb[lanes, rows], probs_r)
    acc[:, own : 2 * own] = jnp.transpose(dk_t[...]) * SCALE
    for c in range(0, 2 * own, 128):
        turned = turn(acc[:, c : c + 128], cosine[...], sine_a[...], sine_b[...], -1.0)
        d_joined[:, c : c + 128] = turned.astype(BF)
    d_joined[:, 2 * own : 3 * own] = jnp.transpose(dv_t[...]).astype(BF)
    d_joined[:, 3 * own :] = jnp.zeros((tokens, d_joined.shape[1] - 3 * own), BF)
    for j in range(4):
        target = lax.bitwise_xor(me, j)
        parts = [out_t[pl.ds(pl.multiple_of(r * 4 * deep + target * deep, 8), deep), :] for r in range(runs)]
        given[j][...] = jnp.concatenate(parts, axis=0).astype(BF)


def attention_grads_kernel(deep, *refs):
    r0, r1, r2, r3, dense, dy, attn_in, d_joined, weights, unit, vectors, own_pair = refs[:12]
    picks, (give, keep), (rows_t, grads, sums) = refs[12:14], refs[14:16], refs[16:]
    me = lax.axis_index("seq")
    core = lax.bitwise_and(me, 1)
    count = r0.shape[0]
    width = dy.shape[1]
    quarter = width // 4
    own = width - quarter
    for j, ref in enumerate((r0, r1, r2, r3)):
        rows_t[pl.ds(pl.multiple_of(lax.bitwise_xor(me, j) * count, 16), count), :] = ref[...]
    attended = jnp.transpose(rows_t[...].astype(F32)).astype(BF)
    gain = vectors[0:1, :]
    size = dy.shape[0] // 4
    sums[...] = jnp.zeros(sums.shape, F32)
    for i in range(4):
        rows = slice(i * size, (i + 1) * size)
        out = dot_nn(attended[rows], dense[...]) + own_pair[i, :, :width].astype(F32)
        back = dot_nt(d_joined[rows, :], weights[...])
        sums[0:1, :] += jnp.sum(back * unit[rows, :], axis=0, keepdims=True)
        sums[1:2, :] += jnp.sum(back, axis=0, keepdims=True)
        sums[5:6, :] += jnp.sum(d_joined[rows, :].astype(F32), axis=0, keepdims=True)
        out = out.astype(BF)
        back = (back * gain + own_pair[i, :, width:].astype(F32)).astype(BF)

        @pl.when(core == i % 2)
        def _():
            keep[i // 2, :, :width] = out
            keep[i // 2, :, width:] = back

        @pl.when(core != i % 2)
        def _():
            give[i // 2, :, :width] = out
            give[i // 2, :, width:] = back

    for c in range(0, width, 128):
        grads[c : c + 128, :] = dot_tn(attn_in[:, c : c + 128], d_joined[...])
    dense_grad = dot_nn(rows_t[...], dy[...])
    for p in range(8):
        for q in range(4):
            start = p * 4 * deep + q * deep
            grads[start : start + deep, own:] = dense_grad[p * deep : (p + 1) * deep, q * quarter : (q + 1) * quarter]
    per_line = 4 * deep
    tail = sums[...]

    def block_of(index):
        block = grads[pl.ds(pl.multiple_of(index * per_line, per_line), per_line), :]
        return jnp.concatenate([block, tail], axis=0).astype(BF)

    pick_blocks(block_of, *picks)


def pack_kernel(deep, *refs):
    qkv, up, by_width, qkv_bias, x, dy, blocks, mine, (all_blocks, row_block) = *refs[:6], refs[6:10], *refs[10:11], refs[11:]
    width = qkv.shape[1] // 3
    own = width // 4
    units = up.shape[1] // 32
    me = lax.axis_index("seq")
    device = 4 * lax.axis_index("dp") + me
    row_block[...] = jnp.zeros(row_block.shape, F32)
    row_block[:6, :deep] = by_width[...].astype(F32)
    vectors = pltpu.roll(row_block[:, :width], device * deep, 1)
    row_block[0:6, :] = jnp.zeros((6, row_block.shape[1]), F32)
    row_block[6:7, : 3 * deep] = qkv_bias[...].astype(F32)
    bias_rows = pltpu.roll(row_block[...], device * (3 * deep), 1)
    up_values, qkv_values = up[...].astype(F32), qkv[...].astype(F32)
    empty = jnp.zeros((deep + 8, own), F32)
    both = jnp.concatenate([qkv_values, bias_rows], axis=0)
    for t in range(4):
        parts = [up_values[:, ((l * 2 + y) * 4 + t) * units :][:, :units] for y in range(2) for l in range(4)]
        all_blocks[t, :deep, :] = jnp.concatenate(parts, axis=1)
        parts = [both[:, part * width + t * own : part * width + (t + 1) * own] for part in range(3)]
        parts = jnp.concatenate(parts + [empty], axis=1)
        all_blocks[t, deep : 2 * deep, :] = parts[:deep]
        all_blocks[t, 2 * deep :, :] = parts[deep:] + vectors
    rows = x.shape[0]
    for j in range(4):
        blocks[j][...] = all_blocks[lax.bitwise_xor(me, j)].astype(BF)
    mine[:rows, :] = x[...]
    mine[rows:, :] = dy[...]


def unpack_kernel(deep, r0, r1, r2, r3, dense, up_bias, attn_piece, up_keep, up_give, up32, qkv32, row_block):
    me = lax.axis_index("seq")
    line, side = line_and_side()
    width = dense.shape[1]
    quarter = width // 4
    half = up_keep.shape[1]
    own = 3 * quarter
    extra = jnp.zeros((8, width), F32)
    for j, ref in enumerate((r0, r1, r2, r3)):
        block = ref[...].astype(F32)
        place = pl.ds(pl.multiple_of(lax.bitwise_xor(me, j) * deep, 8), deep)
        up32[place, :] = block[:deep]
        qkv32[place, :] = block[deep : 2 * deep]
        extra = extra + block[2 * deep :]
    rows = 4 * deep
    first, second = up32[:, :half], up32[:, half:]
    up_keep[...] = jnp.where(side == 0, first, second).astype(BF)
    up_give[...] = jnp.where(side == 0, second, first).astype(BF)
    attn_piece[:rows, :own] = qkv32[:, :own].astype(BF)
    dense_values = dense[...].astype(F32)
    beside = [dense_values[:, q * quarter : (q + 1) * quarter] for q in range(4)]
    attn_piece[:rows, own:] = jnp.concatenate(beside, axis=0).astype(BF)
    units = half // 4
    row_block[...] = jnp.zeros(row_block.shape, F32)
    row_block[7:8, :units] = up_bias[...].astype(F32)
    attn_piece[rows:, :] = (extra + pltpu.roll(row_block[...], side * half + line * units, 1)).astype(BF)


def mlp_tokens(unit, dy, vectors, up, down, mlp_in, act, d_up, sums, side, store):
    half = up.shape[1]
    gain, shift = vectors[2:3, :], vectors[3:4, :]
    bias = jnp.where(side == 0, vectors[7:8, :half], vectors[7:8, half:])
    sums[...] = jnp.zeros(sums.shape, F32)
    size = unit.shape[0] // 4

    def step(i, carry):
        rows = pl.ds(pl.multiple_of(i * size, size), size)
        u = unit[rows, :]
        normed = (u * gain + shift).astype(BF)
        mlp_in[rows, :] = normed
        upper = dot_nn(normed, up[...]) + bias
        cdf = 0.5 * (1.0 + lax.erf(upper * 0.7071067811865476))
        pdf = jnp.exp(-0.5 * upper * upper) * 0.3989422804014327
        act_rows = (upper * cdf).astype(BF)
        act[rows, :] = act_rows
        d_rows = (dot_nt(dy[rows, :], down[...]) * (cdf + upper * pdf)).astype(BF)
        d_up[rows, :] = d_rows
        out = dot_nn(act_rows, down[...]).astype(BF)
        back = dot_nt(d_rows, up[...])
        sums[2:3, :] += jnp.sum(back * u, axis=0, keepdims=True)
        sums[3:4, :] += jnp.sum(back, axis=0, keepdims=True)
        sums[6:7, :half] += jnp.sum(d_rows.astype(F32), axis=0, keepdims=True)
        store(i, out, (back * gain).astype(BF))
        return carry

    lax.fori_loop(0, 4, step, 0)


def mlp_kernel(*refs):
    pieces, (unit, dy, vectors) = refs[:4], refs[4:7]
    give, keep, mlp_in, act, d_up, sums, up, down, done = refs[7:]
    line, side = line_and_side()
    width, half = up.shape
    units = half // 4
    copies = []
    for place, step in enumerate(LINE_ORDER):
        low, high = [pieces[k + place // 2].at[place % 2] for k in (0, 2)]
        l = lax.bitwise_xor(line, step)
        for source, target in (
            (low, down.at[pl.ds(pl.multiple_of(l * units, 32), units), :]),
            (high.at[:, pl.ds(0, half)], up.at[pl.ds(pl.multiple_of(2 * l * units, 32), units), :]),
            (high.at[:, pl.ds(half, half)], up.at[pl.ds(pl.multiple_of((2 * l + 1) * units, 32), units), :]),
        ):
            copies.append(pltpu.make_async_copy(source, target, done.at[len(copies)]))
    for copy in copies:
        copy.start()
    core = lax.bitwise_and(lax.axis_index("seq"), 1)
    for copy in copies:
        copy.wait()

    def store(i, out, back):
        place = lax.shift_right_logical(i, 1)

        @pl.when(lax.bitwise_and(i, 1) == core)
        def _():
            keep[place, :, :width] = out
            keep[place, :, width:] = back

        @pl.when(lax.bitwise_and(i, 1) != core)
        def _():
            give[place, :, :width] = out
            give[place, :, width:] = back

    mlp_tokens(unit, dy, vectors, up, down, mlp_in, act, d_up, sums, side, store)


def mlp_own_kernel(unit, dy, vectors, up, down, own_pair, mlp_in, act, d_up, sums):
    _, side = line_and_side()
    width = up.shape[0]

    def store(i, out, back):
        own_pair[i, :, :width] = out
        own_pair[i, :, width:] = back

    mlp_tokens(unit, dy, vectors, up, down, mlp_in, act, d_up, sums, side, store)
    sums[4:5, :] = 0.25 * jnp.sum(dy[...].astype(F32), axis=0, keepdims=True)


def mlp_grads_kernel(*refs):
    own, other = refs[:5], refs[5:10]
    keep_up, send_up, keep_down, send_down, up_grad, down_grad = refs[10:]
    line, _ = line_and_side()
    half, width = down_grad.shape
    units = half // 4
    for c in range(0, width, 128):
        total = sum(dot_tn(mlp_in[:, c : c + 128], d_up[...]) for mlp_in, _, d_up, _, _ in (own, other))
        up_grad[c : c + 128, :] = total.astype(BF)
    for c in range(0, half, 128):
        total = sum(dot_tn(act[:, c : c + 128], dy[...]) for _, act, _, dy, _ in (own, other))
        down_grad[c : c + 128, :] = total.astype(BF)
    tail = (own[4][...] + other[4][...]).astype(BF)
    for place, step in enumerate(LINE_ORDER):
        ups, downs = ((keep_up, keep_down), (send_up, send_down))[place // 2]
        l = lax.bitwise_xor(line, step)
        downs[place % 2] = down_grad[pl.ds(pl.multiple_of(l * units, 32), units), :]
        ref = ups.at[place % 2]
        ref[:units, :half] = up_grad[pl.ds(pl.multiple_of(2 * l * units, 32), units), :]
        ref[:units, half:] = up_grad[pl.ds(pl.multiple_of((2 * l + 1) * units, 32), units), :]
        ref[units:, :] = tail


def up_sum_kernel(own, far, up_keep, up_give, tail):
    units, half = up_keep.shape
    width = 2 * half
    _, side = line_and_side()

    def total(rows, lanes):
        return own[0, rows, lanes].astype(F32) + far[0, rows, lanes].astype(F32)

    first, second = total(slice(0, units), slice(0, half)), total(slice(0, units), slice(half, width))
    last = total(slice(units, units + 8), slice(None))
    tail[...] = last
    up_keep[...] = jnp.where(side == 0, first, second).astype(BF)
    up_give[:units, :] = jnp.where(side == 0, second, first).astype(BF)
    up_give[units:, :] = jnp.concatenate([last[:, :half], last[:, half:]], axis=0).astype(BF)


def owners_kernel(deep, keep, far, tail, b0, b1, b2, b3, rows32):
    _, side = line_and_side()
    me = lax.axis_index("seq")
    rows, half = keep.shape
    here, there = keep[...].astype(F32), far[:rows, :].astype(F32)
    rows32[:, :half] = jnp.where(side == 0, here, there)
    rows32[:, half:] = jnp.where(side == 0, there, here)
    far_tail = far[rows:, :].astype(F32)
    last = tail[...] + jnp.concatenate([far_tail[:8], far_tail[8:]], axis=1)
    for j, ref in enumerate((b0, b1, b2, b3)):
        target = lax.bitwise_xor(me, j)
        block = rows32[pl.ds(pl.multiple_of(target * deep, 8), deep), :]
        ref[...] = jnp.concatenate([block, last], axis=0).astype(BF)


def owned_kernel(deep, b0, b1, b2, b3, tail, up_own, vec_own, sources):
    line, _ = line_and_side()
    me = lax.axis_index("seq")
    device = 4 * lax.axis_index("dp") + me
    width = tail.shape[1]
    half = width // 2
    units = half // 4
    for j, ref in enumerate((b0, b1, b2, b3)):
        sources[lax.bitwise_xor(me, j)] = ref[...].astype(F32)
    for l in range(4):
        parts = [
            sources[t, :deep, y * half + l * units : y * half + (l + 1) * units] for y in range(2) for t in range(4)
        ]
        up_own[:, l * 2 * half : (l + 1) * 2 * half] = jnp.concatenate(parts, axis=1)
    total = sources[0, deep:] + sources[1, deep:] + sources[2, deep:] + sources[3, deep:]
    rolled = pltpu.roll(total, width - device * deep, 1)
    vec_own[...] = rolled[:, :128]
    rolled = pltpu.roll(tail[...], width - line * units, 1)
    vec_own[6:7, :] = rolled[6:7, :128]


def attention_sum_kernel(deep, own, far, b0, b1, b2, b3, dense_own, total):
    me = lax.axis_index("seq")
    total[...] = own[0].astype(F32) + far[0].astype(F32)
    quarter = total.shape[1] // 4
    last = total[4 * deep :, :]
    for q in range(4):
        dense_own[:, q * quarter : (q + 1) * quarter] = total[q * deep : (q + 1) * deep, 3 * quarter :]
    for j, ref in enumerate((b0, b1, b2, b3)):
        target = lax.bitwise_xor(me, j)
        block = total[pl.ds(pl.multiple_of(target * deep, 8), deep), :]
        ref[...] = jnp.concatenate([block, last], axis=0).astype(BF)


def attention_owned_kernel(deep, b0, b1, b2, b3, qkv_own, vec_own, sources, row_block):
    me = lax.axis_index("seq")
    device = 4 * lax.axis_index("dp") + me
    width = b0.shape[1]
    own = width // 4
    for j, ref in enumerate((b0, b1, b2, b3)):
        sources[lax.bitwise_xor(me, j)] = ref[...].astype(F32)
    total = sources[0, deep:] + sources[1, deep:] + sources[2, deep:] + sources[3, deep:]
    vec_own[...] = pltpu.roll(total, width - device * deep, 1)[:, :128]
    row_block[...] = jnp.zeros(row_block.shape, F32)
    for part in range(3):
        lanes = slice(part * own, (part + 1) * own)
        whole = jnp.concatenate([sources[t, :, lanes] for t in range(4)], axis=1)
        qkv_own[:, part * width : (part + 1) * width] = whole[:deep]
        row_block[5:6, part * width : (part + 1) * width] = whole[deep + 5 : deep + 6]
    rolled = pltpu.roll(row_block[...], 3 * width - device * (3 * deep), 1)
    vec_own[5:6, :] = rolled[5:6, :128]


def with_waits(count, body):
    def wrapped(*refs):
        body(*refs[count:])

    return wrapped


def line_device(
    hidden_in,
    lengths,
    grad_out,
    attn_gain,
    attn_shift,
    mlp_gain,
    mlp_shift,
    qkv_weight,
    qkv_bias,
    dense_weight,
    dense_bias,
    up_weight,
    up_bias,
    down_weight,
    down_bias,
):
    n_dp, n_seq = 8, 4
    dp_me, me = lax.axis_index("dp"), lax.axis_index("seq")
    line, side = lax.shift_right_logical(dp_me, 1), lax.bitwise_and(dp_me, 1)
    chip, core = lax.shift_right_logical(me, 1), lax.bitwise_and(me, 1)
    device = dp_me * n_seq + me
    zero = jnp.int32(0)
    rows, width = hidden_in.shape
    group = rows * n_seq
    hidden_units = up_weight.shape[1]
    units = hidden_units // (n_dp * n_seq)
    half = hidden_units // 8
    deep = width // (n_dp * n_seq)
    per_line = n_seq * deep
    own = width // n_seq
    wide = 2 * half + 3 * own
    flat = (group, width)

    by_width = jnp.stack([attn_gain, attn_shift, mlp_gain, mlp_shift, dense_bias, down_bias])
    *blocks, mine = kernel_call(
        functools.partial(pack_kernel, deep),
        (((2 * deep + 8, width), BF),) * 4 + (((2 * rows, width), BF),),
        (qkv_weight, up_weight, by_width, qkv_bias[None], hidden_in, grad_out),
        scratch=(((4, 2 * deep + 8, width), F32), ((8, 3 * width), F32)),
        megabytes=16,
    )
    attn_piece, up_keep, up_give = kernel_call(
        functools.partial(unpack_kernel, deep),
        (((per_line + 8, width), BF), ((per_line, half), BF), ((per_line, half), BF)),
        (*seq_shuffle(blocks), dense_weight, up_bias[None]),
        scratch=(((per_line, width), F32), ((per_line, width), F32), ((8, width), F32)),
        megabytes=16,
    )

    across = lax.ppermute(mine, "dp", SIDE_SWAP)
    down_half = lax.ppermute(down_weight, "dp", HALF_SWAP)
    attn_piece, up_keep, up_give = once(attn_piece, down_half), up_keep, once(up_give, down_half)
    down_two = jnp.stack([down_weight, down_half])
    down_pair = lax.ppermute(down_two, "dp", PAIR_SWAP)
    attn_half = lax.ppermute(attn_piece, "dp", HALF_SWAP)
    up_far = lax.ppermute(up_give, "dp", SIDE_SWAP)
    chip_far = lax.ppermute(once(mine, up_keep), "seq", CHIP_SWAP)

    attn_two = once(jnp.stack([attn_piece, attn_half]), up_far)
    attn_pair = lax.ppermute(attn_two, "dp", PAIR_SWAP)
    attn_side = lax.ppermute(attn_two, "dp", SIDE_SWAP)
    up_both = jnp.concatenate(
        [jnp.where(side == 0, up_keep, up_far), jnp.where(side == 0, up_far, up_keep)], axis=1
    )
    mlp_piece = once(up_both, attn_half)
    mlp_half = lax.ppermute(mlp_piece, "dp", HALF_SWAP)
    by_chip = once(in_order(chip == 1, mine, chip_far), attn_half, up_far)
    core_far = lax.ppermute(by_chip, "seq", CORE_SWAP)

    attn_far = lax.ppermute(once(attn_pair, mlp_half), "dp", SIDE_SWAP)
    mlp_two = once(jnp.stack([mlp_piece, mlp_half]), attn_pair, down_pair)
    mlp_pair = lax.ppermute(mlp_two, "dp", PAIR_SWAP)
    chip_beyond = lax.ppermute(once(across, mlp_half, attn_pair, attn_side), "seq", CHIP_SWAP)

    def whole_group(values, over):
        full = in_order(core == 1, values, over, axis=1).reshape(n_seq, 2, rows, width)
        return full[:, 0].reshape(flat), full[:, 1].reshape(flat)

    hidden_group, dy = whole_group(by_chip, core_far)
    attn_pieces = (attn_two, attn_pair, attn_side, attn_far)

    row_lengths = lengths[0]
    segment, position = place(row_lengths, jnp.arange(group, dtype=jnp.int32))
    lane = jnp.arange(128, dtype=jnp.int32) % HEAD_DIM
    powers = jnp.power(F32(10000.0), -(2.0 * (lane % (ROT // 2)).astype(F32)) / ROT)
    angles = position.astype(F32)[:, None] * powers[None, :]
    cosine = jnp.where(lane < ROT, jnp.cos(angles), 1.0)
    sine = jnp.sin(angles)
    sine_a = jnp.where(lane < ROT // 2, -sine, 0.0)
    sine_b = jnp.where((lane >= ROT // 2) & (lane < ROT), sine, 0.0)

    def normed(values):
        centered = values - jnp.mean(values, axis=-1, keepdims=True)
        inverse = lax.rsqrt(jnp.mean(centered * centered, axis=-1, keepdims=True) + EPS)
        return centered * inverse, inverse

    unit = normed(hidden_group.astype(F32))[0]

    placed = kernel_call(
        functools.partial(place_kernel, deep),
        ((flat[1:] * 2, BF), ((n_dp * deep, width), BF), ((8, width), F32)) + (((2 * deep, group), BF),) * 4,
        attn_pieces + (dy,),
        scratch=(((n_dp * deep, width), F32), ((n_dp * deep, group), BF)),
        flops=2 * n_dp * deep * width * group,
    )
    weights, dense, vectors = placed[:3]
    by_chip_beyond = once(in_order(chip == 1, across, chip_beyond), weights)
    core_beyond = lax.ppermute(by_chip_beyond, "seq", CORE_SWAP)
    hidden_other, dy_other = whole_group(by_chip_beyond, core_beyond)
    unit_other = normed(hidden_other.astype(F32))[0]
    d_blocks = seq_shuffle(placed[3:])
    attn_in, qk, v = kernel_call(
        project_kernel,
        ((flat, BF), ((group, 2 * own), BF), ((group, own), BF)),
        (unit, weights, vectors, cosine, sine_a, sine_b),
        flops=2 * group * width * width,
    )
    attended = kernel_call(
        with_waits(1, functools.partial(attention_kernel, deep)),
        (((2 * deep, group), BF),) * 4 + ((flat, BF),),
        (mlp_pair, qk, v, *d_blocks, segment[:, None], segment[None, :], cosine, sine_a, sine_b),
        scratch=(((own, group), F32),) * 4 + ((flat, F32),),
        flops=14 * group * group * own,
        megabytes=16,
        apart=1,
    )
    d_joined = attended[4]
    held_shapes = ((flat, BF), ((group, half), BF), ((group, half), BF))
    give, keep, *held_other, up_full, down_full = kernel_call(
        with_waits(1, mlp_kernel),
        (((2, rows, 2 * width), BF),) * 2 + held_shapes + (((8, width), F32), ((width, half), BF), ((half, width), BF)),
        (d_joined, down_two, down_pair, mlp_two, mlp_pair, unit_other, dy_other, vectors),
        scratch=(pltpu.SemaphoreType.DMA((12,)),),
        flops=4 * group * width * 2 * half,
        megabytes=16,
        apart=5,
    )
    row_blocks = seq_shuffle(attended[:4])

    own_pair, *held_own = kernel_call(
        with_waits(1, mlp_own_kernel),
        (((4, rows, 2 * width), BF),) + held_shapes + (((8, width), F32),),
        (d_joined, unit, dy, vectors, up_full, down_full),
        flops=4 * group * width * 2 * half,
        megabytes=16,
        apart=1,
    )
    attn_send, attn_keep, own_give, own_keep = kernel_call(
        functools.partial(attention_grads_kernel, deep),
        (((4, per_line + 8, width), BF),) * 2 + (((2, rows, 2 * width), BF),) * 2,
        (*row_blocks, dense, dy, attn_in, d_joined, weights, unit, vectors, own_pair),
        scratch=(((n_dp * deep, group), BF), ((width, width), F32), ((8, width), F32)),
        flops=5 * group * width * width,
        megabytes=16,
    )
    up_shape, down_shape = ((2, units + 8, width), BF), ((2, units, width), BF)
    keep_up, send_up, keep_down, send_down = kernel_call(
        with_waits(1, mlp_grads_kernel),
        (up_shape, up_shape, down_shape, down_shape),
        (attn_send, *held_own[:3], dy, held_own[3], *held_other[:3], dy_other, held_other[3]),
        scratch=(((width, half), BF), ((half, width), BF)),
        flops=4 * group * width * 2 * half,
        megabytes=16,
        apart=1,
    )

    attn_moved = lax.ppermute(attn_send, "dp", SIDE_SWAP)
    up_got = lax.ppermute(send_up, "dp", PAIR_SWAP)
    down_got = lax.ppermute(send_down, "dp", PAIR_SWAP)
    both = keep.astype(F32) + lax.ppermute(once(give, keep_up), "seq", CORE_SWAP).astype(F32)
    both = both.astype(BF)
    first = (attn_moved, up_got, down_got, both)
    up_mine, up_send = add_blocks(keep_up, up_got, 1, 1)
    up_last = lax.ppermute(once(up_send, *first), "dp", HALF_SWAP)
    attn_mine, attn_send = add_blocks(attn_keep, attn_moved, 2, 2)
    attn_got = lax.ppermute(once(attn_send, *first), "dp", PAIR_SWAP)
    down_mine, down_send = add_blocks(keep_down, down_got, 1, 1)
    down_last = lax.ppermute(once(down_send, *first), "dp", HALF_SWAP)
    beyond = lax.ppermute(once(both, *first), "dp", SIDE_SWAP)
    attn_mine, attn_send = add_blocks(attn_mine, attn_got, 1, 1, waits=(up_last,))
    attn_last = lax.ppermute(attn_send, "dp", HALF_SWAP)

    both = own_keep.astype(F32) + lax.ppermute(own_give, "seq", CORE_SWAP).astype(F32) + beyond.astype(F32)
    chip_last = lax.ppermute(pick(both, 1 - chip).astype(BF), "seq", CHIP_SWAP)
    pair = pick(both, chip) + chip_last.astype(F32)
    x = hidden_in.astype(F32)
    block_out = x + vectors[4] + vectors[5] + pair[:, :width]
    upstream = pair[:, width:]
    own_unit, inverse = normed(x)
    inner = (
        upstream
        - jnp.mean(upstream, axis=-1, keepdims=True)
        - own_unit * jnp.mean(upstream * own_unit, axis=-1, keepdims=True)
    )
    grad_in = grad_out.astype(F32) + inverse * inner

    up_keep, up_give, tail = kernel_call(
        with_waits(1, up_sum_kernel),
        (((per_line, half), BF), ((per_line + 16, half), BF), ((8, width), F32)),
        (attn_got, up_mine, up_last),
        megabytes=8,
        apart=1,
    )
    down_own = down_mine[0].astype(F32) + down_last[0].astype(F32)
    up_far = lax.ppermute(up_give, "dp", SIDE_SWAP)
    blocks = kernel_call(
        with_waits(1, functools.partial(owners_kernel, deep)),
        (((deep + 8, width), BF),) * 4,
        (attn_last, up_keep, up_far, tail),
        scratch=(((per_line, width), F32),),
        megabytes=8,
        apart=1,
    )
    up_own, vec_own = kernel_call(
        with_waits(2, functools.partial(owned_kernel, deep)),
        (((deep, hidden_units), F32), ((8, 128), F32)),
        (chip_last, attn_last, *seq_shuffle(blocks), tail),
        scratch=(((4, deep + 8, width), F32),),
        megabytes=8,
        apart=2,
    )
    *blocks, dense_own = kernel_call(
        with_waits(1, functools.partial(attention_sum_kernel, deep)),
        (((deep + 8, width), BF),) * 4 + (((deep, width), F32),),
        (up_far, attn_mine, attn_last),
        scratch=(((per_line + 8, width), F32),),
        megabytes=8,
        apart=1,
    )
    qkv_own, vec_attn = kernel_call(
        with_waits(1, functools.partial(attention_owned_kernel, deep)),
        (((deep, 3 * width), F32), ((8, 128), F32)),
        (chip_last, *seq_shuffle(blocks)),
        scratch=(((4, deep + 8, width), F32), ((8, 3 * width), F32)),
        megabytes=8,
        apart=1,
    )
    by_width = vec_own[:5, :deep]
    qkv_bias_grad = vec_attn[5, : 3 * deep]
    up_bias_grad = vec_own[6, :units]
    return (
        block_out.astype(BF),
        grad_in.astype(BF),
        vec_attn[0, :deep],
        vec_attn[1, :deep],
        by_width[2],
        by_width[3],
        qkv_own,
        qkv_bias_grad,
        dense_own,
        by_width[4],
        up_own,
        up_bias_grad,
        down_own,
        by_width[4],
    )


def per_device(*args):
    if lax.axis_size("dp") == 8 and lax.axis_size("seq") == 4:
        return line_device(*args)
    return general_device(*args)


def solution(mesh):
    both = ("dp", "seq")
    matrix, vector = P(both, None), P(both)
    params = (vector, vector, vector, vector, matrix, vector, matrix, vector, matrix, vector, matrix, vector)
    return jax.shard_map(
        per_device,
        mesh=mesh,
        in_specs=(matrix, P("dp", None), matrix) + params,
        out_specs=(matrix, matrix) + params,
        check_vma=False,
    )
```
